128 devices in a mesh: row: 8 (over y, core), col: 16 (over z, x).
Axes of the slice: x: 4, y: 4, z: 4, core: 2. Of those that a mesh axis runs over, the one named last changes fastest.
Arguments:
- user_factors: float32 [16384, 128], P('row'), may hold values from -6 to 6
- item_factors: float32 [131072, 128], P(('row', 'col')), may hold values from -0.015625 to 0.015625
- fetch_list: int32 [8, 16, 128, 1], P('row', 'col'), may hold values from 0 to 7
- tile_user: int32 [8, 16, 32], P('row', 'col'), may hold values from 0 to 15
- tile_slot: int32 [8, 16, 32], P('row', 'col'), may hold values from 0 to 127
- entry_row: int32 [8, 16, 32, 512], P('row', 'col'), may hold values from 0 to 127
- entry_col: int32 [8, 16, 32, 512], P('row', 'col'), may hold values from 0 to 127
- entry_count: int32 [8, 16, 32, 512], P('row', 'col'), may hold values from 1 to 8
- tile_count: int32 [8, 16], P('row', 'col'), may hold values from 4 to 32, as said below
Outputs:
- solved: float32 [16384, 128], P('row')
The draws below stay inside these ranges and needn't reach their ends.
Inputs may be any that keep to these rules, and one draw needn't show every extreme that they name: `tile_count`: at least 4 tiles live on every device; some device has all 32 live in every draw.
All inputs are finite; a program needn't handle non-finite values.
Results may differ from the reference program's by a relative error of at most 0.0003.
Values sent between devices are 32-bit elements; how exact they have to be, the bound alone decides.
A program may use at most 128 MiB of HBM per device.

```python
import jax
import jax.numpy as jnp
from jax import lax

K = 128
BLOCK = 128
UB_DEV = 16
IB_DEV = 8
TILES_DEV = 32
NNZ = 512
CAP = 1
ITERS = 3
USERS = 16384
ITEMS = 131072
SLOTS = 128
N_ROW = 8
N_COL = 16
DEVICES = 128


def draw_tile_count(key, part):
    first, second, third = jax.random.split(key, 3)
    power = jax.random.randint(first, (N_ROW, N_COL), 0, 4)
    divisor = jnp.array([1, 2, 4, 8], jnp.int32)[power]
    counts = TILES_DEV // divisor
    row_pick = jax.random.randint(second, (), 0, N_ROW)
    col_pick = jax.random.randint(third, (), 0, N_COL)
    return counts.at[row_pick, col_pick].set(TILES_DEV).astype(jnp.int32)


def set_ends(result, key, low, top_value):
    longest = result.shape.index(max(result.shape))
    spots = []
    for shift in (0, 1):
        where = [jax.random.randint(jax.random.fold_in(key, axis), (), 0, length) for axis, length in enumerate(result.shape)]
        where[longest] = (where[longest] + shift) % result.shape[longest]
        spots.append(tuple(where))
    return result.at[spots[0]].set(low).at[spots[1]].set(top_value)


def block_levels(key, dims, shards, least, top_value):
    gain = 1.0
    for position, shards_of in shards:
        heights = jax.random.uniform(jax.random.fold_in(jax.random.fold_in(key, 6), position), (shards_of,), jnp.float32, least / len(shards), top_value / len(shards))
        gain = gain * jnp.repeat(jnp.exp(heights), dims[position] // shards_of).reshape((-1,) + (1,) * (len(dims) - 1 - position))
    return gain


def bell_draw(stream_key, dims, width, most, pieces=(), kind=jnp.bfloat16):
    result = width * jax.random.normal(stream_key, dims, jnp.float32)
    if pieces:
        result = result * block_levels(stream_key, dims, pieces, -0.22, 0.18)
    return jnp.clip(result, -most, most).astype(kind)


def setup_inputs(seed: int = 0) -> dict:
    keys = jax.random.split(jax.random.key(seed), 10)
    user_factors = bell_draw(keys[0], (USERS, K), 1.0, 6.0, ((0, 8),), jnp.float32)
    item_factors = bell_draw(keys[1], (ITEMS, K), ITEMS ** -0.5, 0.015625, ((0, 128),), jnp.float32)
    fetch_list = set_ends(jax.random.randint(keys[2], (N_ROW, N_COL, DEVICES, CAP), 0, IB_DEV), jax.random.fold_in(keys[2], 1), 0, IB_DEV - 1).astype(jnp.int32)
    tile_user = set_ends(jax.random.randint(keys[3], (N_ROW, N_COL, TILES_DEV), 0, UB_DEV), jax.random.fold_in(keys[3], 1), 0, UB_DEV - 1).astype(jnp.int32)
    tile_slot = set_ends(jax.random.randint(keys[4], (N_ROW, N_COL, TILES_DEV), 0, SLOTS), jax.random.fold_in(keys[4], 1), 0, SLOTS - 1).astype(jnp.int32)
    entry_row = set_ends(jax.random.randint(keys[5], (N_ROW, N_COL, TILES_DEV, NNZ), 0, BLOCK), jax.random.fold_in(keys[5], 1), 0, BLOCK - 1).astype(jnp.int32)
    entry_col = set_ends(jax.random.randint(keys[6], (N_ROW, N_COL, TILES_DEV, NNZ), 0, BLOCK), jax.random.fold_in(keys[6], 1), 0, BLOCK - 1).astype(jnp.int32)
    entry_count = set_ends(jax.random.randint(keys[7], (N_ROW, N_COL, TILES_DEV, NNZ), 1, 9), jax.random.fold_in(keys[7], 1), 1, 8).astype(jnp.int32)
    tile_count = draw_tile_count(jax.random.fold_in(keys[9], 71), 0)
    return {"user_factors": user_factors, "item_factors": item_factors, "fetch_list": fetch_list, "tile_user": tile_user, "tile_slot": tile_slot, "entry_row": entry_row, "entry_col": entry_col, "entry_count": entry_count, "tile_count": tile_count}


HIGHEST = lax.Precision.HIGHEST
CONFIDENCE_SCALE = 40.0
RIDGE = 0.5
EPSILON = 1e-6


def reference(user_factors, item_factors, fetch_list, tile_user, tile_slot, entry_row, entry_col, entry_count, tile_count):
    gram = jnp.dot(item_factors.T, item_factors, precision=HIGHEST, preferred_element_type=jnp.float32)
    user_rows = UB_DEV * BLOCK
    starting = user_factors.reshape(N_ROW, user_rows, K)

    def one_shard(packed):
        start_point, fetched, users, slot_ids, rows_in, cols_in, counts, live = packed
        alive = (jnp.arange(TILES_DEV, dtype=jnp.int32)[None, :] < live[:, None]).astype(jnp.float32)
        owner = slot_ids // CAP
        member = slot_ids % CAP
        col_index = jnp.broadcast_to(jnp.arange(N_COL, dtype=jnp.int32)[:, None], owner.shape)
        local_id = fetched[col_index, owner, member]
        global_block = owner * IB_DEV + local_id
        item_index = (global_block[..., None] * BLOCK + cols_in).reshape(-1).astype(jnp.int32)
        user_index = (users[..., None] * BLOCK + rows_in).reshape(-1).astype(jnp.int32)
        excess = CONFIDENCE_SCALE * counts.astype(jnp.float32)
        weight_fit = (excess * alive[..., None]).reshape(-1)
        weight_rhs = ((1.0 + excess) * alive[..., None]).reshape(-1)
        picked = jnp.take(item_factors, item_index, axis=0)

        def apply_operator(vector):
            inner = jnp.sum(picked * jnp.take(vector, user_index, axis=0), axis=1)
            data = jax.ops.segment_sum((weight_fit * inner)[:, None] * picked, user_index, num_segments=user_rows)
            return data + jnp.dot(vector, gram, precision=HIGHEST, preferred_element_type=jnp.float32) + RIDGE * vector

        rhs = jax.ops.segment_sum(weight_rhs[:, None] * picked, user_index, num_segments=user_rows)
        iterate = start_point
        residual = rhs - apply_operator(iterate)
        direction = residual
        norm_now = jnp.sum(residual * residual, axis=1, keepdims=True)
        for iteration in range(ITERS):
            image = apply_operator(direction)
            alpha = norm_now / (jnp.sum(direction * image, axis=1, keepdims=True) + EPSILON)
            iterate = iterate + alpha * direction
            residual = residual - alpha * image
            norm_next = jnp.sum(residual * residual, axis=1, keepdims=True)
            direction = residual + (norm_next / (norm_now + EPSILON)) * direction
            norm_now = norm_next
        return iterate

    solved = lax.map(one_shard, (starting, fetch_list, tile_user, tile_slot, entry_row, entry_col, entry_count, tile_count))
    return solved.reshape(USERS, K)
```

```python
import functools

import jax
import jax.numpy as jnp
from jax import lax
from jax.experimental import pallas as pl
from jax.experimental.pallas import tpu as pltpu
from jax.sharding import PartitionSpec as P

K = 128
BLOCK = 128
UB = 16
IB = 8
TILES = 32
NNZ = 512
NZ = NX = 4
NY = 4
ROWS = 8
COLS = 16
ALL_TILES = COLS * TILES
LIST = 1024
GROUP = 4
HELD = 32
STAGE = 3 * TILES + 8
HALF = 56
SCALE = 40.0
RIDGE = 0.5
EPSILON = 1e-06
MESH = pl.DeviceIdType.MESH
F32 = jnp.float32
BF16 = jnp.bfloat16
NT = (((1,), (1,)), ((), ()))
TN = (((0,), (0,)), ((), ()))
NN = (((1,), (0,)), ((), ()))
ANY = pl.BlockSpec(memory_space=pl.ANY)
VMEM = pl.BlockSpec(memory_space=pltpu.VMEM)
SMEM = pl.BlockSpec(memory_space=pltpu.SMEM)
BIG = 48 * 2**20


def dot(a, b, dims):
    return lax.dot_general(a, b, dims, preferred_element_type=F32)


def split(a):
    high = a.astype(BF16)
    return high, (a - high.astype(F32)).astype(BF16)


def dot3(a, b, dims):
    return dot(a[0], b[0], dims) + (dot(a[0], b[1], dims) + dot(a[1], b[0], dims))


def greet(peers):
    barrier = pltpu.get_barrier_semaphore()
    for peer in peers:
        pl.semaphore_signal(barrier, inc=1, device_id=peer, device_id_type=MESH)
    pl.semaphore_wait(barrier, len(peers))


class Copies:
    def __init__(self, send_sem, recv_sem):
        self.send_sem, self.recv_sem, self.made = send_sem, recv_sem, []

    def send(self, src, dst, peer):
        i = len(self.made)
        copy = pltpu.make_async_remote_copy(
            src_ref=src,
            dst_ref=dst,
            send_sem=self.send_sem.at[i],
            recv_sem=self.recv_sem.at[i],
            device_id=peer,
            device_id_type=MESH,
        )
        copy.start()
        self.made.append(copy)
        return copy

    def finish(self):
        for copy in self.made:
            copy.wait_send()


def col_place():
    c = lax.axis_index("col")
    z, x = c // NX, c % NX
    along_x = [{"col": z * NX + (x + d) % NX} for d in range(1, NX)]
    along_z = [{"col": ((z + d) % NZ) * NX + x} for d in range(1, NZ)]
    return c, z, x, along_x, along_z


def gather_kernel(
    items, fetch, user, slot, er, ec, en, count, yh, yl, gram, ent, stage, land, send_sem, recv_sem, own_sem
):
    c, z, x, along_x, along_z = col_place()
    r = lax.axis_index("row")
    y, core = r // 2, r % 2
    right, left, across = (((y + d) % NY) * 2 + core for d in (1, 3, 2))
    other = y * 2 + 1 - core
    to_right, to_left, to_other = {"row": right}, {"row": left}, {"row": other}
    stage[0:TILES] = er[...]
    stage[TILES : 2 * TILES] = ec[...]
    stage[2 * TILES : 3 * TILES] = en[...]
    last = 3 * TILES
    stage[last : last + 1, 0:128] = fetch[...]
    stage[last + 1 : last + 2, 0:TILES] = slot[...]
    stage[last + 2 : last + 3, 0:TILES] = user[...]
    stage[last + 3 : last + 4, 0:128] = jnp.broadcast_to(count[...], (1, 128))
    own = pltpu.make_async_copy(stage, ent.at[z, x], own_sem)
    own.start()

    greet(along_x + along_z + [to_right, to_left, to_other])
    copies = Copies(send_sem, recv_sem)
    send = copies.send

    mine = [items.at[pl.ds(2 * i, 2)] for i in range(4)]
    there = [land.at[r, pl.ds(2 * i, 2)] for i in range(4)]
    from_left, from_right = {}, {}
    for i, j in zip((0, 1, 2, 3), (2, 3, 0, 1)):
        from_left[i] = send(mine[i], there[i], to_right)
        from_right[j] = send(mine[j], there[j], to_left)
    first, second = pl.ds(0, HALF), pl.ds(HALF, STAGE - HALF)
    by_x = [send(stage.at[first], ent.at[z, x, first], peer) for peer in along_x]
    by_z = [send(stage.at[second], ent.at[z, x, second], peer) for peer in along_z]
    between = [send(items, land.at[r], to_other)]
    own.wait()
    late = []
    for copy in by_x:
        copy.wait_recv()
    late += [send(ent.at[z, :, first], ent.at[z, :, first], peer) for peer in along_z]
    for copy in by_z:
        copy.wait_recv()
    late += [send(ent.at[:, x, second], ent.at[:, x, second], peer) for peer in along_x]
    far = []
    for i, j in ((0, 2), (1, 3)):
        from_left[i].wait_recv()
        piece = land.at[left, pl.ds(2 * i, 2)]
        far.append(send(piece, piece, to_right))
        from_right[j].wait_recv()
        piece = land.at[right, pl.ds(2 * j, 2)]
        far.append(send(piece, piece, to_left))
    for i, j in ((2, 0), (3, 1)):
        from_left[i].wait_recv()
        from_right[j].wait_recv()
    between.append(send(land.at[left], land.at[left], to_other))
    between.append(send(land.at[right], land.at[right], to_other))
    for copy in far:
        copy.wait_recv()
    between.append(send(land.at[across], land.at[across], to_other))
    for copy in between:
        copy.wait_recv()
    land[pl.ds(r, 1)] = items[...][None]

    def add(i, sums):
        high, low = split(land[i // IB, i % IB])
        yh[i] = high
        yl[i] = low
        return sums[0] + dot(high, high, TN), sums[1] + dot(high, low, TN)

    zero = jnp.zeros((K, K), F32)
    main, mixed = lax.fori_loop(0, ROWS * IB, add, (zero, zero))
    gram[...] = main + (mixed + mixed.T)
    for copy in late:
        copy.wait_recv()
    copies.finish()


def gather(items, fetch, user, slot, er, ec, en, count):
    n = 8 + 6 + 4 + 6 + 4
    return pl.pallas_call(
        gather_kernel,
        out_shape=(
            jax.ShapeDtypeStruct((ROWS * IB, BLOCK, K), BF16),
            jax.ShapeDtypeStruct((ROWS * IB, BLOCK, K), BF16),
            jax.ShapeDtypeStruct((K, K), F32),
            jax.ShapeDtypeStruct((NZ, NX, STAGE, NNZ), jnp.int32),
        ),
        in_specs=[VMEM] * 8,
        out_specs=(VMEM, VMEM, VMEM, ANY),
        scratch_shapes=[
            pltpu.VMEM((STAGE, NNZ), jnp.int32),
            pltpu.VMEM((ROWS, IB, BLOCK, K), F32),
            pltpu.SemaphoreType.DMA((n,)),
            pltpu.SemaphoreType.DMA((n,)),
            pltpu.SemaphoreType.DMA,
        ],
        compiler_params=pltpu.CompilerParams(
            collective_id=0, has_side_effects=True, vmem_limit_bytes=BIG
        ),
        name="gather",
    )(items, fetch, user, slot, er, ec, en, count)


def build_kernel(place, ent, yh, yl, gram, start, out, weights, order, meta, held, sem, meta_sem):
    fetched = pltpu.make_async_copy(
        ent.at[:, pl.ds(3 * TILES, 8), pl.ds(0, 128)], meta, meta_sem
    )
    fetched.start()
    g = split(gram[...])

    def begin(b, _):
        at = pl.ds(pl.multiple_of(b * BLOCK, BLOCK), BLOCK)
        out[at] = -dot3(split(start[at]), g, NN)
        return 0

    lax.fori_loop(0, UB, begin, 0)
    fetched.wait()
    me = place[0]

    def scan(c, n):
        def one(t, n):
            s = meta[c, 1, t]
            block = (s // COLS) * IB + meta[c, 0, s]
            order[n] = ((c * TILES + t) * 64 + block) * UB + meta[c, 2, t]
            return n + jnp.where(s % COLS == me, 1, 0)

        return lax.fori_loop(0, meta[c, 3, 0], one, n)

    n = lax.fori_loop(0, COLS, scan, 0)
    order[LIST - 1] = n
    ids = lax.broadcasted_iota(jnp.int32, (BLOCK, NNZ), 0)

    def out_copy(j):
        slot = j % 4
        return pltpu.make_async_copy(held.at[slot], weights.at[j], sem.at[slot])

    def tile(j, _):
        code = order[j]
        b, block, at = code % UB, (code // UB) % 64, code // (64 * UB)
        c, t = at // TILES, at % TILES
        rows = ent[c, pl.ds(t, 1), :]
        cols = ent[c, pl.ds(TILES + t, 1), :]
        counts = ent[c, pl.ds(2 * TILES + t, 1), :].astype(F32)
        row_hot = ids == rows
        col_hot = jnp.where(ids == cols, 1.0, 0.0).astype(BF16)
        ones = jnp.where(row_hot, 1.0, 0.0).astype(BF16)
        many = jnp.where(row_hot, counts, 0.0).astype(BF16)
        times = dot(ones, col_hot, NT)
        excess = SCALE * dot(many, col_hot, NT)

        @pl.when(j >= 4)
        def _():
            out_copy(j - 4).wait()

        held[j % 4] = excess
        out_copy(j).start()
        where = pl.ds(pl.multiple_of(b * BLOCK, BLOCK), BLOCK)
        item = (yh[block], yl[block])
        scores = dot3(split(start[where]), item, NT)
        pull = times + excess * (1.0 - scores)
        out[where] += dot3(split(pull), item, NN)
        return 0

    lax.fori_loop(0, n, tile, 0)

    def drain(j, _):
        out_copy(j).wait()
        return 0

    lax.fori_loop(jnp.maximum(n - 4, 0), n, drain, 0)


def build(place, ent, yh, yl, gram, start):
    return pl.pallas_call(
        build_kernel,
        out_shape=(
            jax.ShapeDtypeStruct((UB * BLOCK, K), F32),
            jax.ShapeDtypeStruct((ALL_TILES, BLOCK, BLOCK), F32),
            jax.ShapeDtypeStruct((LIST,), jnp.int32),
        ),
        in_specs=[SMEM] + [VMEM] * 5,
        out_specs=(VMEM, ANY, SMEM),
        scratch_shapes=[
            pltpu.SMEM((COLS, 8, 128), jnp.int32),
            pltpu.VMEM((4, BLOCK, BLOCK), F32),
            pltpu.SemaphoreType.DMA((4,)),
            pltpu.SemaphoreType.DMA,
        ],
        compiler_params=pltpu.CompilerParams(vmem_limit_bytes=BIG),
        name="build",
    )(place, ent, yh, yl, gram, start)


def each_tile(order, weights, held, sem, work):
    n = order[LIST - 1]

    def copy(base, i):
        return pltpu.make_async_copy(weights.at[base + i], held.at[i], sem.at[i])

    def batch(k, _):
        base = k * HELD
        here = jnp.minimum(n - base, HELD)

        def begin(i, _):
            copy(base, i).start()
            return 0

        lax.fori_loop(0, here, begin, 0)

        def group(q, _):
            for u in range(GROUP):
                i = q * GROUP + u

                @pl.when(i < here)
                def _(i=i):
                    copy(base, i).wait()

            for u in range(GROUP):
                i = q * GROUP + u
                live = i < here
                code = jnp.where(live, order[base + i], 0)
                w = jnp.where(live, held[i], 0.0)
                work(code % UB, (code // UB) % 64, w)
            return 0

        lax.fori_loop(0, (here + GROUP - 1) // GROUP, group, 0)
        return 0

    lax.fori_loop(0, (n + HELD - 1) // HELD, batch, 0)


def rows_of(b):
    return pl.ds(pl.multiple_of(b * BLOCK, BLOCK), BLOCK)


def dots(a, b):
    return jnp.sum(a * b, axis=1, keepdims=True)


def pull_tiles(order, weights, held, sem, yh, yl, vh, vl, out):
    def work(b, block, w):
        at = rows_of(b)
        item = (yh[block], yl[block])
        scores = dot3((vh[at], vl[at]), item, NT)
        out[at] += dot3(split(w * scores), item, NN)

    each_tile(order, weights, held, sem, work)


def first_kernel(order, total, start, yh, yl, gram, weights, out, residual, vh, vl, held, sem):
    g = split(gram[...])

    def begin(b, _):
        at = rows_of(b)
        v = total[at] - RIDGE * start[at]
        residual[at] = v
        high, low = split(v)
        vh[at], vl[at] = high, low
        out[at] = dot3((high, low), g, NN)
        return 0

    lax.fori_loop(0, UB, begin, 0)
    pull_tiles(order, weights, held, sem, yh, yl, vh, vl, out)


def update(total, iterate, residual, direction):
    image = total + RIDGE * direction
    now = dots(residual, residual)
    alpha = now / (dots(direction, image) + EPSILON)
    iterate = iterate + alpha * direction
    residual = residual - alpha * image
    after = dots(residual, residual)
    direction = residual + after / (now + EPSILON) * direction
    return iterate, residual, direction


def second_kernel(
    order, total, iterate, residual, yh, yl, gram, weights, out, new_x, new_r, new_p, vh, vl, held, sem
):
    g = split(gram[...])

    def begin(b, _):
        at = rows_of(b)
        r = residual[at]
        new_x[at], new_r[at], p = update(total[at], iterate[at], r, r)
        new_p[at] = p
        high, low = split(p)
        vh[at], vl[at] = high, low
        out[at] = dot3((high, low), g, NN)
        return 0

    lax.fori_loop(0, UB, begin, 0)
    pull_tiles(order, weights, held, sem, yh, yl, vh, vl, out)


def third_kernel(
    order, total, iterate, residual, direction, yh, yl, gram, weights,
    squares, new_x, new_r, new_p, vh, vl, acc, held, sem,
):
    g = split(gram[...])

    def begin(b, _):
        at = rows_of(b)
        new_x[at], new_r[at], p = update(total[at], iterate[at], residual[at], direction[at])
        new_p[at] = p
        high, low = split(p)
        vh[at], vl[at] = high, low
        acc[at] = p * dot3((high, low), g, NN)
        return 0

    lax.fori_loop(0, UB, begin, 0)

    def work(b, block, w):
        at = rows_of(b)
        scores = dot3((vh[at], vl[at]), (yh[block], yl[block]), NT)
        acc[at] += w * scores * scores

    each_tile(order, weights, held, sem, work)
    for b in range(UB):
        squares[b : b + 1] = jnp.sum(acc[b * BLOCK : (b + 1) * BLOCK].T, axis=0, keepdims=True)


def last_kernel(squares, iterate, residual, direction, out):
    sums = jnp.sum(squares[...], axis=0)
    for b in range(UB):
        at = pl.ds(b * BLOCK, BLOCK)
        p = direction[at]
        r = residual[at]
        below = jnp.broadcast_to(sums[b : b + 1], (BLOCK, BLOCK)).T + RIDGE * dots(p, p)
        out[at] = iterate[at] + dots(r, r) / (below + EPSILON) * p


USERS = jax.ShapeDtypeStruct((UB * BLOCK, K), F32)


def local(kernel, name, outs, specs, scratch=()):
    tiles = [
        pltpu.VMEM((UB * BLOCK, K), BF16),
        pltpu.VMEM((UB * BLOCK, K), BF16),
        *scratch,
        pltpu.VMEM((HELD, BLOCK, BLOCK), F32),
        pltpu.SemaphoreType.DMA((HELD,)),
    ]
    return pl.pallas_call(
        kernel,
        out_shape=outs,
        in_specs=specs,
        out_specs=tuple(VMEM for _ in outs),
        scratch_shapes=tiles,
        compiler_params=pltpu.CompilerParams(vmem_limit_bytes=BIG),
        name=name,
    )


def reduce_kernel(part, out, land_a, land_b, sum_a, sum_b, near_a, near_b, send_sem, recv_sem):
    c, z, x, along_x, along_z = col_place()
    greet(along_x + along_z)
    copies = Copies(send_sem, recv_sem)
    send = copies.send
    upper, lower = pl.ds(0, 64), pl.ds(64, 64)
    step_a = [
        send(part.at[:, (x + d) % NX, upper], land_a.at[d - 1], along_x[d - 1]) for d in (1, 2, 3)
    ]
    step_b = [
        send(part.at[(z + d) % NZ, :, lower], land_b.at[d - 1], along_z[d - 1]) for d in (1, 2, 3)
    ]
    for copy in step_a:
        copy.wait_recv()
    sum_a[...] = part[:, x, 0:64] + land_a[0] + (land_a[1] + land_a[2])
    next_a = [
        send(sum_a.at[(z + d) % NZ], near_a.at[d - 1], along_z[d - 1]) for d in (1, 2, 3)
    ]
    for copy in step_b:
        copy.wait_recv()
    sum_b[...] = part[z, :, 64:128] + land_b[0] + (land_b[1] + land_b[2])
    next_b = [
        send(sum_b.at[(x + d) % NX], near_b.at[d - 1], along_x[d - 1]) for d in (1, 2, 3)
    ]
    for copy in next_a:
        copy.wait_recv()
    out[z, x, 0:64] = sum_a[z] + near_a[0] + (near_a[1] + near_a[2])
    here = out.at[z, x, upper]
    back_a = [send(here, here, peer) for peer in along_z]
    for copy in next_b:
        copy.wait_recv()
    out[z, x, 64:128] = sum_b[x] + near_b[0] + (near_b[1] + near_b[2])
    here = out.at[z, x, lower]
    back_b = [send(here, here, peer) for peer in along_x]
    for copy in back_a:
        copy.wait_recv()
    line = out.at[:, x, upper]
    end = [send(line, line, peer) for peer in along_x]
    for copy in back_b:
        copy.wait_recv()
    line = out.at[z, :, lower]
    end += [send(line, line, peer) for peer in along_z]
    for copy in end:
        copy.wait_recv()
    copies.finish()


def reduce(part):
    out = pl.pallas_call(
        reduce_kernel,
        out_shape=jax.ShapeDtypeStruct((NZ, NX, BLOCK, K), F32),
        in_specs=[VMEM],
        out_specs=VMEM,
        scratch_shapes=[
            pltpu.VMEM((3, 4, 64, K), F32),
            pltpu.VMEM((3, 4, 64, K), F32),
            pltpu.VMEM((4, 64, K), F32),
            pltpu.VMEM((4, 64, K), F32),
            pltpu.VMEM((3, 64, K), F32),
            pltpu.VMEM((3, 64, K), F32),
            pltpu.SemaphoreType.DMA((24,)),
            pltpu.SemaphoreType.DMA((24,)),
        ],
        compiler_params=pltpu.CompilerParams(
            collective_id=1, has_side_effects=True, vmem_limit_bytes=BIG
        ),
        name="reduce",
    )(part.reshape(NZ, NX, BLOCK, K))
    return out.reshape(UB * BLOCK, K)


def scalars_kernel(mine, out, send_sem, recv_sem):
    c = lax.axis_index("col")
    peers = [{"col": (c + d) % COLS} for d in range(1, COLS)]
    greet(peers)
    copies = Copies(send_sem, recv_sem)
    made = [copies.send(mine, out.at[c], peer) for peer in peers]
    out[pl.ds(c, 1)] = mine[...][None]
    for copy in made:
        copy.wait_recv()
    copies.finish()


def gather_scalars(mine):
    return pl.pallas_call(
        scalars_kernel,
        out_shape=jax.ShapeDtypeStruct((COLS, UB, BLOCK), F32),
        in_specs=[VMEM],
        out_specs=VMEM,
        scratch_shapes=[
            pltpu.SemaphoreType.DMA((COLS - 1,)),
            pltpu.SemaphoreType.DMA((COLS - 1,)),
        ],
        compiler_params=pltpu.CompilerParams(collective_id=2, has_side_effects=True),
        name="scalars",
    )(mine)


def shards(user_factors, item_factors, fetch_list, tile_user, tile_slot, er, ec, en, tile_count):
    yh, yl, gram, ent = gather(
        item_factors.reshape(IB, BLOCK, K),
        fetch_list.reshape(1, 128),
        tile_user.reshape(1, TILES),
        tile_slot.reshape(1, TILES),
        er.reshape(TILES, NNZ),
        ec.reshape(TILES, NNZ),
        en.reshape(TILES, NNZ),
        tile_count.reshape(1, 1),
    )
    place = lax.axis_index("col").astype(jnp.int32).reshape(1)
    part, weights, order = build(
        place, ent.reshape(COLS, STAGE, NNZ), yh, yl, gram, user_factors
    )
    total = reduce(part)
    tail = [VMEM] * 3 + [ANY]
    part, residual = local(first_kernel, "first", (USERS,) * 2, [SMEM, VMEM, VMEM] + tail)(
        order, total, user_factors, yh, yl, gram, weights
    )
    total = reduce(part)
    part, iterate, residual, direction = local(
        second_kernel, "second", (USERS,) * 4, [SMEM] + [VMEM] * 3 + tail
    )(order, total, user_factors, residual, yh, yl, gram, weights)
    total = reduce(part)
    squares = jax.ShapeDtypeStruct((UB, BLOCK), F32)
    part, iterate, residual, direction = local(
        third_kernel,
        "third",
        (squares,) + (USERS,) * 3,
        [SMEM] + [VMEM] * 4 + tail,
        [pltpu.VMEM((UB * BLOCK, K), F32)],
    )(order, total, iterate, residual, direction, yh, yl, gram, weights)
    squares = gather_scalars(part)
    return pl.pallas_call(
        last_kernel,
        out_shape=USERS,
        in_specs=[VMEM] * 4,
        out_specs=VMEM,
        compiler_params=pltpu.CompilerParams(vmem_limit_bytes=BIG),
        name="last",
    )(squares, iterate, residual, direction)


def solution(mesh):
    return jax.shard_map(
        shards,
        mesh=mesh,
        in_specs=(
            P("row", None),
            P(("row", "col"), None),
            P("row", "col", None, None),
            P("row", "col", None),
            P("row", "col", None),
            P("row", "col", None, None),
            P("row", "col", None, None),
            P("row", "col", None, None),
            P("row", "col"),
        ),
        out_specs=P("row", None),
        check_vma=False,
    )
```

```python
import functools

import jax
import jax.numpy as jnp
from jax import lax
from jax.experimental import pallas as pl
from jax.experimental.pallas import tpu as pltpu
from jax.sharding import PartitionSpec as P

K = 128
BLOCK = 128
UB = 16
IB = 8
TILES = 32
NNZ = 512
NZ = NX = 4
NY = 4
ROWS = 8
COLS = 16
ALL_TILES = COLS * TILES
LIST = 1024
UNROLL = 4
BUILD = 4
SLOTS = 2 * BUILD
GROUP = 4
HELD = 32
STAGE = 3 * TILES + 8
HALF = 56
SCALE = 40.0
RIDGE = 0.5
EPSILON = 1e-06
MESH = pl.DeviceIdType.MESH
F32 = jnp.float32
BF16 = jnp.bfloat16
NT = (((1,), (1,)), ((), ()))
NN = (((1,), (0,)), ((), ()))
ANY = pl.BlockSpec(memory_space=pl.ANY)
VMEM = pl.BlockSpec(memory_space=pltpu.VMEM)
SMEM = pl.BlockSpec(memory_space=pltpu.SMEM)
BIG = 24 * 2**20


def dot(a, b, dims):
    return lax.dot_general(a, b, dims, preferred_element_type=F32)


def split(a):
    high = a.astype(BF16)
    return high, (a - high.astype(F32)).astype(BF16)


def pair(a):
    return jnp.concatenate(split(a), axis=1)


def fold(wide):
    return wide[:, 0:128] + wide[:, 128:256]


def by_cols(high, low):
    both = jnp.concatenate([high, low], axis=1)
    return jnp.concatenate([both, both], axis=0)


def greet(peers):
    barrier = pltpu.get_barrier_semaphore()
    for peer in peers:
        pl.semaphore_signal(barrier, inc=1, device_id=peer, device_id_type=MESH)
    pl.semaphore_wait(barrier, len(peers))


class Copies:
    def __init__(self, send_sem, recv_sem):
        self.send_sem, self.recv_sem, self.made = send_sem, recv_sem, []

    def send(self, src, dst, peer):
        i = len(self.made)
        copy = pltpu.make_async_remote_copy(
            src_ref=src,
            dst_ref=dst,
            send_sem=self.send_sem.at[i],
            recv_sem=self.recv_sem.at[i],
            device_id=peer,
            device_id_type=MESH,
        )
        copy.start()
        self.made.append(copy)
        return copy

    def finish(self):
        for copy in self.made:
            copy.wait_send()


def col_place():
    c = lax.axis_index("col")
    z, x = c // NX, c % NX
    along_x = [{"col": z * NX + (x + d) % NX} for d in range(1, NX)]
    along_z = [{"col": ((z + d) % NZ) * NX + x} for d in range(1, NZ)]
    return c, z, x, along_x, along_z


def gather_kernel(
    items, fetch, user, slot, er, ec, en, count, yh, yl, th, tl, gram, ent,
    stage, land, fetch_in, slot_in, user_in, small, send_sem, recv_sem, own_sem, in_sem,
):
    c, z, x, along_x, along_z = col_place()
    r = lax.axis_index("row")
    y, core = r // 2, r % 2
    right, left, across = (((y + d) % NY) * 2 + core for d in (1, 3, 2))
    other = y * 2 + 1 - core
    to_right, to_left, to_other = {"row": right}, {"row": left}, {"row": other}
    loads = [
        pltpu.make_async_copy(src, dst, in_sem.at[i])
        for i, (src, dst) in enumerate(
            (
                (er, stage.at[pl.ds(0, TILES)]),
                (ec, stage.at[pl.ds(TILES, TILES)]),
                (en, stage.at[pl.ds(2 * TILES, TILES)]),
                (items, land.at[r]),
                (fetch, fetch_in),
                (slot, slot_in),
                (user, user_in),
            )
        )
    ]
    for load in loads:
        load.start()
    greet(along_x + along_z + [to_right, to_left, to_other])
    copies = Copies(send_sem, recv_sem)
    send = copies.send

    half = [items.at[pl.ds(4 * i, 4)] for i in (0, 1)]
    there = [land.at[r, pl.ds(4 * i, 4)] for i in (0, 1)]
    from_left, from_right = [None, None], [None, None]
    for i in (0, 1):
        from_left[i] = send(half[i], there[i], to_right)
        from_right[1 - i] = send(half[1 - i], there[1 - i], to_left)
    between = [send(items, land.at[r], to_other)]

    for load in loads[4:]:
        load.wait()
    small[...] = jnp.zeros_like(small)
    small[0:1, 0:TILES] = slot_in[...]
    small[1:2, 0:TILES] = user_in[...]
    slots = small[0:1]
    table = jnp.broadcast_to(fetch_in[...].astype(F32), (128, 128)).T
    ids = lax.broadcasted_iota(jnp.int32, (128, 128), 0)
    local_id = jnp.sum(jnp.where(ids == slots, table, 0.0), axis=0, keepdims=True).astype(jnp.int32)
    lanes = lax.broadcasted_iota(jnp.int32, (1, 128), 1)
    last = 3 * TILES
    stage[last : last + 1, 0:128] = jnp.where(lanes < count[0, 0], slots & (COLS - 1), -1)
    stage[last + 1 : last + 2, 0:128] = ((slots >> 4) * IB + local_id) * UB + small[1:2]
    for load in loads[:3]:
        load.wait()
    own = pltpu.make_async_copy(stage, ent.at[z, x], own_sem)
    own.start()

    first, second = pl.ds(0, HALF), pl.ds(HALF, STAGE - HALF)
    parts = (pl.ds(0, 32), pl.ds(32, 24)), (pl.ds(56, 24), pl.ds(80, 24))
    ways = (
        (first, along_x, along_z, lambda d, e: ent.at[(z + e) % NZ, (x + d) % NX]),
        (second, along_z, along_x, lambda d, e: ent.at[(z + d) % NZ, (x + e) % NX]),
    )
    near = [[None] * 4, [None] * 4]
    up = [[None] * 4, [None] * 4]
    down = [[None] * 4, [None] * 4]

    def spread(w, d, source):
        rows, _, across_way, at = ways[w]
        to = at(-d, 0).at[rows]
        up[w][d] = send(source, to, across_way[0])
        down[w][d] = send(source, to, across_way[2])

    for w, (rows, along, _, at) in enumerate(ways):
        for d in (1, 3, 2):
            near[w][d] = send(stage.at[rows], at(0, 0).at[rows], along[d - 1])
        spread(w, 0, stage.at[rows])

    far = []

    def pass_on(w, d):
        _, _, across_way, at = ways[w]
        up[w][d].wait_recv()
        piece = at(-d, -1).at[parts[w][0]]
        far.append(send(piece, piece, across_way[0]))
        down[w][d].wait_recv()
        piece = at(-d, 1).at[parts[w][1]]
        far.append(send(piece, piece, across_way[2]))

    def add(row, sums):
        def one(i, sums):
            block = land[row, i]
            high, low = split(block)
            high_t, low_t = split(block.T)
            at = row * IB + i
            yh[at] = high
            yl[at] = low
            th[at] = high_t
            tl[at] = low_t
            return sums[0] + dot(high_t, high, NN), sums[1] + dot(high_t, low, NN)

        return lax.fori_loop(0, IB, one, sums, unroll=2)

    loads[3].wait()
    zero = jnp.zeros((K, K), F32)
    sums = add(r, (zero, zero))
    for d in (1, 3, 2):
        for w in (0, 1):
            near[w][d].wait_recv()
            rows, _, _, at = ways[w]
            spread(w, d, at(-d, 0).at[rows])
    for w in (0, 1):
        pass_on(w, 0)
    from_left[0].wait_recv()
    piece = land.at[left, pl.ds(0, 4)]
    round_y = [send(piece, piece, to_right)]
    from_right[1].wait_recv()
    piece = land.at[right, pl.ds(4, 4)]
    round_y.append(send(piece, piece, to_left))
    between[0].wait_recv()
    sums = add(other, sums)
    for d in (1, 3):
        for w in (0, 1):
            pass_on(w, d)
    from_left[1].wait_recv()
    between.append(send(land.at[left], land.at[left], to_other))
    from_right[0].wait_recv()
    between.append(send(land.at[right], land.at[right], to_other))
    for w in (0, 1):
        pass_on(w, 2)
    sums = add(left, sums)
    sums = add(right, sums)
    for copy in round_y:
        copy.wait_recv()
    between.append(send(land.at[across], land.at[across], to_other))
    sums = add(across, sums)
    for copy, d in zip(between[1:], (3, 1, 2)):
        copy.wait_recv()
        sums = add(((y + d) % NY) * 2 + 1 - core, sums)
    gram[...] = sums[0] + (sums[1] + sums[1].T)
    own.wait()
    for copy in far:
        copy.wait_recv()
    copies.finish()


def gather(items, fetch, user, slot, er, ec, en, count):
    n = 6 + 4 + 2 * (3 + 8 + 8)
    return pl.pallas_call(
        gather_kernel,
        out_shape=(
            *[jax.ShapeDtypeStruct((ROWS * IB, BLOCK, K), BF16)] * 4,
            jax.ShapeDtypeStruct((K, K), F32),
            jax.ShapeDtypeStruct((NZ, NX, STAGE, NNZ), jnp.int32),
        ),
        in_specs=[ANY] * 7 + [SMEM],
        out_specs=(VMEM, VMEM, VMEM, VMEM, VMEM, ANY),
        scratch_shapes=[
            pltpu.VMEM((STAGE, NNZ), jnp.int32),
            pltpu.VMEM((ROWS, IB, BLOCK, K), F32),
            pltpu.VMEM((1, 128), jnp.int32),
            pltpu.VMEM((1, TILES), jnp.int32),
            pltpu.VMEM((1, TILES), jnp.int32),
            pltpu.VMEM((8, 128), jnp.int32),
            pltpu.SemaphoreType.DMA((n,)),
            pltpu.SemaphoreType.DMA((n,)),
            pltpu.SemaphoreType.DMA,
            pltpu.SemaphoreType.DMA((7,)),
        ],
        compiler_params=pltpu.CompilerParams(
            collective_id=0, has_side_effects=True, vmem_limit_bytes=BIG
        ),
        name="gather",
    )(items, fetch, user, slot, er, ec, en, count)


def build_kernel(
    ent, yh, yl, th, tl, gram, start, out, weights, order, meta, held, v, sem, meta_sem
):
    fetched = pltpu.make_async_copy(
        ent.at[:, pl.ds(3 * TILES, 8), pl.ds(0, 128)], meta, meta_sem
    )
    fetched.start()
    g = by_cols(*split(gram[...]))

    def begin(b, _):
        at = rows_of(b)
        both = pair(start[at])
        v[at] = both
        out[at] = -fold(dot(both, g, NN))
        return 0

    lax.fori_loop(0, UB, begin, 0, unroll=UNROLL)
    fetched.wait()
    me = lax.axis_index("col")

    def scan(c, n):
        for t in range(TILES):
            order[n] = (c * TILES + t) * (64 * UB) + meta[c, 1, t]
            n = n + jnp.where(meta[c, 0, t] == me, 1, 0)
        return n

    n = lax.fori_loop(0, COLS, scan, 0)
    order[LIST - 1] = n
    ids = lax.broadcasted_iota(jnp.int32, (BLOCK, NNZ), 0).astype(F32).astype(BF16)
    one, none = jnp.ones((), BF16), jnp.zeros((), BF16)

    def out_copy(j):
        slot = j % SLOTS
        return pltpu.make_async_copy(held.at[slot], weights.at[j], sem.at[slot])

    def group(q, _):
        for u in range(BUILD):
            j = q * BUILD + u

            @pl.when((j >= SLOTS) & (j - SLOTS < n))
            def _(j=j):
                out_copy(j - SLOTS).wait()

        for u in range(BUILD):
            j = q * BUILD + u
            code = jnp.where(j < n, order[j], 0)
            b, block, at = code % UB, (code // UB) % 64, code // (64 * UB)
            c, t = at // TILES, at % TILES
            rows = jnp.where(j < n, ent[c, pl.ds(t, 1), :], BLOCK).astype(F32).astype(BF16)
            cols = ent[c, pl.ds(TILES + t, 1), :].astype(F32).astype(BF16)
            counts = ent[c, pl.ds(2 * TILES + t, 1), :].astype(F32).astype(BF16)
            row_hot = ids == rows
            col_hot = jnp.where(ids == cols, one, none)
            ones = jnp.where(row_hot, one, none)
            many = jnp.where(row_hot, counts, none)
            both = dot(jnp.concatenate([ones, many], axis=0), col_hot, NT)
            excess = SCALE * both[BLOCK:]
            held[j % SLOTS] = excess
            where = rows_of(b)
            scores = fold(dot(v[where], by_cols(th[block], tl[block]), NN))
            pull = both[:BLOCK] + excess * (1.0 - scores)
            out[where] += fold(dot(pair(pull), by_cols(yh[block], yl[block]), NN))
        for u in range(BUILD):
            j = q * BUILD + u

            @pl.when(j < n)
            def _(j=j):
                out_copy(j).start()

        return 0

    groups = (n + BUILD - 1) // BUILD
    lax.fori_loop(0, groups, group, 0)

    def drain(j, _):
        out_copy(j).wait()
        return 0

    lax.fori_loop(jnp.maximum(groups * BUILD - SLOTS, 0), n, drain, 0)


def build(ent, yh, yl, th, tl, gram, start):
    return pl.pallas_call(
        build_kernel,
        out_shape=(
            jax.ShapeDtypeStruct((UB * BLOCK, K), F32),
            jax.ShapeDtypeStruct((ALL_TILES, BLOCK, BLOCK), F32),
            jax.ShapeDtypeStruct((LIST,), jnp.int32),
        ),
        in_specs=[VMEM] * 7,
        out_specs=(VMEM, ANY, SMEM),
        scratch_shapes=[
            pltpu.SMEM((COLS, 8, 128), jnp.int32),
            pltpu.VMEM((SLOTS, BLOCK, BLOCK), F32),
            pltpu.VMEM((UB * BLOCK, 2 * K), BF16),
            pltpu.SemaphoreType.DMA((SLOTS,)),
            pltpu.SemaphoreType.DMA,
        ],
        compiler_params=pltpu.CompilerParams(vmem_limit_bytes=BIG),
        name="build",
    )(ent, yh, yl, th, tl, gram, start)


def fetch_tiles(order, weights, held, sem, base):
    here = jnp.minimum(order[LIST - 1] - base, HELD)

    def begin(i, _):
        pltpu.make_async_copy(weights.at[base + i], held.at[i], sem.at[i]).start()
        return 0

    lax.fori_loop(0, here, begin, 0)
    return here


def each_tile(order, weights, held, sem, work):
    n = order[LIST - 1]

    def batch(k, _):
        base = k * HELD
        here = jnp.minimum(n - base, HELD)

        def group(q, _):
            for u in range(GROUP):
                i = q * GROUP + u

                @pl.when(i < here)
                def _(i=i):
                    pltpu.make_async_copy(weights.at[base + i], held.at[i], sem.at[i]).wait()

            for u in range(GROUP):
                i = q * GROUP + u
                live = i < here
                code = jnp.where(live, order[base + i], 0)
                w = jnp.where(live, held[i], 0.0)
                work(code % UB, (code // UB) % 64, w)
            return 0

        lax.fori_loop(0, (here + GROUP - 1) // GROUP, group, 0)

        @pl.when(n > base + HELD)
        def _():
            fetch_tiles(order, weights, held, sem, base + HELD)

        return 0

    lax.fori_loop(0, (n + HELD - 1) // HELD, batch, 0)


def rows_of(b):
    return pl.ds(pl.multiple_of(b * BLOCK, BLOCK), BLOCK)


def dots(a, b):
    return jnp.sum(a * b, axis=1, keepdims=True)


def pull_tiles(order, weights, held, sem, yh, yl, th, tl, v, out):
    def work(b, block, w):
        at = rows_of(b)
        scores = fold(dot(v[at], by_cols(th[block], tl[block]), NN))
        out[at] += fold(dot(pair(w * scores), by_cols(yh[block], yl[block]), NN))

    each_tile(order, weights, held, sem, work)


def first_kernel(order, total, start, yh, yl, th, tl, gram, weights, out, residual, v, held, sem):
    fetch_tiles(order, weights, held, sem, 0)
    g = by_cols(*split(gram[...]))

    def begin(b, _):
        at = rows_of(b)
        p = total[at] - RIDGE * start[at]
        residual[at] = p
        both = pair(p)
        v[at] = both
        out[at] = fold(dot(both, g, NN))
        return 0

    lax.fori_loop(0, UB, begin, 0, unroll=UNROLL)
    pull_tiles(order, weights, held, sem, yh, yl, th, tl, v, out)


def update(total, iterate, residual, direction):
    image = total + RIDGE * direction
    now = dots(residual, residual)
    alpha = now / (dots(direction, image) + EPSILON)
    iterate = iterate + alpha * direction
    residual = residual - alpha * image
    after = dots(residual, residual)
    direction = residual + after / (now + EPSILON) * direction
    return iterate, residual, direction


def second_kernel(
    order, total, iterate, residual, yh, yl, th, tl, gram, weights, out, new_x, new_r, new_p, v, held, sem
):
    fetch_tiles(order, weights, held, sem, 0)
    g = by_cols(*split(gram[...]))

    def begin(b, _):
        at = rows_of(b)
        r = residual[at]
        new_x[at], new_r[at], p = update(total[at], iterate[at], r, r)
        new_p[at] = p
        both = pair(p)
        v[at] = both
        out[at] = fold(dot(both, g, NN))
        return 0

    lax.fori_loop(0, UB, begin, 0, unroll=UNROLL)
    pull_tiles(order, weights, held, sem, yh, yl, th, tl, v, out)


def third_kernel(
    order, total, iterate, residual, direction, yh, yl, th, tl, gram, weights,
    squares, new_x, new_r, new_p, v, acc, held, sem,
):
    fetch_tiles(order, weights, held, sem, 0)
    g = by_cols(*split(gram[...]))

    def begin(b, _):
        at = rows_of(b)
        new_x[at], new_r[at], p = update(total[at], iterate[at], residual[at], direction[at])
        new_p[at] = p
        both = pair(p)
        v[at] = both
        acc[at] = p * fold(dot(both, g, NN))
        return 0

    lax.fori_loop(0, UB, begin, 0, unroll=UNROLL)

    def work(b, block, w):
        at = rows_of(b)
        scores = fold(dot(v[at], by_cols(th[block], tl[block]), NN))
        acc[at] += w * scores * scores

    each_tile(order, weights, held, sem, work)
    for b in range(UB):
        squares[b : b + 1] = jnp.sum(acc[b * BLOCK : (b + 1) * BLOCK].T, axis=0, keepdims=True)


def last_kernel(squares, iterate, residual, direction, out):
    sums = squares[...]
    for b in range(UB):
        at = pl.ds(b * BLOCK, BLOCK)
        p = direction[at]
        r = residual[at]
        below = jnp.broadcast_to(sums[b : b + 1], (BLOCK, BLOCK)).T + RIDGE * dots(p, p)
        out[at] = iterate[at] + dots(r, r) / (below + EPSILON) * p


USERS = jax.ShapeDtypeStruct((UB * BLOCK, K), F32)


def local(kernel, name, outs, specs, scratch=()):
    tiles = [
        pltpu.VMEM((UB * BLOCK, 2 * K), BF16),
        *scratch,
        pltpu.VMEM((HELD, BLOCK, BLOCK), F32),
        pltpu.SemaphoreType.DMA((HELD,)),
    ]
    return pl.pallas_call(
        kernel,
        out_shape=outs,
        in_specs=specs,
        out_specs=tuple(VMEM for _ in outs),
        scratch_shapes=tiles,
        compiler_params=pltpu.CompilerParams(vmem_limit_bytes=BIG),
        name=name,
    )


def reduce_kernel(part, out, land_a, land_b, sum_a, sum_b, near_a, near_b, send_sem, recv_sem):
    c, z, x, along_x, along_z = col_place()
    greet(along_x + along_z)
    copies = Copies(send_sem, recv_sem)
    send = copies.send
    upper, lower = pl.ds(0, 64), pl.ds(64, 64)
    step_a = [
        send(part.at[:, (x + d) % NX, upper], land_a.at[d - 1], along_x[d - 1]) for d in (1, 2, 3)
    ]
    step_b = [
        send(part.at[(z + d) % NZ, :, lower], land_b.at[d - 1], along_z[d - 1]) for d in (1, 2, 3)
    ]
    for copy in step_a:
        copy.wait_recv()
    sum_a[...] = part[:, x, 0:64] + land_a[0] + (land_a[1] + land_a[2])
    next_a = [
        send(sum_a.at[(z + d) % NZ], near_a.at[d - 1], along_z[d - 1]) for d in (1, 2, 3)
    ]
    for copy in step_b:
        copy.wait_recv()
    sum_b[...] = part[z, :, 64:128] + land_b[0] + (land_b[1] + land_b[2])
    next_b = [
        send(sum_b.at[(x + d) % NX], near_b.at[d - 1], along_x[d - 1]) for d in (1, 2, 3)
    ]
    for copy in next_a:
        copy.wait_recv()
    out[z, x, 0:64] = sum_a[z] + near_a[0] + (near_a[1] + near_a[2])
    here = out.at[z, x, upper]
    back_a = [send(here, here, peer) for peer in along_z]
    for copy in next_b:
        copy.wait_recv()
    out[z, x, 64:128] = sum_b[x] + near_b[0] + (near_b[1] + near_b[2])
    here = out.at[z, x, lower]
    back_b = [send(here, here, peer) for peer in along_x]
    for copy in back_a:
        copy.wait_recv()
    line = out.at[:, x, upper]
    end = [send(line, line, peer) for peer in along_x]
    for copy in back_b:
        copy.wait_recv()
    line = out.at[z, :, lower]
    end += [send(line, line, peer) for peer in along_z]
    for copy in end:
        copy.wait_recv()
    copies.finish()


def reduce(part):
    out = pl.pallas_call(
        reduce_kernel,
        out_shape=jax.ShapeDtypeStruct((NZ, NX, BLOCK, K), F32),
        in_specs=[VMEM],
        out_specs=VMEM,
        scratch_shapes=[
            pltpu.VMEM((3, 4, 64, K), F32),
            pltpu.VMEM((3, 4, 64, K), F32),
            pltpu.VMEM((4, 64, K), F32),
            pltpu.VMEM((4, 64, K), F32),
            pltpu.VMEM((3, 64, K), F32),
            pltpu.VMEM((3, 64, K), F32),
            pltpu.SemaphoreType.DMA((24,)),
            pltpu.SemaphoreType.DMA((24,)),
        ],
        compiler_params=pltpu.CompilerParams(
            collective_id=1, has_side_effects=True, vmem_limit_bytes=BIG
        ),
        name="reduce",
    )(part.reshape(NZ, NX, BLOCK, K))
    return out.reshape(UB * BLOCK, K)


def scalars_kernel(mine, out, land_x, land_z, half, send_sem, recv_sem):
    _, _, _, along_x, along_z = col_place()
    greet(along_x + along_z)
    copies = Copies(send_sem, recv_sem)
    for copy in [copies.send(mine, land_x.at[i], peer) for i, peer in enumerate(along_x)]:
        copy.wait_recv()
    half[...] = mine[...] + land_x[0] + (land_x[1] + land_x[2])
    for copy in [copies.send(half, land_z.at[i], peer) for i, peer in enumerate(along_z)]:
        copy.wait_recv()
    out[...] = half[...] + land_z[0] + (land_z[1] + land_z[2])
    copies.finish()


def sum_scalars(mine):
    return pl.pallas_call(
        scalars_kernel,
        out_shape=jax.ShapeDtypeStruct((UB, BLOCK), F32),
        in_specs=[VMEM],
        out_specs=VMEM,
        scratch_shapes=[
            pltpu.VMEM((3, UB, BLOCK), F32),
            pltpu.VMEM((3, UB, BLOCK), F32),
            pltpu.VMEM((UB, BLOCK), F32),
            pltpu.SemaphoreType.DMA((6,)),
            pltpu.SemaphoreType.DMA((6,)),
        ],
        compiler_params=pltpu.CompilerParams(collective_id=2, has_side_effects=True),
        name="scalars",
    )(mine)


def shards(user_factors, item_factors, fetch_list, tile_user, tile_slot, er, ec, en, tile_count):
    yh, yl, th, tl, gram, ent = gather(
        item_factors.reshape(IB, BLOCK, K),
        fetch_list.reshape(1, 128),
        tile_user.reshape(1, TILES),
        tile_slot.reshape(1, TILES),
        er.reshape(TILES, NNZ),
        ec.reshape(TILES, NNZ),
        en.reshape(TILES, NNZ),
        tile_count.reshape(1, 1),
    )
    part, weights, order = build(
        ent.reshape(COLS, STAGE, NNZ), yh, yl, th, tl, gram, user_factors
    )
    total = reduce(part)
    tail = [VMEM] * 5 + [ANY]
    part, residual = local(first_kernel, "first", (USERS,) * 2, [SMEM, VMEM, VMEM] + tail)(
        order, total, user_factors, yh, yl, th, tl, gram, weights
    )
    total = reduce(part)
    part, iterate, residual, direction = local(
        second_kernel, "second", (USERS,) * 4, [SMEM] + [VMEM] * 3 + tail
    )(order, total, user_factors, residual, yh, yl, th, tl, gram, weights)
    total = reduce(part)
    squares = jax.ShapeDtypeStruct((UB, BLOCK), F32)
    part, iterate, residual, direction = local(
        third_kernel,
        "third",
        (squares,) + (USERS,) * 3,
        [SMEM] + [VMEM] * 4 + tail,
        [pltpu.VMEM((UB * BLOCK, K), F32)],
    )(order, total, iterate, residual, direction, yh, yl, th, tl, gram, weights)
    squares = sum_scalars(part)
    return pl.pallas_call(
        last_kernel,
        out_shape=USERS,
        in_specs=[VMEM] * 4,
        out_specs=VMEM,
        compiler_params=pltpu.CompilerParams(vmem_limit_bytes=BIG),
        name="last",
    )(squares, iterate, residual, direction)


def solution(mesh):
    return jax.shard_map(
        shards,
        mesh=mesh,
        in_specs=(
            P("row", None),
            P(("row", "col"), None),
            P("row", "col", None, None),
            P("row", "col", None),
            P("row", "col", None),
            P("row", "col", None, None),
            P("row", "col", None, None),
            P("row", "col", None, None),
            P("row", "col"),
        ),
        out_specs=P("row", None),
        check_vma=False,
    )
```

```python
import functools

import jax
import jax.numpy as jnp
from jax import lax
from jax.experimental import pallas as pl
from jax.experimental.pallas import tpu as pltpu
from jax.sharding import PartitionSpec as P

K = 128
BLOCK = 128
UB = 16
IB = 8
TILES = 32
NNZ = 512
NZ = NX = 4
NY = 4
ROWS = 8
COLS = 16
ALL_TILES = COLS * TILES
LIST = 1024
SUB = 32
UNROLL = 4
BUILD = 4
SLOTS = 2 * BUILD
GROUP = 4
HELD = 32
STAGE = 3 * TILES + 8
HALF = 56
SCALE = 40.0
RIDGE = 0.5
EPSILON = 1e-06
MESH = pl.DeviceIdType.MESH
F32 = jnp.float32
BF16 = jnp.bfloat16
NT = (((1,), (1,)), ((), ()))
NN = (((1,), (0,)), ((), ()))
ANY = pl.BlockSpec(memory_space=pl.ANY)
VMEM = pl.BlockSpec(memory_space=pltpu.VMEM)
SMEM = pl.BlockSpec(memory_space=pltpu.SMEM)
HBM = pl.BlockSpec(memory_space=pltpu.HBM)
BIG = 24 * 2**20


def dot(a, b, dims):
    return lax.dot_general(a, b, dims, preferred_element_type=F32)


def split(a):
    high = a.astype(BF16)
    return high, (a - high.astype(F32)).astype(BF16)


def pair(a):
    return jnp.concatenate(split(a), axis=1)


def fold(wide):
    return wide[:, 0:128] + wide[:, 128:256]


def by_cols(high, low):
    both = jnp.concatenate([high, low], axis=1)
    return jnp.concatenate([both, both], axis=0)


def greet(peers):
    barrier = pltpu.get_barrier_semaphore()
    for peer in peers:
        pl.semaphore_signal(barrier, inc=1, device_id=peer, device_id_type=MESH)
    pl.semaphore_wait(barrier, len(peers))


class Copies:
    def __init__(self, send_sem, recv_sem):
        self.send_sem, self.recv_sem, self.made = send_sem, recv_sem, []

    def send(self, src, dst, peer):
        i = len(self.made)
        copy = pltpu.make_async_remote_copy(
            src_ref=src,
            dst_ref=dst,
            send_sem=self.send_sem.at[i],
            recv_sem=self.recv_sem.at[i],
            device_id=peer,
            device_id_type=MESH,
        )
        copy.start()
        self.made.append(copy)
        return copy

    def finish(self):
        for copy in self.made:
            copy.wait_send()


def col_place():
    c = lax.axis_index("col")
    z, x = c // NX, c % NX
    along_x = [{"col": z * NX + (x + d) % NX} for d in range(1, NX)]
    along_z = [{"col": ((z + d) % NZ) * NX + x} for d in range(1, NZ)]
    return c, z, x, along_x, along_z


def gather_kernel(
    items, fetch, user, slot, er, ec, en, count, yh, yl, th, tl, gram, ent,
    stage, land, fetch_in, slot_in, user_in, small, send_sem, recv_sem, own_sem, in_sem,
):
    c, z, x, along_x, along_z = col_place()
    r = lax.axis_index("row")
    y, core = r // 2, r % 2
    right, left, across = (((y + d) % NY) * 2 + core for d in (1, 3, 2))
    other = y * 2 + 1 - core
    to_right, to_left, to_other = {"row": right}, {"row": left}, {"row": other}
    loads = [
        pltpu.make_async_copy(src, dst, in_sem.at[i])
        for i, (src, dst) in enumerate(
            (
                (er, stage.at[pl.ds(0, TILES)]),
                (ec, stage.at[pl.ds(TILES, TILES)]),
                (en, stage.at[pl.ds(2 * TILES, TILES)]),
                (items, land.at[r]),
                (fetch, fetch_in),
                (slot, slot_in),
                (user, user_in),
            )
        )
    ]
    for load in loads:
        load.start()
    greet(along_x + along_z + [to_right, to_left, to_other])
    copies = Copies(send_sem, recv_sem)
    send = copies.send

    half = [items.at[pl.ds(4 * i, 4)] for i in (0, 1)]
    there = [land.at[r, pl.ds(4 * i, 4)] for i in (0, 1)]
    from_left, from_right = [None, None], [None, None]
    for i in (0, 1):
        from_left[i] = send(half[i], there[i], to_right)
        from_right[1 - i] = send(half[1 - i], there[1 - i], to_left)
    between = [send(items, land.at[r], to_other)]

    for load in loads[4:]:
        load.wait()
    small[...] = jnp.zeros_like(small)
    small[0:1, 0:TILES] = slot_in[...]
    small[1:2, 0:TILES] = user_in[...]
    slots = small[0:1]
    table = jnp.broadcast_to(fetch_in[...].astype(F32), (128, 128)).T
    ids = lax.broadcasted_iota(jnp.int32, (128, 128), 0)
    local_id = jnp.sum(jnp.where(ids == slots, table, 0.0), axis=0, keepdims=True).astype(jnp.int32)
    lanes = lax.broadcasted_iota(jnp.int32, (1, 128), 1)
    last = 3 * TILES
    stage[last : last + 1, 0:128] = jnp.where(lanes < count[0, 0], slots & (COLS - 1), -1)
    stage[last + 1 : last + 2, 0:128] = ((slots >> 4) * IB + local_id) * UB + small[1:2]
    for load in loads[:3]:
        load.wait()
    own = pltpu.make_async_copy(stage, ent.at[z, x], own_sem)
    own.start()

    first, second = pl.ds(0, HALF), pl.ds(HALF, STAGE - HALF)
    parts = (pl.ds(0, 32), pl.ds(32, 24)), (pl.ds(56, 24), pl.ds(80, 24))
    ways = (
        (first, along_x, along_z, lambda d, e: ent.at[(z + e) % NZ, (x + d) % NX]),
        (second, along_z, along_x, lambda d, e: ent.at[(z + d) % NZ, (x + e) % NX]),
    )
    near = [[None] * 4, [None] * 4]
    up = [[None] * 4, [None] * 4]
    down = [[None] * 4, [None] * 4]

    def spread(w, d, source):
        rows, _, across_way, at = ways[w]
        to = at(-d, 0).at[rows]
        up[w][d] = send(source, to, across_way[0])
        down[w][d] = send(source, to, across_way[2])

    for w, (rows, along, _, at) in enumerate(ways):
        for d in (1, 3, 2):
            near[w][d] = send(stage.at[rows], at(0, 0).at[rows], along[d - 1])
        spread(w, 0, stage.at[rows])

    far = []

    def pass_on(w, d):
        _, _, across_way, at = ways[w]
        up[w][d].wait_recv()
        piece = at(-d, -1).at[parts[w][0]]
        far.append(send(piece, piece, across_way[0]))
        down[w][d].wait_recv()
        piece = at(-d, 1).at[parts[w][1]]
        far.append(send(piece, piece, across_way[2]))

    def add(row, sums):
        def one(i, sums):
            high, low = split(land[row, i])
            high_t = high.T
            at = row * IB + i
            yh[at] = high
            yl[at] = low
            th[at] = high_t
            tl[at] = low.T
            return sums + dot(high_t, jnp.concatenate([high, low], axis=1), NN)

        return lax.fori_loop(0, IB, one, sums, unroll=4)

    loads[3].wait()
    sums = add(r, jnp.zeros((K, 2 * K), F32))
    for d in (1, 3, 2):
        for w in (0, 1):
            near[w][d].wait_recv()
            rows, _, _, at = ways[w]
            spread(w, d, at(-d, 0).at[rows])
    for w in (0, 1):
        pass_on(w, 0)
    from_left[0].wait_recv()
    piece = land.at[left, pl.ds(0, 4)]
    round_y = [send(piece, piece, to_right)]
    from_right[1].wait_recv()
    piece = land.at[right, pl.ds(4, 4)]
    round_y.append(send(piece, piece, to_left))
    between[0].wait_recv()
    sums = add(other, sums)
    for d in (1, 3):
        for w in (0, 1):
            pass_on(w, d)
    from_left[1].wait_recv()
    between.append(send(land.at[left], land.at[left], to_other))
    from_right[0].wait_recv()
    between.append(send(land.at[right], land.at[right], to_other))
    for w in (0, 1):
        pass_on(w, 2)
    sums = add(left, sums)
    sums = add(right, sums)
    for copy in round_y:
        copy.wait_recv()
    between.append(send(land.at[across], land.at[across], to_other))
    sums = add(across, sums)
    for copy, d in zip(between[1:], (3, 1, 2)):
        copy.wait_recv()
        sums = add(((y + d) % NY) * 2 + 1 - core, sums)
    mixed = sums[:, K:]
    gram[...] = sums[:, :K] + (mixed + mixed.T)
    own.wait()
    for copy in far:
        copy.wait_recv()
    copies.finish()


def gather(items, fetch, user, slot, er, ec, en, count):
    n = 6 + 4 + 2 * (3 + 8 + 8)
    return pl.pallas_call(
        gather_kernel,
        out_shape=(
            *[jax.ShapeDtypeStruct((ROWS * IB, BLOCK, K), BF16)] * 4,
            jax.ShapeDtypeStruct((K, K), F32),
            jax.ShapeDtypeStruct((NZ, NX, STAGE, NNZ), jnp.int32),
        ),
        in_specs=[HBM] * 7 + [SMEM],
        out_specs=(VMEM, VMEM, VMEM, VMEM, VMEM, ANY),
        scratch_shapes=[
            pltpu.VMEM((STAGE, NNZ), jnp.int32),
            pltpu.VMEM((ROWS, IB, BLOCK, K), F32),
            pltpu.VMEM((1, 128), jnp.int32),
            pltpu.VMEM((1, TILES), jnp.int32),
            pltpu.VMEM((1, TILES), jnp.int32),
            pltpu.VMEM((8, 128), jnp.int32),
            pltpu.SemaphoreType.DMA((n,)),
            pltpu.SemaphoreType.DMA((n,)),
            pltpu.SemaphoreType.DMA,
            pltpu.SemaphoreType.DMA((7,)),
        ],
        compiler_params=pltpu.CompilerParams(
            collective_id=0, has_side_effects=True, vmem_limit_bytes=BIG
        ),
        name="gather",
    )(*[pltpu.with_memory_space_constraint(a, pltpu.HBM) for a in (items, fetch, user, slot, er, ec, en)], count)


def build_kernel(
    ent, yh, yl, th, tl, gram, start, out, weights, order, meta, held, v, sem, meta_sem
):
    fetched = pltpu.make_async_copy(
        ent.at[:, pl.ds(3 * TILES, 8), pl.ds(0, 128)], meta, meta_sem
    )
    fetched.start()
    g = by_cols(*split(gram[...]))

    def begin(b, _):
        at = rows_of(b)
        both = pair(start[at])
        v[at] = both
        out[at] = -fold(dot(both, g, NN))
        return 0

    lax.fori_loop(0, UB, begin, 0, unroll=UNROLL)
    fetched.wait()
    me = lax.axis_index("col")

    def scan(c, n):
        for t in range(TILES):
            order[n] = (c * TILES + t) * (64 * UB) + meta[c, 1, t]
            n = n + jnp.where(meta[c, 0, t] == me, 1, 0)
        return n

    n = lax.fori_loop(0, COLS, scan, 0)
    order[LIST - 1] = n
    ids = lax.broadcasted_iota(jnp.int32, (BLOCK, NNZ), 0).astype(F32).astype(BF16)
    one, none = jnp.ones((), BF16), jnp.zeros((), BF16)

    def out_copy(j):
        slot = j % SLOTS
        return pltpu.make_async_copy(held.at[slot], weights.at[j], sem.at[slot])

    def group(q, _):
        for u in range(BUILD):
            j = q * BUILD + u

            @pl.when((j >= SLOTS) & (j - SLOTS < n))
            def _(j=j):
                out_copy(j - SLOTS).wait()

        for u in range(BUILD):
            j = q * BUILD + u
            code = jnp.where(j < n, order[j], 0)
            b, block, at = code % UB, (code // UB) % 64, code // (64 * UB)
            c, t = at // TILES, at % TILES
            rows = jnp.where(j < n, ent[c, pl.ds(t, 1), :], BLOCK).astype(F32).astype(BF16)
            cols = ent[c, pl.ds(TILES + t, 1), :].astype(F32).astype(BF16)
            counts = ent[c, pl.ds(2 * TILES + t, 1), :].astype(F32).astype(BF16)
            row_hot = ids == rows
            col_hot = jnp.where(ids == cols, one, none)
            ones = jnp.where(row_hot, one, none)
            many = jnp.where(row_hot, counts, none)
            both = dot(jnp.concatenate([ones, many], axis=0), col_hot, NT)
            excess = SCALE * both[BLOCK:]
            held[j % SLOTS] = excess
            where = rows_of(b)
            scores = fold(dot(v[where], by_cols(th[block], tl[block]), NN))
            pull = both[:BLOCK] + excess * (1.0 - scores)
            out[where] += fold(dot(pair(pull), by_cols(yh[block], yl[block]), NN))
        for u in range(BUILD):
            j = q * BUILD + u

            @pl.when(j < n)
            def _(j=j):
                out_copy(j).start()

        return 0

    groups = (n + BUILD - 1) // BUILD
    lax.fori_loop(0, groups, group, 0)

    def drain(j, _):
        out_copy(j).wait()
        return 0

    lax.fori_loop(jnp.maximum(groups * BUILD - SLOTS, 0), n, drain, 0)


def build(ent, yh, yl, th, tl, gram, start):
    return pl.pallas_call(
        build_kernel,
        out_shape=(
            jax.ShapeDtypeStruct((UB * BLOCK, K), F32),
            jax.ShapeDtypeStruct((ALL_TILES, BLOCK, BLOCK), F32),
            jax.ShapeDtypeStruct((LIST,), jnp.int32),
        ),
        in_specs=[VMEM] * 7,
        out_specs=(VMEM, ANY, SMEM),
        scratch_shapes=[
            pltpu.SMEM((COLS, 8, 128), jnp.int32),
            pltpu.VMEM((SLOTS, BLOCK, BLOCK), F32),
            pltpu.VMEM((UB * BLOCK, 2 * K), BF16),
            pltpu.SemaphoreType.DMA((SLOTS,)),
            pltpu.SemaphoreType.DMA,
        ],
        compiler_params=pltpu.CompilerParams(vmem_limit_bytes=BIG),
        name="build",
    )(ent, yh, yl, th, tl, gram, start)


def fetch_tiles(order, weights, held, sem, base):
    here = jnp.minimum(order[LIST - 1] - base, HELD)

    def begin(i, _):
        pltpu.make_async_copy(weights.at[base + i], held.at[i], sem.at[i]).start()
        return 0

    lax.fori_loop(0, here, begin, 0)
    return here


def each_tile(order, weights, held, sem, work):
    n = order[LIST - 1]

    def batch(k, _):
        base = k * HELD
        here = jnp.minimum(n - base, HELD)

        def group(q, _):
            for u in range(GROUP):
                i = q * GROUP + u

                @pl.when(i < here)
                def _(i=i):
                    pltpu.make_async_copy(weights.at[base + i], held.at[i], sem.at[i]).wait()

            for u in range(GROUP):
                i = q * GROUP + u
                live = i < here
                code = jnp.where(live, order[base + i], 0)
                w = jnp.where(live, held[i], 0.0)
                work(code % UB, (code // UB) % 64, w)
            return 0

        lax.fori_loop(0, (here + GROUP - 1) // GROUP, group, 0)

        @pl.when(n > base + HELD)
        def _():
            fetch_tiles(order, weights, held, sem, base + HELD)

        return 0

    lax.fori_loop(0, (n + HELD - 1) // HELD, batch, 0)


def rows_of(b):
    return pl.ds(pl.multiple_of(b * BLOCK, BLOCK), BLOCK)


def dots(a, b):
    return jnp.sum(a * b, axis=1, keepdims=True)


def pull_tiles(order, weights, held, sem, yh, yl, th, tl, v, out):
    def work(b, block, w):
        at = rows_of(b)
        scores = fold(dot(v[at], by_cols(th[block], tl[block]), NN))
        out[at] += fold(dot(pair(w * scores), by_cols(yh[block], yl[block]), NN))

    each_tile(order, weights, held, sem, work)


def first_kernel(order, total, start, yh, yl, th, tl, gram, weights, out, residual, v, held, sem):
    fetch_tiles(order, weights, held, sem, 0)
    g = by_cols(*split(gram[...]))

    def begin(b, _):
        at = rows_of(b)
        p = total[at] - RIDGE * start[at]
        residual[at] = p
        both = pair(p)
        v[at] = both
        out[at] = fold(dot(both, g, NN))
        return 0

    lax.fori_loop(0, UB, begin, 0, unroll=UNROLL)
    pull_tiles(order, weights, held, sem, yh, yl, th, tl, v, out)


def update(total, iterate, residual, direction):
    image = total + RIDGE * direction
    now = dots(residual, residual)
    alpha = now / (dots(direction, image) + EPSILON)
    iterate = iterate + alpha * direction
    residual = residual - alpha * image
    after = dots(residual, residual)
    direction = residual + after / (now + EPSILON) * direction
    return iterate, residual, direction


def second_kernel(
    order, total, iterate, residual, yh, yl, th, tl, gram, weights, out, new_x, new_r, new_p, v, held, sem
):
    fetch_tiles(order, weights, held, sem, 0)
    g = by_cols(*split(gram[...]))

    def begin(b, _):
        at = rows_of(b)
        r = residual[at]
        new_x[at], new_r[at], p = update(total[at], iterate[at], r, r)
        new_p[at] = p
        both = pair(p)
        v[at] = both
        out[at] = fold(dot(both, g, NN))
        return 0

    lax.fori_loop(0, UB, begin, 0, unroll=UNROLL)
    pull_tiles(order, weights, held, sem, yh, yl, th, tl, v, out)


def third_kernel(
    order, total, iterate, residual, direction, yh, yl, th, tl, gram, weights,
    squares, new_x, new_r, new_p, v, acc, held, sem,
):
    fetch_tiles(order, weights, held, sem, 0)
    g = by_cols(*split(gram[...]))

    def begin(b, _):
        at = rows_of(b)
        new_x[at], new_r[at], p = update(total[at], iterate[at], residual[at], direction[at])
        new_p[at] = p
        both = pair(p)
        v[at] = both
        acc[at] = p * fold(dot(both, g, NN))
        return 0

    lax.fori_loop(0, UB, begin, 0, unroll=UNROLL)

    def work(b, block, w):
        at = rows_of(b)
        scores = fold(dot(v[at], by_cols(th[block], tl[block]), NN))
        acc[at] += w * scores * scores

    each_tile(order, weights, held, sem, work)
    for b in range(UB):
        squares[b : b + 1] = jnp.sum(acc[b * BLOCK : (b + 1) * BLOCK].T, axis=0, keepdims=True)


def last_kernel(squares, iterate, residual, direction, out):
    sums = squares[...]
    for b in range(UB):
        at = pl.ds(b * BLOCK, BLOCK)
        p = direction[at]
        r = residual[at]
        below = jnp.broadcast_to(sums[b : b + 1], (BLOCK, BLOCK)).T + RIDGE * dots(p, p)
        out[at] = iterate[at] + dots(r, r) / (below + EPSILON) * p


USERS = jax.ShapeDtypeStruct((UB * BLOCK, K), F32)


def local(kernel, name, outs, specs, scratch=()):
    tiles = [
        pltpu.VMEM((UB * BLOCK, 2 * K), BF16),
        *scratch,
        pltpu.VMEM((HELD, BLOCK, BLOCK), F32),
        pltpu.SemaphoreType.DMA((HELD,)),
    ]
    return pl.pallas_call(
        kernel,
        out_shape=outs,
        in_specs=specs,
        out_specs=tuple(VMEM for _ in outs),
        scratch_shapes=tiles,
        compiler_params=pltpu.CompilerParams(vmem_limit_bytes=BIG),
        name=name,
    )


def reduce_kernel(part, out, land, sums, near, send_sem, recv_sem):
    c, z, x, along_x, along_z = col_place()
    greet(along_x + along_z)
    copies = Copies(send_sem, recv_sem)
    send = copies.send
    streams = [(pl.ds(SUB * i, SUB), i % 2 == 0) for i in range(BLOCK // SUB)]

    def line(ref, way, d, rows):
        return ref.at[:, (x + d) % NX, rows] if way else ref.at[(z + d) % NZ, :, rows]

    def axes(way):
        return (along_x, along_z, z) if way else (along_z, along_x, x)

    far = [
        [send(line(part, way, d, rows), land.at[i, d - 1], axes(way)[0][d - 1]) for d in (1, 2, 3)]
        for i, (rows, way) in enumerate(streams)
    ]
    close = []
    for i, (rows, way) in enumerate(streams):
        _, along, me = axes(way)
        for copy in far[i]:
            copy.wait_recv()
        mine = part[:, x, rows] if way else part[z, :, rows]
        sums[i] = mine + land[i, 0] + (land[i, 1] + land[i, 2])
        close.append(
            [send(sums.at[i, (me + d) % 4], near.at[i, d - 1], along[d - 1]) for d in (1, 2, 3)]
        )
    back = []
    for i, (rows, way) in enumerate(streams):
        _, along, me = axes(way)
        for copy in close[i]:
            copy.wait_recv()
        out[z, x, rows] = sums[i, me] + near[i, 0] + (near[i, 1] + near[i, 2])
        here = out.at[z, x, rows]
        back.append([send(here, here, peer) for peer in along])
    end = []
    for i, (rows, way) in enumerate(streams):
        for copy in back[i]:
            copy.wait_recv()
        here = line(out, way, 0, rows)
        end += [send(here, here, peer) for peer in axes(way)[0]]
    for copy in end:
        copy.wait_recv()
    copies.finish()


def reduce(part):
    n = BLOCK // SUB
    out = pl.pallas_call(
        reduce_kernel,
        out_shape=jax.ShapeDtypeStruct((NZ, NX, BLOCK, K), F32),
        in_specs=[VMEM],
        out_specs=VMEM,
        scratch_shapes=[
            pltpu.VMEM((n, 3, 4, SUB, K), F32),
            pltpu.VMEM((n, 4, SUB, K), F32),
            pltpu.VMEM((n, 3, SUB, K), F32),
            pltpu.SemaphoreType.DMA((12 * n,)),
            pltpu.SemaphoreType.DMA((12 * n,)),
        ],
        compiler_params=pltpu.CompilerParams(
            collective_id=1, has_side_effects=True, vmem_limit_bytes=BIG
        ),
        name="reduce",
    )(part.reshape(NZ, NX, BLOCK, K))
    return out.reshape(UB * BLOCK, K)


def scalars_kernel(mine, out, land_x, land_z, half, send_sem, recv_sem):
    _, _, _, along_x, along_z = col_place()
    greet(along_x + along_z)
    copies = Copies(send_sem, recv_sem)
    for copy in [copies.send(mine, land_x.at[i], peer) for i, peer in enumerate(along_x)]:
        copy.wait_recv()
    half[...] = mine[...] + land_x[0] + (land_x[1] + land_x[2])
    for copy in [copies.send(half, land_z.at[i], peer) for i, peer in enumerate(along_z)]:
        copy.wait_recv()
    out[...] = half[...] + land_z[0] + (land_z[1] + land_z[2])
    copies.finish()


def sum_scalars(mine):
    return pl.pallas_call(
        scalars_kernel,
        out_shape=jax.ShapeDtypeStruct((UB, BLOCK), F32),
        in_specs=[VMEM],
        out_specs=VMEM,
        scratch_shapes=[
            pltpu.VMEM((3, UB, BLOCK), F32),
            pltpu.VMEM((3, UB, BLOCK), F32),
            pltpu.VMEM((UB, BLOCK), F32),
            pltpu.SemaphoreType.DMA((6,)),
            pltpu.SemaphoreType.DMA((6,)),
        ],
        compiler_params=pltpu.CompilerParams(collective_id=2, has_side_effects=True, vmem_limit_bytes=BIG),
        name="scalars",
    )(mine)


def shards(user_factors, item_factors, fetch_list, tile_user, tile_slot, er, ec, en, tile_count):
    yh, yl, th, tl, gram, ent = gather(
        item_factors.reshape(IB, BLOCK, K),
        fetch_list.reshape(1, 128),
        tile_user.reshape(1, TILES),
        tile_slot.reshape(1, TILES),
        er.reshape(TILES, NNZ),
        ec.reshape(TILES, NNZ),
        en.reshape(TILES, NNZ),
        tile_count.reshape(1, 1),
    )
    part, weights, order = build(
        ent.reshape(COLS, STAGE, NNZ), yh, yl, th, tl, gram, user_factors
    )
    total = reduce(part)
    tail = [VMEM] * 5 + [ANY]
    part, residual = local(first_kernel, "first", (USERS,) * 2, [SMEM, VMEM, VMEM] + tail)(
        order, total, user_factors, yh, yl, th, tl, gram, weights
    )
    total = reduce(part)
    part, iterate, residual, direction = local(
        second_kernel, "second", (USERS,) * 4, [SMEM] + [VMEM] * 3 + tail
    )(order, total, user_factors, residual, yh, yl, th, tl, gram, weights)
    total = reduce(part)
    squares = jax.ShapeDtypeStruct((UB, BLOCK), F32)
    part, iterate, residual, direction = local(
        third_kernel,
        "third",
        (squares,) + (USERS,) * 3,
        [SMEM] + [VMEM] * 4 + tail,
        [pltpu.VMEM((UB * BLOCK, K), F32)],
    )(order, total, iterate, residual, direction, yh, yl, th, tl, gram, weights)
    squares = sum_scalars(part)
    return pl.pallas_call(
        last_kernel,
        out_shape=USERS,
        in_specs=[VMEM] * 4,
        out_specs=VMEM,
        compiler_params=pltpu.CompilerParams(vmem_limit_bytes=BIG),
        name="last",
    )(squares, iterate, residual, direction)


def solution(mesh):
    return jax.shard_map(
        shards,
        mesh=mesh,
        in_specs=(
            P("row", None),
            P(("row", "col"), None),
            P("row", "col", None, None),
            P("row", "col", None),
            P("row", "col", None),
            P("row", "col", None, None),
            P("row", "col", None, None),
            P("row", "col", None, None),
            P("row", "col"),
        ),
        out_specs=P("row", None),
        check_vma=False,
    )
```

```python
import functools

import jax
import jax.numpy as jnp
from jax import lax
from jax.experimental import pallas as pl
from jax.experimental.pallas import tpu as pltpu
from jax.sharding import PartitionSpec as P

K = 128
BLOCK = 128
UB = 16
IB = 8
TILES = 32
NNZ = 512
NZ = NX = 4
NY = 4
ROWS = 8
COLS = 16
ALL_TILES = COLS * TILES
LIST = 1024
LAST = 512
FAST = 40
QUARTER = 10
STEP = 5
SUB = 32
UNROLL = 4
BUILD = 4
SLOTS = 2 * BUILD
GROUP = 4
HELD = 32
STAGE = 3 * TILES + 8
HALF = 56
SCALE = 40.0
RIDGE = 0.5
EPSILON = 1e-06
MESH = pl.DeviceIdType.MESH
F32 = jnp.float32
BF16 = jnp.bfloat16
NT = (((1,), (1,)), ((), ()))
NN = (((1,), (0,)), ((), ()))
ANY = pl.BlockSpec(memory_space=pl.ANY)
VMEM = pl.BlockSpec(memory_space=pltpu.VMEM)
SMEM = pl.BlockSpec(memory_space=pltpu.SMEM)
HBM = pl.BlockSpec(memory_space=pltpu.HBM)
BIG = 24 * 2**20
WHOLE = 40 * 2**20


def dot(a, b, dims):
    return lax.dot_general(a, b, dims, preferred_element_type=F32)


def split(a):
    high = a.astype(BF16)
    return high, (a - high.astype(F32)).astype(BF16)


def pair(a):
    return jnp.concatenate(split(a), axis=1)


def fold(wide):
    return wide[:, 0:128] + wide[:, 128:256]


def by_cols(high, low):
    both = jnp.concatenate([high, low], axis=1)
    return jnp.concatenate([both, both], axis=0)


def greet(peers):
    barrier = pltpu.get_barrier_semaphore()
    for peer in peers:
        pl.semaphore_signal(barrier, inc=1, device_id=peer, device_id_type=MESH)
    pl.semaphore_wait(barrier, len(peers))


class Copies:
    def __init__(self, send_sem, recv_sem):
        self.send_sem, self.recv_sem, self.made = send_sem, recv_sem, []

    def send(self, src, dst, peer):
        i = len(self.made)
        copy = pltpu.make_async_remote_copy(
            src_ref=src,
            dst_ref=dst,
            send_sem=self.send_sem.at[i],
            recv_sem=self.recv_sem.at[i],
            device_id=peer,
            device_id_type=MESH,
        )
        copy.start()
        self.made.append(copy)
        return copy

    def finish(self):
        for copy in self.made:
            copy.wait_send()


def col_place():
    c = lax.axis_index("col")
    z, x = c // NX, c % NX
    along_x = [{"col": z * NX + (x + d) % NX} for d in range(1, NX)]
    along_z = [{"col": ((z + d) % NZ) * NX + x} for d in range(1, NZ)]
    return c, z, x, along_x, along_z


def gather_kernel(
    items, fetch, user, slot, er, ec, en, count, yh, yl, th, tl, gram, ent, peak,
    stage, land, fetch_in, slot_in, user_in, small, keys, most, seen, send_sem, recv_sem, own_sem, in_sem,
):
    c, z, x, along_x, along_z = col_place()
    r = lax.axis_index("row")
    y, core = r // 2, r % 2
    right, left, across = (((y + d) % NY) * 2 + core for d in (1, 3, 2))
    other = y * 2 + 1 - core
    to_right, to_left, to_other = {"row": right}, {"row": left}, {"row": other}
    loads = [
        pltpu.make_async_copy(src, dst, in_sem.at[i])
        for i, (src, dst) in enumerate(
            (
                (er, stage.at[pl.ds(0, TILES)]),
                (ec, stage.at[pl.ds(TILES, TILES)]),
                (en, stage.at[pl.ds(2 * TILES, TILES)]),
                (items, land.at[r]),
                (fetch, fetch_in),
                (slot, slot_in),
                (user, user_in),
            )
        )
    ]
    for load in loads:
        load.start()
    greet(along_x + along_z + [to_right, to_left, to_other])
    copies = Copies(send_sem, recv_sem)
    send = copies.send

    half = [items.at[pl.ds(4 * i, 4)] for i in (0, 1)]
    there = [land.at[r, pl.ds(4 * i, 4)] for i in (0, 1)]
    from_left, from_right = [None, None], [None, None]
    for i in (0, 1):
        from_left[i] = send(half[i], there[i], to_right)
        from_right[1 - i] = send(half[1 - i], there[1 - i], to_left)
    between = [send(items, land.at[r], to_other)]

    for load in loads[4:]:
        load.wait()
    small[...] = jnp.zeros_like(small)
    small[0:1, 0:TILES] = slot_in[...]
    small[1:2, 0:TILES] = user_in[...]
    slots = small[0:1]
    table = jnp.broadcast_to(fetch_in[...].astype(F32), (128, 128)).T
    ids = lax.broadcasted_iota(jnp.int32, (128, 128), 0)
    local_id = jnp.sum(jnp.where(ids == slots, table, 0.0), axis=0, keepdims=True).astype(jnp.int32)
    lanes = lax.broadcasted_iota(jnp.int32, (1, 128), 1)
    last = 3 * TILES
    stage[last : last + 1, 0:128] = jnp.where(lanes < count[0, 0], slots & (COLS - 1), -1)
    stage[last + 1 : last + 2, 0:128] = ((slots >> 4) * IB + local_id) * UB + small[1:2]
    for load in loads[:3]:
        load.wait()
    own = pltpu.make_async_copy(stage, ent.at[z, x], own_sem)
    own.start()

    first, second = pl.ds(0, HALF), pl.ds(HALF, STAGE - HALF)
    parts = (pl.ds(0, 32), pl.ds(32, 24)), (pl.ds(56, 24), pl.ds(80, 24))
    ways = (
        (first, along_x, along_z, lambda d, e: ent.at[(z + e) % NZ, (x + d) % NX]),
        (second, along_z, along_x, lambda d, e: ent.at[(z + d) % NZ, (x + e) % NX]),
    )
    near = [[None] * 4, [None] * 4]
    up = [[None] * 4, [None] * 4]
    down = [[None] * 4, [None] * 4]

    def spread(w, d, source):
        rows, _, across_way, at = ways[w]
        to = at(-d, 0).at[rows]
        up[w][d] = send(source, to, across_way[0])
        down[w][d] = send(source, to, across_way[2])

    for w, (rows, along, _, at) in enumerate(ways):
        for d in (1, 3, 2):
            near[w][d] = send(stage.at[rows], at(0, 0).at[rows], along[d - 1])
        spread(w, 0, stage.at[rows])

    far = []

    def pass_on(w, d):
        _, _, across_way, at = ways[w]
        up[w][d].wait_recv()
        piece = at(-d, -1).at[parts[w][0]]
        far.append(send(piece, piece, across_way[0]))
        down[w][d].wait_recv()
        piece = at(-d, 1).at[parts[w][1]]
        far.append(send(piece, piece, across_way[2]))

    def add(row, sums):
        def one(i, sums):
            high, low = split(land[row, i])
            high_t = high.T
            at = row * IB + i
            yh[at] = high
            yl[at] = low
            th[at] = high_t
            tl[at] = low.T
            return sums + dot(high_t, jnp.concatenate([high, low], axis=1), NN)

        return lax.fori_loop(0, IB, one, sums, unroll=4)

    loads[3].wait()
    sums = add(r, jnp.zeros((K, 2 * K), F32))
    for d in (1, 3, 2):
        for w in (0, 1):
            near[w][d].wait_recv()
            rows, _, _, at = ways[w]
            spread(w, d, at(-d, 0).at[rows])
    for w in (0, 1):
        pass_on(w, 0)
    from_left[0].wait_recv()
    piece = land.at[left, pl.ds(0, 4)]
    round_y = [send(piece, piece, to_right)]
    from_right[1].wait_recv()
    piece = land.at[right, pl.ds(4, 4)]
    round_y.append(send(piece, piece, to_left))
    between[0].wait_recv()
    sums = add(other, sums)
    for d in (1, 3):
        for w in (0, 1):
            pass_on(w, d)
    from_left[1].wait_recv()
    between.append(send(land.at[left], land.at[left], to_other))
    from_right[0].wait_recv()
    between.append(send(land.at[right], land.at[right], to_other))
    for w in (0, 1):
        pass_on(w, 2)
    sums = add(left, sums)
    sums = add(right, sums)
    for copy in far:
        copy.wait_recv()
    own.wait()
    load = pltpu.make_async_copy(ent.at[:, :, pl.ds(last, 8), pl.ds(0, 128)], keys, own_sem)
    load.start()
    load.wait()

    owners = keys[:, :, 0, :].reshape(COLS, 128)
    longest = jnp.zeros((1, 1), jnp.int32)
    for column in range(COLS):
        here = jnp.where(owners == column, 1, 0)
        here = jnp.sum(jnp.sum(here, axis=0, keepdims=True), axis=1, keepdims=True)
        longest = jnp.maximum(longest, here)
    most[0] = jnp.broadcast_to(longest, (8, 128))

    def tell(i):
        return [
            send(most.at[i], seen.at[i, n], peer)
            for n, peer in enumerate((to_right, to_left, to_other))
        ]

    def learn(i, told):
        for copy in told:
            copy.wait_recv()
        most[i + 1] = jnp.maximum(
            jnp.maximum(most[i], seen[i, 0]), jnp.maximum(seen[i, 1], seen[i, 2])
        )

    told = tell(0)
    for copy in round_y:
        copy.wait_recv()
    between.append(send(land.at[across], land.at[across], to_other))
    learn(0, told)
    told = tell(1)
    sums = add(across, sums)
    learn(1, told)
    told = tell(2)
    for copy, d in zip(between[1:], (3, 1, 2)):
        copy.wait_recv()
        sums = add(((y + d) % NY) * 2 + 1 - core, sums)
    learn(2, told)
    peak[...] = most[3]
    mixed = sums[:, K:]
    gram[...] = sums[:, :K] + (mixed + mixed.T)
    copies.finish()


def gather(items, fetch, user, slot, er, ec, en, count):
    n = 6 + 4 + 2 * (3 + 8 + 8) + 9
    return pl.pallas_call(
        gather_kernel,
        out_shape=(
            *[jax.ShapeDtypeStruct((ROWS * IB, BLOCK, K), BF16)] * 4,
            jax.ShapeDtypeStruct((K, K), F32),
            jax.ShapeDtypeStruct((NZ, NX, STAGE, NNZ), jnp.int32),
            jax.ShapeDtypeStruct((8, 128), jnp.int32),
        ),
        in_specs=[HBM] * 7 + [SMEM],
        out_specs=(VMEM, VMEM, VMEM, VMEM, VMEM, ANY, VMEM),
        scratch_shapes=[
            pltpu.VMEM((STAGE, NNZ), jnp.int32),
            pltpu.VMEM((ROWS, IB, BLOCK, K), F32),
            pltpu.VMEM((1, 128), jnp.int32),
            pltpu.VMEM((1, TILES), jnp.int32),
            pltpu.VMEM((1, TILES), jnp.int32),
            pltpu.VMEM((8, 128), jnp.int32),
            pltpu.VMEM((NZ, NX, 8, 128), jnp.int32),
            pltpu.VMEM((4, 8, 128), jnp.int32),
            pltpu.VMEM((3, 3, 8, 128), jnp.int32),
            pltpu.SemaphoreType.DMA((n,)),
            pltpu.SemaphoreType.DMA((n,)),
            pltpu.SemaphoreType.DMA,
            pltpu.SemaphoreType.DMA((7,)),
        ],
        compiler_params=pltpu.CompilerParams(
            collective_id=0, has_side_effects=True, vmem_limit_bytes=BIG
        ),
        name="gather",
    )(*[pltpu.with_memory_space_constraint(a, pltpu.HBM) for a in (items, fetch, user, slot, er, ec, en)], count)


def build_kernel(
    ent, yh, yl, th, tl, gram, start, out, weights, order, meta, found, place, held, v, sem, meta_sem
):
    fetched = pltpu.make_async_copy(
        ent.at[:, pl.ds(3 * TILES, 8), pl.ds(0, 128)], meta, meta_sem
    )
    fetched.start()
    g = by_cols(*split(gram[...]))

    def begin(b, _):
        at = rows_of(b)
        both = pair(start[at])
        v[at] = both
        out[at] = -fold(dot(both, g, NN))
        return 0

    lax.fori_loop(0, UB, begin, 0, unroll=UNROLL)
    fetched.wait()
    me = lax.axis_index("col")

    def scan(c, n):
        for t in range(TILES):
            found[n] = (c * TILES + t) * (64 * UB) + meta[c, 1, t]
            n = n + jnp.where(meta[c, 0, t] == me, 1, 0)
        return n

    n = lax.fori_loop(0, COLS, scan, 0)
    order[LIST - 1] = n

    for b in range(UB):
        place[b] = 0

    def count(j, _):
        b = found[j] & (UB - 1)
        place[b] = place[b] + 1
        return 0

    lax.fori_loop(0, n, count, 0)
    total = 0
    for b in range(UB):
        of_b = place[b]
        order[LAST + b] = jnp.where(of_b > 0, total + of_b - 1, -1)
        place[b] = total
        total = total + of_b

    def put(j, _):
        code = found[j]
        b = code & (UB - 1)
        to = place[b]
        order[to] = code
        place[b] = to + 1
        return 0

    lax.fori_loop(0, n, put, 0)
    ids = lax.broadcasted_iota(jnp.int32, (BLOCK, NNZ), 0).astype(F32).astype(BF16)
    one, none = jnp.ones((), BF16), jnp.zeros((), BF16)

    def out_copy(j):
        slot = j % SLOTS
        return pltpu.make_async_copy(held.at[slot], weights.at[j], sem.at[slot])

    def group(q, _):
        for u in range(BUILD):
            j = q * BUILD + u

            @pl.when((j >= SLOTS) & (j - SLOTS < n))
            def _(j=j):
                out_copy(j - SLOTS).wait()

        for u in range(BUILD):
            j = q * BUILD + u
            code = jnp.where(j < n, order[j], 0)
            b, block, at = code % UB, (code // UB) % 64, code // (64 * UB)
            c, t = at // TILES, at % TILES
            rows = jnp.where(j < n, ent[c, pl.ds(t, 1), :], BLOCK).astype(F32).astype(BF16)
            cols = ent[c, pl.ds(TILES + t, 1), :].astype(F32).astype(BF16)
            counts = ent[c, pl.ds(2 * TILES + t, 1), :].astype(F32).astype(BF16)
            row_hot = ids == rows
            col_hot = jnp.where(ids == cols, one, none)
            ones = jnp.where(row_hot, one, none)
            many = jnp.where(row_hot, counts, none)
            both = dot(jnp.concatenate([ones, many], axis=0), col_hot, NT)
            excess = SCALE * both[BLOCK:]
            held[j % SLOTS] = excess
            where = rows_of(b)
            scores = fold(dot(v[where], by_cols(th[block], tl[block]), NN))
            pull = both[:BLOCK] + excess * (1.0 - scores)
            out[where] += fold(dot(pair(pull), by_cols(yh[block], yl[block]), NN))
        for u in range(BUILD):
            j = q * BUILD + u

            @pl.when(j < n)
            def _(j=j):
                out_copy(j).start()

        return 0

    groups = (n + BUILD - 1) // BUILD
    lax.fori_loop(0, groups, group, 0)

    def drain(j, _):
        out_copy(j).wait()
        return 0

    lax.fori_loop(jnp.maximum(groups * BUILD - SLOTS, 0), n, drain, 0)


def build(ent, yh, yl, th, tl, gram, start):
    return pl.pallas_call(
        build_kernel,
        out_shape=(
            jax.ShapeDtypeStruct((UB * BLOCK, K), F32),
            jax.ShapeDtypeStruct((ALL_TILES, BLOCK, BLOCK), F32),
            jax.ShapeDtypeStruct((LIST,), jnp.int32),
        ),
        in_specs=[VMEM] * 7,
        out_specs=(VMEM, ANY, SMEM),
        scratch_shapes=[
            pltpu.SMEM((COLS, 8, 128), jnp.int32),
            pltpu.SMEM((LIST,), jnp.int32),
            pltpu.SMEM((UB,), jnp.int32),
            pltpu.VMEM((SLOTS, BLOCK, BLOCK), F32),
            pltpu.VMEM((UB * BLOCK, 2 * K), BF16),
            pltpu.SemaphoreType.DMA((SLOTS,)),
            pltpu.SemaphoreType.DMA,
        ],
        compiler_params=pltpu.CompilerParams(vmem_limit_bytes=BIG),
        name="build",
    )(ent, yh, yl, th, tl, gram, start)


def fetch_tiles(order, weights, held, sem, base):
    here = jnp.minimum(order[LIST - 1] - base, HELD)

    def begin(i, _):
        pltpu.make_async_copy(weights.at[base + i], held.at[i], sem.at[i]).start()
        return 0

    lax.fori_loop(0, here, begin, 0)
    return here


def each_tile(order, weights, held, sem, work):
    n = order[LIST - 1]

    def batch(k, _):
        base = k * HELD
        here = jnp.minimum(n - base, HELD)

        def group(q, _):
            for u in range(GROUP):
                i = q * GROUP + u

                @pl.when(i < here)
                def _(i=i):
                    pltpu.make_async_copy(weights.at[base + i], held.at[i], sem.at[i]).wait()

            for u in range(GROUP):
                i = q * GROUP + u
                live = i < here
                code = jnp.where(live, order[base + i], 0)
                w = jnp.where(live, held[i], 0.0)
                work(code % UB, (code // UB) % 64, w)
            return 0

        lax.fori_loop(0, (here + GROUP - 1) // GROUP, group, 0)

        @pl.when(n > base + HELD)
        def _():
            fetch_tiles(order, weights, held, sem, base + HELD)

        return 0

    lax.fori_loop(0, (n + HELD - 1) // HELD, batch, 0)


def rows_of(b):
    return pl.ds(pl.multiple_of(b * BLOCK, BLOCK), BLOCK)


def dots(a, b):
    return jnp.sum(a * b, axis=1, keepdims=True)


def pull_tiles(order, weights, held, sem, yh, yl, th, tl, v, out):
    def work(b, block, w):
        at = rows_of(b)
        scores = fold(dot(v[at], by_cols(th[block], tl[block]), NN))
        out[at] += fold(dot(pair(w * scores), by_cols(yh[block], yl[block]), NN))

    each_tile(order, weights, held, sem, work)


def first_kernel(order, total, start, yh, yl, th, tl, gram, weights, out, residual, v, held, sem):
    fetch_tiles(order, weights, held, sem, 0)
    g = by_cols(*split(gram[...]))

    def begin(b, _):
        at = rows_of(b)
        p = total[at] - RIDGE * start[at]
        residual[at] = p
        both = pair(p)
        v[at] = both
        out[at] = fold(dot(both, g, NN))
        return 0

    lax.fori_loop(0, UB, begin, 0, unroll=UNROLL)
    pull_tiles(order, weights, held, sem, yh, yl, th, tl, v, out)


def update(total, iterate, residual, direction):
    image = total + RIDGE * direction
    now = dots(residual, residual)
    alpha = now / (dots(direction, image) + EPSILON)
    iterate = iterate + alpha * direction
    residual = residual - alpha * image
    after = dots(residual, residual)
    direction = residual + after / (now + EPSILON) * direction
    return iterate, residual, direction


def second_kernel(
    order, total, iterate, residual, yh, yl, th, tl, gram, weights, out, new_x, new_r, new_p, v, held, sem
):
    fetch_tiles(order, weights, held, sem, 0)
    g = by_cols(*split(gram[...]))

    def begin(b, _):
        at = rows_of(b)
        r = residual[at]
        new_x[at], new_r[at], p = update(total[at], iterate[at], r, r)
        new_p[at] = p
        both = pair(p)
        v[at] = both
        out[at] = fold(dot(both, g, NN))
        return 0

    lax.fori_loop(0, UB, begin, 0, unroll=UNROLL)
    pull_tiles(order, weights, held, sem, yh, yl, th, tl, v, out)


def third_kernel(
    order, total, iterate, residual, direction, yh, yl, th, tl, gram, weights,
    squares, new_x, new_r, new_p, v, acc, held, sem,
):
    fetch_tiles(order, weights, held, sem, 0)
    g = by_cols(*split(gram[...]))

    def begin(b, _):
        at = rows_of(b)
        new_x[at], new_r[at], p = update(total[at], iterate[at], residual[at], direction[at])
        new_p[at] = p
        both = pair(p)
        v[at] = both
        acc[at] = p * fold(dot(both, g, NN))
        return 0

    lax.fori_loop(0, UB, begin, 0, unroll=UNROLL)

    def work(b, block, w):
        at = rows_of(b)
        scores = fold(dot(v[at], by_cols(th[block], tl[block]), NN))
        acc[at] += w * scores * scores

    each_tile(order, weights, held, sem, work)
    for b in range(UB):
        squares[b : b + 1] = jnp.sum(acc[b * BLOCK : (b + 1) * BLOCK].T, axis=0, keepdims=True)


def last_kernel(squares, iterate, residual, direction, out):
    sums = squares[...]
    for b in range(UB):
        at = pl.ds(b * BLOCK, BLOCK)
        p = direction[at]
        r = residual[at]
        below = jnp.broadcast_to(sums[b : b + 1], (BLOCK, BLOCK)).T + RIDGE * dots(p, p)
        out[at] = iterate[at] + dots(r, r) / (below + EPSILON) * p


USERS = jax.ShapeDtypeStruct((UB * BLOCK, K), F32)


def local(kernel, name, outs, specs, scratch=()):
    tiles = [
        pltpu.VMEM((UB * BLOCK, 2 * K), BF16),
        *scratch,
        pltpu.VMEM((HELD, BLOCK, BLOCK), F32),
        pltpu.SemaphoreType.DMA((HELD,)),
    ]
    return pl.pallas_call(
        kernel,
        out_shape=outs,
        in_specs=specs,
        out_specs=tuple(VMEM for _ in outs),
        scratch_shapes=tiles,
        compiler_params=pltpu.CompilerParams(vmem_limit_bytes=BIG),
        name=name,
    )


def reduce_kernel(part, out, land, sums, near, send_sem, recv_sem):
    c, z, x, along_x, along_z = col_place()
    greet(along_x + along_z)
    copies = Copies(send_sem, recv_sem)
    send = copies.send
    streams = [(pl.ds(SUB * i, SUB), i % 2 == 0) for i in range(BLOCK // SUB)]

    def line(ref, way, d, rows):
        return ref.at[:, (x + d) % NX, rows] if way else ref.at[(z + d) % NZ, :, rows]

    def axes(way):
        return (along_x, along_z, z) if way else (along_z, along_x, x)

    far = [
        [send(line(part, way, d, rows), land.at[i, d - 1], axes(way)[0][d - 1]) for d in (1, 2, 3)]
        for i, (rows, way) in enumerate(streams)
    ]
    close = []
    for i, (rows, way) in enumerate(streams):
        _, along, me = axes(way)
        for copy in far[i]:
            copy.wait_recv()
        mine = part[:, x, rows] if way else part[z, :, rows]
        sums[i] = mine + land[i, 0] + (land[i, 1] + land[i, 2])
        close.append(
            [send(sums.at[i, (me + d) % 4], near.at[i, d - 1], along[d - 1]) for d in (1, 2, 3)]
        )
    back = []
    for i, (rows, way) in enumerate(streams):
        _, along, me = axes(way)
        for copy in close[i]:
            copy.wait_recv()
        out[z, x, rows] = sums[i, me] + near[i, 0] + (near[i, 1] + near[i, 2])
        here = out.at[z, x, rows]
        back.append([send(here, here, peer) for peer in along])
    end = []
    for i, (rows, way) in enumerate(streams):
        for copy in back[i]:
            copy.wait_recv()
        here = line(out, way, 0, rows)
        end += [send(here, here, peer) for peer in axes(way)[0]]
    for copy in end:
        copy.wait_recv()
    copies.finish()


def reduce(part):
    n = BLOCK // SUB
    out = pl.pallas_call(
        reduce_kernel,
        out_shape=jax.ShapeDtypeStruct((NZ, NX, BLOCK, K), F32),
        in_specs=[VMEM],
        out_specs=VMEM,
        scratch_shapes=[
            pltpu.VMEM((n, 3, 4, SUB, K), F32),
            pltpu.VMEM((n, 4, SUB, K), F32),
            pltpu.VMEM((n, 3, SUB, K), F32),
            pltpu.SemaphoreType.DMA((12 * n,)),
            pltpu.SemaphoreType.DMA((12 * n,)),
        ],
        compiler_params=pltpu.CompilerParams(
            collective_id=1, has_side_effects=True, vmem_limit_bytes=BIG
        ),
        name="reduce",
    )(part.reshape(NZ, NX, BLOCK, K))
    return out.reshape(UB * BLOCK, K)


def scalars_kernel(mine, out, land_x, land_z, half, send_sem, recv_sem):
    _, _, _, along_x, along_z = col_place()
    greet(along_x + along_z)
    copies = Copies(send_sem, recv_sem)
    for copy in [copies.send(mine, land_x.at[i], peer) for i, peer in enumerate(along_x)]:
        copy.wait_recv()
    half[...] = mine[...] + land_x[0] + (land_x[1] + land_x[2])
    for copy in [copies.send(half, land_z.at[i], peer) for i, peer in enumerate(along_z)]:
        copy.wait_recv()
    out[...] = half[...] + land_z[0] + (land_z[1] + land_z[2])
    copies.finish()


def sum_scalars(mine):
    return pl.pallas_call(
        scalars_kernel,
        out_shape=jax.ShapeDtypeStruct((UB, BLOCK), F32),
        in_specs=[VMEM],
        out_specs=VMEM,
        scratch_shapes=[
            pltpu.VMEM((3, UB, BLOCK), F32),
            pltpu.VMEM((3, UB, BLOCK), F32),
            pltpu.VMEM((UB, BLOCK), F32),
            pltpu.SemaphoreType.DMA((6,)),
            pltpu.SemaphoreType.DMA((6,)),
        ],
        compiler_params=pltpu.CompilerParams(collective_id=2, has_side_effects=True, vmem_limit_bytes=BIG),
        name="scalars",
    )(mine)


def cg_kernel(
    order, part, start, yh, yl, th, tl, gram, weights, out,
    held, v, x_now, r_now, p_now, pulls, squares, parts, tot, land, sums, near,
    row_sums, land_x, land_z, half, send_sem, recv_sem, w_sem,
):
    _, z, x, along_x, along_z = col_place()
    load = pltpu.make_async_copy(weights.at[pl.ds(0, FAST)], held, w_sem)
    load.start()
    greet(along_x + along_z)
    copies = Copies(send_sem, recv_sem)
    send = copies.send
    far, close, back, end = {}, {}, {}, {}
    rounds = (part, parts.at[0], parts.at[1])

    def streams(s):
        for i in (2 * s, 2 * s + 1):
            way = i % 2 == 0
            first, second, me = (along_x, along_z, z) if way else (along_z, along_x, x)
            yield i, pl.ds(SUB * i, SUB), way, first, second, me

    def line(ref, way, d, rows):
        return ref.at[:, (x + d) % NX, rows] if way else ref.at[(z + d) % NZ, :, rows]

    def begin(k, s):
        for i, rows, way, first, _, _ in streams(s):
            far[k, i] = [
                send(line(rounds[k], way, d, rows), land.at[k, i, d - 1], first[d - 1])
                for d in (1, 2, 3)
            ]

    def sum_first(k, s):
        for i, rows, way, _, second, me in streams(s):
            for copy in far[k, i]:
                copy.wait_recv()
            mine = rounds[k][:, x, rows] if way else rounds[k][z, :, rows]
            sums[k, i] = mine + land[k, i, 0] + (land[k, i, 1] + land[k, i, 2])
            close[k, i] = [
                send(sums.at[k, i, (me + d) % 4], near.at[k, i, d - 1], second[d - 1])
                for d in (1, 2, 3)
            ]

    def sum_second(k, s):
        for i, rows, _, _, second, me in streams(s):
            for copy in close[k, i]:
                copy.wait_recv()
            tot[k, z, x, rows] = sums[k, i, me] + near[k, i, 0] + (near[k, i, 1] + near[k, i, 2])
            here = tot.at[k, z, x, rows]
            back[k, i] = [send(here, here, peer) for peer in second]

    def spread(k, s):
        for i, rows, way, first, _, _ in streams(s):
            for copy in back[k, i]:
                copy.wait_recv()
            here = line(tot.at[k], way, 0, rows)
            end[k, i] = [send(here, here, peer) for peer in first]

    def arrive(k, s):
        for i in (2 * s, 2 * s + 1):
            for copy in end[k, i]:
                copy.wait_recv()

    g = by_cols(*split(gram[...]))
    n = order[LIST - 1]

    def compute(k, s, between):
        rows = pl.ds(64 * s, 64)
        between[0]()

        def step(b, _):
            total = tot[k - 1, b // NX, b % NX, rows]
            if k == 1:
                p = total - RIDGE * start[b, rows]
                r_now[b, rows] = p
            else:
                before = start[b, rows] if k == 2 else x_now[b, rows]
                r = r_now[b, rows]
                old = r if k == 2 else p_now[b, rows]
                x_now[b, rows], r_now[b, rows], p = update(total, before, r, old)
            p_now[b, rows] = p
            v[b, rows] = pair(p)
            return 0

        lax.fori_loop(0, UB, step, 0, unroll=4)

        def quarter(i, acc):
            def some(q, acc):
                last_b, acc = acc
                for u in range(STEP):
                    j = i * QUARTER + q * STEP + u
                    code = order[j]
                    b, block = code & (UB - 1), (code >> 4) & 63
                    w = jnp.where(j < n, held[j, rows], 0.0)
                    scores = fold(dot(v[b, rows], by_cols(th[block], tl[block]), NN))
                    if k < 3:
                        pull = fold(dot(pair(w * scores), by_cols(yh[block], yl[block]), NN))
                    else:
                        pull = w * scores * scores
                    acc = jnp.where(b == last_b, acc, 0.0) + pull
                    last_b = b
                    pulls[s, j] = acc
                return last_b, acc

            return lax.fori_loop(0, QUARTER // STEP, some, acc)

        acc = jnp.int32(-1), jnp.zeros((64, K), F32)
        acc = quarter(0, acc)
        between[1]()
        acc = quarter(1, acc)
        acc = quarter(2, acc)
        between[2]()
        acc = quarter(3, acc)

        def close_up(b, _):
            end_of = order[LAST + b]
            pulled = jnp.where(end_of >= 0, pulls[s, jnp.maximum(end_of, 0)], 0.0)
            whole = fold(dot(v[b, rows], g, NN))
            if k < 3:
                parts[k - 1, b // NX, b % NX, rows] = whole + pulled
            else:
                squares[b, rows] = p_now[b, rows] * whole + pulled
            return 0

        lax.fori_loop(0, UB, close_up, 0, unroll=4)

    def nothing():
        pass

    def handlers(k, s):
        return [functools.partial(f, k, s) for f in (sum_first, sum_second, spread)]

    begin(0, 0)
    begin(0, 1)
    for work in (sum_first, sum_second, spread):
        work(0, 0)
        work(0, 1)
    load.wait()
    arrive(0, 0)
    compute(1, 0, [nothing] * 3)
    begin(1, 0)
    arrive(0, 1)
    compute(1, 1, handlers(1, 0))
    begin(1, 1)
    arrive(1, 0)
    compute(2, 0, handlers(1, 1))
    begin(2, 0)
    arrive(1, 1)
    compute(2, 1, handlers(2, 0))
    begin(2, 1)
    arrive(2, 0)
    compute(3, 0, handlers(2, 1))
    arrive(2, 1)
    compute(3, 1, [nothing] * 3)

    for b in range(UB):
        row_sums[b : b + 1] = jnp.sum(squares[b].T, axis=0, keepdims=True)
    for copy in [send(row_sums, land_x.at[i], peer) for i, peer in enumerate(along_x)]:
        copy.wait_recv()
    half[...] = row_sums[...] + land_x[0] + (land_x[1] + land_x[2])
    for copy in [send(half, land_z.at[i], peer) for i, peer in enumerate(along_z)]:
        copy.wait_recv()
    both = half[...] + land_z[0] + (land_z[1] + land_z[2])
    for b in range(UB):
        p, r = p_now[b], r_now[b]
        below = jnp.broadcast_to(both[b : b + 1], (BLOCK, BLOCK)).T + RIDGE * dots(p, p)
        out[b] = x_now[b] + dots(r, r) / (below + EPSILON) * p
    copies.finish()


def all_steps(order, part, start, yh, yl, th, tl, gram, weights):
    n = BLOCK // SUB
    copies = 3 * 12 * n + 6
    blocks = (UB, BLOCK, K)
    out = pl.pallas_call(
        cg_kernel,
        out_shape=jax.ShapeDtypeStruct(blocks, F32),
        in_specs=[SMEM] + [VMEM] * 7 + [ANY],
        out_specs=VMEM,
        scratch_shapes=[
            pltpu.VMEM((FAST, BLOCK, BLOCK), F32),
            pltpu.VMEM((UB, BLOCK, 2 * K), BF16),
            pltpu.VMEM(blocks, F32),
            pltpu.VMEM(blocks, F32),
            pltpu.VMEM(blocks, F32),
            pltpu.VMEM((2, FAST, 64, K), F32),
            pltpu.VMEM(blocks, F32),
            pltpu.VMEM((2, NZ, NX, BLOCK, K), F32),
            pltpu.VMEM((3, NZ, NX, BLOCK, K), F32),
            pltpu.VMEM((3, n, 3, 4, SUB, K), F32),
            pltpu.VMEM((3, n, 4, SUB, K), F32),
            pltpu.VMEM((3, n, 3, SUB, K), F32),
            pltpu.VMEM((UB, BLOCK), F32),
            pltpu.VMEM((3, UB, BLOCK), F32),
            pltpu.VMEM((3, UB, BLOCK), F32),
            pltpu.VMEM((UB, BLOCK), F32),
            pltpu.SemaphoreType.DMA((copies,)),
            pltpu.SemaphoreType.DMA((copies,)),
            pltpu.SemaphoreType.DMA,
        ],
        compiler_params=pltpu.CompilerParams(
            collective_id=3, has_side_effects=True, vmem_limit_bytes=WHOLE
        ),
        name="steps",
    )(order, part.reshape(NZ, NX, BLOCK, K), start.reshape(blocks), yh, yl, th, tl, gram, weights)
    return out.reshape(UB * BLOCK, K)


def step_by_step(order, part, start, yh, yl, th, tl, gram, weights):
    total = reduce(part)
    tail = [VMEM] * 5 + [ANY]
    part, residual = local(first_kernel, "first", (USERS,) * 2, [SMEM, VMEM, VMEM] + tail)(
        order, total, start, yh, yl, th, tl, gram, weights
    )
    total = reduce(part)
    part, iterate, residual, direction = local(
        second_kernel, "second", (USERS,) * 4, [SMEM] + [VMEM] * 3 + tail
    )(order, total, start, residual, yh, yl, th, tl, gram, weights)
    total = reduce(part)
    squares = jax.ShapeDtypeStruct((UB, BLOCK), F32)
    part, iterate, residual, direction = local(
        third_kernel,
        "third",
        (squares,) + (USERS,) * 3,
        [SMEM] + [VMEM] * 4 + tail,
        [pltpu.VMEM((UB * BLOCK, K), F32)],
    )(order, total, iterate, residual, direction, yh, yl, th, tl, gram, weights)
    squares = sum_scalars(part)
    return pl.pallas_call(
        last_kernel,
        out_shape=USERS,
        in_specs=[VMEM] * 4,
        out_specs=VMEM,
        compiler_params=pltpu.CompilerParams(vmem_limit_bytes=BIG),
        name="last",
    )(squares, iterate, residual, direction)


def shards(user_factors, item_factors, fetch_list, tile_user, tile_slot, er, ec, en, tile_count):
    yh, yl, th, tl, gram, ent, peak = gather(
        item_factors.reshape(IB, BLOCK, K),
        fetch_list.reshape(1, 128),
        tile_user.reshape(1, TILES),
        tile_slot.reshape(1, TILES),
        er.reshape(TILES, NNZ),
        ec.reshape(TILES, NNZ),
        en.reshape(TILES, NNZ),
        tile_count.reshape(1, 1),
    )
    part, weights, order = build(
        ent.reshape(COLS, STAGE, NNZ), yh, yl, th, tl, gram, user_factors
    )
    return lax.cond(
        peak[0, 0] <= FAST,
        all_steps,
        step_by_step,
        order, part, user_factors, yh, yl, th, tl, gram, weights,
    )


def solution(mesh):
    return jax.shard_map(
        shards,
        mesh=mesh,
        in_specs=(
            P("row", None),
            P(("row", "col"), None),
            P("row", "col", None, None),
            P("row", "col", None),
            P("row", "col", None),
            P("row", "col", None, None),
            P("row", "col", None, None),
            P("row", "col", None, None),
            P("row", "col"),
        ),
        out_specs=P("row", None),
        check_vma=False,
    )
```

```python
import functools

import jax
import jax.numpy as jnp
from jax import lax
from jax.experimental import pallas as pl
from jax.experimental.pallas import tpu as pltpu
from jax.sharding import PartitionSpec as P

K = 128
BLOCK = 128
UB = 16
IB = 8
TILES = 32
NNZ = 512
NZ = NX = 4
NY = 4
ROWS = 8
COLS = 16
ALL_TILES = COLS * TILES
LIST = 1024
LAST = 512
FAST = 40
STEP = 20
SUB = 32
UNROLL = 4
BUILD = 4
SLOTS = 2 * BUILD
GROUP = 4
HELD = 32
STAGE = 3 * TILES + 8
HALF = 56
SCALE = 40.0
RIDGE = 0.5
EPSILON = 1e-06
MESH = pl.DeviceIdType.MESH
F32 = jnp.float32
BF16 = jnp.bfloat16
NT = (((1,), (1,)), ((), ()))
NN = (((1,), (0,)), ((), ()))
ANY = pl.BlockSpec(memory_space=pl.ANY)
VMEM = pl.BlockSpec(memory_space=pltpu.VMEM)
SMEM = pl.BlockSpec(memory_space=pltpu.SMEM)
HBM = pl.BlockSpec(memory_space=pltpu.HBM)
BIG = 24 * 2**20
WHOLE = 40 * 2**20


def dot(a, b, dims):
    return lax.dot_general(a, b, dims, preferred_element_type=F32)


def split(a):
    high = a.astype(BF16)
    return high, (a - high.astype(F32)).astype(BF16)


def pair(a):
    return jnp.concatenate(split(a), axis=1)


def fold(wide):
    return wide[:, 0:128] + wide[:, 128:256]


def by_cols(high, low):
    both = jnp.concatenate([high, low], axis=1)
    return jnp.concatenate([both, both], axis=0)


def greet(peers):
    barrier = pltpu.get_barrier_semaphore()
    for peer in peers:
        pl.semaphore_signal(barrier, inc=1, device_id=peer, device_id_type=MESH)
    pl.semaphore_wait(barrier, len(peers))


class Copies:
    def __init__(self, send_sem, recv_sem):
        self.send_sem, self.recv_sem, self.made = send_sem, recv_sem, []

    def send(self, src, dst, peer):
        i = len(self.made)
        copy = pltpu.make_async_remote_copy(
            src_ref=src,
            dst_ref=dst,
            send_sem=self.send_sem.at[i],
            recv_sem=self.recv_sem.at[i],
            device_id=peer,
            device_id_type=MESH,
        )
        copy.start()
        self.made.append(copy)
        return copy

    def finish(self):
        for copy in self.made:
            copy.wait_send()


def col_place():
    c = lax.axis_index("col")
    z, x = c // NX, c % NX
    along_x = [{"col": z * NX + (x + d) % NX} for d in range(1, NX)]
    along_z = [{"col": ((z + d) % NZ) * NX + x} for d in range(1, NZ)]
    return c, z, x, along_x, along_z


def gather_kernel(
    items, fetch, user, slot, er, ec, en, count, yh, yl, th, tl, gram, ent, peak,
    stage, land, fetch_in, slot_in, user_in, small, keys, most, seen, send_sem, recv_sem, own_sem, in_sem,
):
    c, z, x, along_x, along_z = col_place()
    r = lax.axis_index("row")
    y, core = r // 2, r % 2
    right, left, across = (((y + d) % NY) * 2 + core for d in (1, 3, 2))
    other = y * 2 + 1 - core
    to_right, to_left, to_other = {"row": right}, {"row": left}, {"row": other}
    loads = [
        pltpu.make_async_copy(src, dst, in_sem.at[i])
        for i, (src, dst) in enumerate(
            (
                (er, stage.at[pl.ds(0, TILES)]),
                (ec, stage.at[pl.ds(TILES, TILES)]),
                (en, stage.at[pl.ds(2 * TILES, TILES)]),
                (items, land.at[r]),
                (fetch, fetch_in),
                (slot, slot_in),
                (user, user_in),
            )
        )
    ]
    for load in loads:
        load.start()
    for load in loads[4:]:
        load.wait()
    small[...] = jnp.zeros_like(small)
    small[0:1, 0:TILES] = slot_in[...]
    small[1:2, 0:TILES] = user_in[...]
    slots = small[0:1]
    table = jnp.broadcast_to(fetch_in[...].astype(F32), (128, 128)).T
    ids = lax.broadcasted_iota(jnp.int32, (128, 128), 0)
    local_id = jnp.sum(jnp.where(ids == slots, table, 0.0), axis=0, keepdims=True).astype(jnp.int32)
    lanes = lax.broadcasted_iota(jnp.int32, (1, 128), 1)
    last = 3 * TILES
    stage[last : last + 1, 0:128] = jnp.where(lanes < count[0, 0], slots & (COLS - 1), -1)
    stage[last + 1 : last + 2, 0:128] = ((slots >> 4) * IB + local_id) * UB + small[1:2]
    first_key = stage[last : last + 1, 0:128]
    keys[z, x] = jnp.broadcast_to(first_key, (8, 128))
    greet(along_x + along_z + [to_right, to_left, to_other])
    copies = Copies(send_sem, recv_sem)
    send = copies.send
    mine = keys.at[z, x]
    told_keys = [send(mine, mine, peer) for peer in along_x]

    half = [items.at[pl.ds(4 * i, 4)] for i in (0, 1)]
    there = [land.at[r, pl.ds(4 * i, 4)] for i in (0, 1)]
    from_left, from_right = [None, None], [None, None]
    for i in (0, 1):
        from_left[i] = send(half[i], there[i], to_right)
        from_right[1 - i] = send(half[1 - i], there[1 - i], to_left)
    between = [send(items, land.at[r], to_other)]

    for load in loads[:3]:
        load.wait()
    own = pltpu.make_async_copy(stage, ent.at[z, x], own_sem)
    own.start()

    first, second = pl.ds(0, HALF), pl.ds(HALF, STAGE - HALF)
    parts = (pl.ds(0, 32), pl.ds(32, 24)), (pl.ds(56, 24), pl.ds(80, 24))
    ways = (
        (first, along_x, along_z, lambda d, e: ent.at[(z + e) % NZ, (x + d) % NX]),
        (second, along_z, along_x, lambda d, e: ent.at[(z + d) % NZ, (x + e) % NX]),
    )
    near = [[None] * 4, [None] * 4]
    up = [[None] * 4, [None] * 4]
    down = [[None] * 4, [None] * 4]

    def spread(w, d, source):
        rows, _, across_way, at = ways[w]
        to = at(-d, 0).at[rows]
        up[w][d] = send(source, to, across_way[0])
        down[w][d] = send(source, to, across_way[2])

    for w, (rows, along, _, at) in enumerate(ways):
        for d in (1, 3, 2):
            near[w][d] = send(stage.at[rows], at(0, 0).at[rows], along[d - 1])
        spread(w, 0, stage.at[rows])

    far = []

    def pass_on(w, d):
        _, _, across_way, at = ways[w]
        up[w][d].wait_recv()
        piece = at(-d, -1).at[parts[w][0]]
        far.append(send(piece, piece, across_way[0]))
        down[w][d].wait_recv()
        piece = at(-d, 1).at[parts[w][1]]
        far.append(send(piece, piece, across_way[2]))

    def add(row, sums):
        def one(i, sums):
            high, low = split(land[row, i])
            high_t = high.T
            at = row * IB + i
            yh[at] = high
            yl[at] = low
            th[at] = high_t
            tl[at] = low.T
            return sums + dot(high_t, jnp.concatenate([high, low], axis=1), NN)

        return lax.fori_loop(0, IB, one, sums, unroll=4)

    loads[3].wait()
    sums = add(r, jnp.zeros((K, 2 * K), F32))
    for copy in told_keys:
        copy.wait_recv()
    mine = keys.at[z]
    told_keys = [send(mine, mine, peer) for peer in along_z]

    def tell(i):
        return [
            send(most.at[i], seen.at[i, n], peer)
            for n, peer in enumerate((to_right, to_left, to_other))
        ]

    def learn(i, told):
        for copy in told:
            copy.wait_recv()
        most[i + 1] = jnp.maximum(
            jnp.maximum(most[i], seen[i, 0]), jnp.maximum(seen[i, 1], seen[i, 2])
        )

    for d in (1, 3, 2):
        for w in (0, 1):
            near[w][d].wait_recv()
            rows, _, _, at = ways[w]
            spread(w, d, at(-d, 0).at[rows])
    for w in (0, 1):
        pass_on(w, 0)
    from_left[0].wait_recv()
    piece = land.at[left, pl.ds(0, 4)]
    round_y = [send(piece, piece, to_right)]
    from_right[1].wait_recv()
    piece = land.at[right, pl.ds(4, 4)]
    round_y.append(send(piece, piece, to_left))
    for copy in told_keys:
        copy.wait_recv()
    owners = keys[:, :, 0, :].reshape(COLS, 128)
    longest = jnp.zeros((1, 1), jnp.int32)
    for column in range(COLS):
        here = jnp.where(owners == column, 1, 0)
        here = jnp.sum(jnp.sum(here, axis=0, keepdims=True), axis=1, keepdims=True)
        longest = jnp.maximum(longest, here)
    most[0] = jnp.broadcast_to(longest, (8, 128))

    told = tell(0)
    between[0].wait_recv()
    sums = add(other, sums)
    for d in (1, 3):
        for w in (0, 1):
            pass_on(w, d)
    from_left[1].wait_recv()
    between.append(send(land.at[left], land.at[left], to_other))
    from_right[0].wait_recv()
    between.append(send(land.at[right], land.at[right], to_other))
    for w in (0, 1):
        pass_on(w, 2)
    learn(0, told)
    told = tell(1)
    sums = add(left, sums)
    sums = add(right, sums)
    learn(1, told)
    told = tell(2)
    for copy in round_y:
        copy.wait_recv()
    between.append(send(land.at[across], land.at[across], to_other))
    sums = add(across, sums)
    for copy, d in zip(between[1:], (3, 1, 2)):
        copy.wait_recv()
        sums = add(((y + d) % NY) * 2 + 1 - core, sums)
    learn(2, told)
    peak[...] = most[3]
    for copy in far:
        copy.wait_recv()
    own.wait()
    mixed = sums[:, K:]
    gram[...] = sums[:, :K] + (mixed + mixed.T)
    copies.finish()


def gather(items, fetch, user, slot, er, ec, en, count):
    n = 6 + 4 + 2 * (3 + 8 + 8) + 9 + 6
    return pl.pallas_call(
        gather_kernel,
        out_shape=(
            *[jax.ShapeDtypeStruct((ROWS * IB, BLOCK, K), BF16)] * 4,
            jax.ShapeDtypeStruct((K, K), F32),
            jax.ShapeDtypeStruct((NZ, NX, STAGE, NNZ), jnp.int32),
            jax.ShapeDtypeStruct((8, 128), jnp.int32),
        ),
        in_specs=[HBM] * 7 + [SMEM],
        out_specs=(VMEM, VMEM, VMEM, VMEM, VMEM, ANY, VMEM),
        scratch_shapes=[
            pltpu.VMEM((STAGE, NNZ), jnp.int32),
            pltpu.VMEM((ROWS, IB, BLOCK, K), F32),
            pltpu.VMEM((1, 128), jnp.int32),
            pltpu.VMEM((1, TILES), jnp.int32),
            pltpu.VMEM((1, TILES), jnp.int32),
            pltpu.VMEM((8, 128), jnp.int32),
            pltpu.VMEM((NZ, NX, 8, 128), jnp.int32),
            pltpu.VMEM((4, 8, 128), jnp.int32),
            pltpu.VMEM((3, 3, 8, 128), jnp.int32),
            pltpu.SemaphoreType.DMA((n,)),
            pltpu.SemaphoreType.DMA((n,)),
            pltpu.SemaphoreType.DMA,
            pltpu.SemaphoreType.DMA((7,)),
        ],
        compiler_params=pltpu.CompilerParams(
            collective_id=0, has_side_effects=True, vmem_limit_bytes=BIG
        ),
        name="gather",
    )(*[pltpu.with_memory_space_constraint(a, pltpu.HBM) for a in (items, fetch, user, slot, er, ec, en)], count)


def build_kernel(
    ent, yh, yl, th, tl, gram, start, out, weights, order, meta, found, place, held, v, sem, meta_sem
):
    fetched = pltpu.make_async_copy(
        ent.at[:, pl.ds(3 * TILES, 8), pl.ds(0, 128)], meta, meta_sem
    )
    fetched.start()
    g = by_cols(*split(gram[...]))

    def begin(b, _):
        at = rows_of(b)
        both = pair(start[at])
        v[at] = both
        out[at] = -fold(dot(both, g, NN))
        return 0

    lax.fori_loop(0, UB, begin, 0, unroll=UNROLL)
    fetched.wait()
    me = lax.axis_index("col")

    def scan(c, n):
        for t in range(TILES):
            found[n] = (c * TILES + t) * (64 * UB) + meta[c, 1, t]
            n = n + jnp.where(meta[c, 0, t] == me, 1, 0)
        return n

    n = lax.fori_loop(0, COLS, scan, 0)
    order[LIST - 1] = n

    for b in range(UB):
        place[b] = 0

    def count(j, _):
        b = found[j] & (UB - 1)
        place[b] = place[b] + 1
        return 0

    lax.fori_loop(0, n, count, 0)
    total = 0
    for b in range(UB):
        of_b = place[b]
        order[LAST + b] = jnp.where(of_b > 0, total + of_b - 1, -1)
        place[b] = total
        total = total + of_b

    def put(j, _):
        code = found[j]
        b = code & (UB - 1)
        to = place[b]
        order[to] = code
        place[b] = to + 1
        return 0

    lax.fori_loop(0, n, put, 0)
    ids = lax.broadcasted_iota(jnp.int32, (BLOCK, NNZ), 0).astype(F32).astype(BF16)
    one, none = jnp.ones((), BF16), jnp.zeros((), BF16)

    def out_copy(j):
        slot = j % SLOTS
        return pltpu.make_async_copy(held.at[slot], weights.at[j], sem.at[slot])

    def group(q, _):
        for u in range(BUILD):
            j = q * BUILD + u

            @pl.when((j >= SLOTS) & (j - SLOTS < n))
            def _(j=j):
                out_copy(j - SLOTS).wait()

        for u in range(BUILD):
            j = q * BUILD + u
            code = jnp.where(j < n, order[j], 0)
            b, block, at = code % UB, (code // UB) % 64, code // (64 * UB)
            c, t = at // TILES, at % TILES
            rows = jnp.where(j < n, ent[c, pl.ds(t, 1), :], BLOCK).astype(F32).astype(BF16)
            cols = ent[c, pl.ds(TILES + t, 1), :].astype(F32).astype(BF16)
            counts = ent[c, pl.ds(2 * TILES + t, 1), :].astype(F32).astype(BF16)
            row_hot = ids == rows
            col_hot = jnp.where(ids == cols, one, none)
            ones = jnp.where(row_hot, one, none)
            many = jnp.where(row_hot, counts, none)
            both = dot(jnp.concatenate([ones, many], axis=0), col_hot, NT)
            excess = SCALE * both[BLOCK:]
            held[j % SLOTS] = excess
            where = rows_of(b)
            scores = fold(dot(v[where], by_cols(th[block], tl[block]), NN))
            pull = both[:BLOCK] + excess * (1.0 - scores)
            out[where] += fold(dot(pair(pull), by_cols(yh[block], yl[block]), NN))
        for u in range(BUILD):
            j = q * BUILD + u

            @pl.when(j < n)
            def _(j=j):
                out_copy(j).start()

        return 0

    groups = (n + BUILD - 1) // BUILD
    lax.fori_loop(0, groups, group, 0)

    def drain(j, _):
        out_copy(j).wait()
        return 0

    lax.fori_loop(jnp.maximum(groups * BUILD - SLOTS, 0), n, drain, 0)


def build(ent, yh, yl, th, tl, gram, start):
    return pl.pallas_call(
        build_kernel,
        out_shape=(
            jax.ShapeDtypeStruct((UB * BLOCK, K), F32),
            jax.ShapeDtypeStruct((ALL_TILES, BLOCK, BLOCK), F32),
            jax.ShapeDtypeStruct((LIST,), jnp.int32),
        ),
        in_specs=[VMEM] * 7,
        out_specs=(VMEM, ANY, SMEM),
        scratch_shapes=[
            pltpu.SMEM((COLS, 8, 128), jnp.int32),
            pltpu.SMEM((LIST,), jnp.int32),
            pltpu.SMEM((UB,), jnp.int32),
            pltpu.VMEM((SLOTS, BLOCK, BLOCK), F32),
            pltpu.VMEM((UB * BLOCK, 2 * K), BF16),
            pltpu.SemaphoreType.DMA((SLOTS,)),
            pltpu.SemaphoreType.DMA,
        ],
        compiler_params=pltpu.CompilerParams(vmem_limit_bytes=BIG),
        name="build",
    )(ent, yh, yl, th, tl, gram, start)


def fetch_tiles(order, weights, held, sem, base):
    here = jnp.minimum(order[LIST - 1] - base, HELD)

    def begin(i, _):
        pltpu.make_async_copy(weights.at[base + i], held.at[i], sem.at[i]).start()
        return 0

    lax.fori_loop(0, here, begin, 0)
    return here


def each_tile(order, weights, held, sem, work):
    n = order[LIST - 1]

    def batch(k, _):
        base = k * HELD
        here = jnp.minimum(n - base, HELD)

        def group(q, _):
            for u in range(GROUP):
                i = q * GROUP + u

                @pl.when(i < here)
                def _(i=i):
                    pltpu.make_async_copy(weights.at[base + i], held.at[i], sem.at[i]).wait()

            for u in range(GROUP):
                i = q * GROUP + u
                live = i < here
                code = jnp.where(live, order[base + i], 0)
                w = jnp.where(live, held[i], 0.0)
                work(code % UB, (code // UB) % 64, w)
            return 0

        lax.fori_loop(0, (here + GROUP - 1) // GROUP, group, 0)

        @pl.when(n > base + HELD)
        def _():
            fetch_tiles(order, weights, held, sem, base + HELD)

        return 0

    lax.fori_loop(0, (n + HELD - 1) // HELD, batch, 0)


def rows_of(b):
    return pl.ds(pl.multiple_of(b * BLOCK, BLOCK), BLOCK)


def dots(a, b):
    return jnp.sum(a * b, axis=1, keepdims=True)


def pull_tiles(order, weights, held, sem, yh, yl, th, tl, v, out):
    def work(b, block, w):
        at = rows_of(b)
        scores = fold(dot(v[at], by_cols(th[block], tl[block]), NN))
        out[at] += fold(dot(pair(w * scores), by_cols(yh[block], yl[block]), NN))

    each_tile(order, weights, held, sem, work)


def first_kernel(order, total, start, yh, yl, th, tl, gram, weights, out, residual, v, held, sem):
    fetch_tiles(order, weights, held, sem, 0)
    g = by_cols(*split(gram[...]))

    def begin(b, _):
        at = rows_of(b)
        p = total[at] - RIDGE * start[at]
        residual[at] = p
        both = pair(p)
        v[at] = both
        out[at] = fold(dot(both, g, NN))
        return 0

    lax.fori_loop(0, UB, begin, 0, unroll=UNROLL)
    pull_tiles(order, weights, held, sem, yh, yl, th, tl, v, out)


def update(total, iterate, residual, direction):
    image = total + RIDGE * direction
    now = dots(residual, residual)
    alpha = now / (dots(direction, image) + EPSILON)
    iterate = iterate + alpha * direction
    residual = residual - alpha * image
    after = dots(residual, residual)
    direction = residual + after / (now + EPSILON) * direction
    return iterate, residual, direction


def second_kernel(
    order, total, iterate, residual, yh, yl, th, tl, gram, weights, out, new_x, new_r, new_p, v, held, sem
):
    fetch_tiles(order, weights, held, sem, 0)
    g = by_cols(*split(gram[...]))

    def begin(b, _):
        at = rows_of(b)
        r = residual[at]
        new_x[at], new_r[at], p = update(total[at], iterate[at], r, r)
        new_p[at] = p
        both = pair(p)
        v[at] = both
        out[at] = fold(dot(both, g, NN))
        return 0

    lax.fori_loop(0, UB, begin, 0, unroll=UNROLL)
    pull_tiles(order, weights, held, sem, yh, yl, th, tl, v, out)


def third_kernel(
    order, total, iterate, residual, direction, yh, yl, th, tl, gram, weights,
    squares, new_x, new_r, new_p, v, acc, held, sem,
):
    fetch_tiles(order, weights, held, sem, 0)
    g = by_cols(*split(gram[...]))

    def begin(b, _):
        at = rows_of(b)
        new_x[at], new_r[at], p = update(total[at], iterate[at], residual[at], direction[at])
        new_p[at] = p
        both = pair(p)
        v[at] = both
        acc[at] = p * fold(dot(both, g, NN))
        return 0

    lax.fori_loop(0, UB, begin, 0, unroll=UNROLL)

    def work(b, block, w):
        at = rows_of(b)
        scores = fold(dot(v[at], by_cols(th[block], tl[block]), NN))
        acc[at] += w * scores * scores

    each_tile(order, weights, held, sem, work)
    for b in range(UB):
        squares[b : b + 1] = jnp.sum(acc[b * BLOCK : (b + 1) * BLOCK].T, axis=0, keepdims=True)


def last_kernel(squares, iterate, residual, direction, out):
    sums = squares[...]
    for b in range(UB):
        at = pl.ds(b * BLOCK, BLOCK)
        p = direction[at]
        r = residual[at]
        below = jnp.broadcast_to(sums[b : b + 1], (BLOCK, BLOCK)).T + RIDGE * dots(p, p)
        out[at] = iterate[at] + dots(r, r) / (below + EPSILON) * p


USERS = jax.ShapeDtypeStruct((UB * BLOCK, K), F32)


def local(kernel, name, outs, specs, scratch=()):
    tiles = [
        pltpu.VMEM((UB * BLOCK, 2 * K), BF16),
        *scratch,
        pltpu.VMEM((HELD, BLOCK, BLOCK), F32),
        pltpu.SemaphoreType.DMA((HELD,)),
    ]
    return pl.pallas_call(
        kernel,
        out_shape=outs,
        in_specs=specs,
        out_specs=tuple(VMEM for _ in outs),
        scratch_shapes=tiles,
        compiler_params=pltpu.CompilerParams(vmem_limit_bytes=BIG),
        name=name,
    )


def reduce_kernel(part, out, land, sums, near, send_sem, recv_sem):
    c, z, x, along_x, along_z = col_place()
    greet(along_x + along_z)
    copies = Copies(send_sem, recv_sem)
    send = copies.send
    streams = [(pl.ds(SUB * i, SUB), i % 2 == 0) for i in range(BLOCK // SUB)]

    def line(ref, way, d, rows):
        return ref.at[:, (x + d) % NX, rows] if way else ref.at[(z + d) % NZ, :, rows]

    def axes(way):
        return (along_x, along_z, z) if way else (along_z, along_x, x)

    far = [
        [send(line(part, way, d, rows), land.at[i, d - 1], axes(way)[0][d - 1]) for d in (1, 2, 3)]
        for i, (rows, way) in enumerate(streams)
    ]
    close = []
    for i, (rows, way) in enumerate(streams):
        _, along, me = axes(way)
        for copy in far[i]:
            copy.wait_recv()
        mine = part[:, x, rows] if way else part[z, :, rows]
        sums[i] = mine + land[i, 0] + (land[i, 1] + land[i, 2])
        close.append(
            [send(sums.at[i, (me + d) % 4], near.at[i, d - 1], along[d - 1]) for d in (1, 2, 3)]
        )
    back = []
    for i, (rows, way) in enumerate(streams):
        _, along, me = axes(way)
        for copy in close[i]:
            copy.wait_recv()
        out[z, x, rows] = sums[i, me] + near[i, 0] + (near[i, 1] + near[i, 2])
        here = out.at[z, x, rows]
        back.append([send(here, here, peer) for peer in along])
    end = []
    for i, (rows, way) in enumerate(streams):
        for copy in back[i]:
            copy.wait_recv()
        here = line(out, way, 0, rows)
        end += [send(here, here, peer) for peer in axes(way)[0]]
    for copy in end:
        copy.wait_recv()
    copies.finish()


def reduce(part):
    n = BLOCK // SUB
    out = pl.pallas_call(
        reduce_kernel,
        out_shape=jax.ShapeDtypeStruct((NZ, NX, BLOCK, K), F32),
        in_specs=[VMEM],
        out_specs=VMEM,
        scratch_shapes=[
            pltpu.VMEM((n, 3, 4, SUB, K), F32),
            pltpu.VMEM((n, 4, SUB, K), F32),
            pltpu.VMEM((n, 3, SUB, K), F32),
            pltpu.SemaphoreType.DMA((12 * n,)),
            pltpu.SemaphoreType.DMA((12 * n,)),
        ],
        compiler_params=pltpu.CompilerParams(
            collective_id=1, has_side_effects=True, vmem_limit_bytes=BIG
        ),
        name="reduce",
    )(part.reshape(NZ, NX, BLOCK, K))
    return out.reshape(UB * BLOCK, K)


def scalars_kernel(mine, out, land_x, land_z, half, send_sem, recv_sem):
    _, _, _, along_x, along_z = col_place()
    greet(along_x + along_z)
    copies = Copies(send_sem, recv_sem)
    for copy in [copies.send(mine, land_x.at[i], peer) for i, peer in enumerate(along_x)]:
        copy.wait_recv()
    half[...] = mine[...] + land_x[0] + (land_x[1] + land_x[2])
    for copy in [copies.send(half, land_z.at[i], peer) for i, peer in enumerate(along_z)]:
        copy.wait_recv()
    out[...] = half[...] + land_z[0] + (land_z[1] + land_z[2])
    copies.finish()


def sum_scalars(mine):
    return pl.pallas_call(
        scalars_kernel,
        out_shape=jax.ShapeDtypeStruct((UB, BLOCK), F32),
        in_specs=[VMEM],
        out_specs=VMEM,
        scratch_shapes=[
            pltpu.VMEM((3, UB, BLOCK), F32),
            pltpu.VMEM((3, UB, BLOCK), F32),
            pltpu.VMEM((UB, BLOCK), F32),
            pltpu.SemaphoreType.DMA((6,)),
            pltpu.SemaphoreType.DMA((6,)),
        ],
        compiler_params=pltpu.CompilerParams(collective_id=2, has_side_effects=True, vmem_limit_bytes=BIG),
        name="scalars",
    )(mine)


def cg_kernel(
    order, part, start, yh, yl, th, tl, gram, weights, out,
    held, v, x_now, r_now, p_now, pulls, squares, parts, tot, land, sums, near,
    row_sums, land_x, land_z, half, send_sem, recv_sem, w_sem,
):
    _, z, x, along_x, along_z = col_place()
    load = pltpu.make_async_copy(weights.at[pl.ds(0, FAST)], held, w_sem)
    load.start()
    greet(along_x + along_z)
    copies = Copies(send_sem, recv_sem)
    send = copies.send
    far, close, back, end = {}, {}, {}, {}
    rounds = (part, parts.at[0], parts.at[1])

    def streams(s):
        for i in (2 * s, 2 * s + 1):
            way = i % 2 == 0
            first, second, me = (along_x, along_z, z) if way else (along_z, along_x, x)
            yield i, pl.ds(SUB * i, SUB), way, first, second, me

    def line(ref, way, d, rows):
        return ref.at[:, (x + d) % NX, rows] if way else ref.at[(z + d) % NZ, :, rows]

    def begin(k, s):
        for i, rows, way, first, _, _ in streams(s):
            far[k, i] = [
                send(line(rounds[k], way, d, rows), land.at[k, i, d - 1], first[d - 1])
                for d in (1, 2, 3)
            ]

    def sum_first(k, s):
        for i, rows, way, _, second, me in streams(s):
            for copy in far[k, i]:
                copy.wait_recv()
            mine = rounds[k][:, x, rows] if way else rounds[k][z, :, rows]
            sums[k, i] = mine + land[k, i, 0] + (land[k, i, 1] + land[k, i, 2])
            close[k, i] = [
                send(sums.at[k, i, (me + d) % 4], near.at[k, i, d - 1], second[d - 1])
                for d in (1, 2, 3)
            ]

    def sum_second(k, s):
        for i, rows, _, _, second, me in streams(s):
            for copy in close[k, i]:
                copy.wait_recv()
            tot[k, z, x, rows] = sums[k, i, me] + near[k, i, 0] + (near[k, i, 1] + near[k, i, 2])
            here = tot.at[k, z, x, rows]
            back[k, i] = [send(here, here, peer) for peer in second]

    def spread(k, s):
        for i, rows, way, first, _, _ in streams(s):
            for copy in back[k, i]:
                copy.wait_recv()
            here = line(tot.at[k], way, 0, rows)
            end[k, i] = [send(here, here, peer) for peer in first]

    def arrive(k, s):
        for i in (2 * s, 2 * s + 1):
            for copy in end[k, i]:
                copy.wait_recv()

    g = by_cols(*split(gram[...]))
    n = order[LIST - 1]

    def compute(k, s, before_end):
        rows = pl.ds(64 * s, 64)

        def step(b, _):
            total = tot[k - 1, b // NX, b % NX, rows]
            if k == 1:
                p = total - RIDGE * start[b, rows]
                r_now[b, rows] = p
            else:
                before = start[b, rows] if k == 2 else x_now[b, rows]
                r = r_now[b, rows]
                old = r if k == 2 else p_now[b, rows]
                x_now[b, rows], r_now[b, rows], p = update(total, before, r, old)
            p_now[b, rows] = p
            v[b, rows] = pair(p)
            return 0

        lax.fori_loop(0, UB, step, 0, unroll=16)

        def some(q, acc):
            last_b, acc = acc
            for u in range(STEP):
                j = q * STEP + u
                code = order[j]
                b, block = code & (UB - 1), (code >> 4) & 63
                w = jnp.where(j < n, held[j, rows], 0.0)
                scores = fold(dot(v[b, rows], by_cols(th[block], tl[block]), NN))
                if k < 3:
                    pull = fold(dot(pair(w * scores), by_cols(yh[block], yl[block]), NN))
                else:
                    pull = w * scores * scores
                acc = jnp.where(b == last_b, acc, 0.0) + pull
                last_b = b
                pulls[s, j] = acc
            return last_b, acc

        lax.fori_loop(0, FAST // STEP, some, (jnp.int32(-1), jnp.zeros((64, K), F32)))
        before_end()

        def close_up(b, _):
            end_of = order[LAST + b]
            pulled = jnp.where(end_of >= 0, pulls[s, jnp.maximum(end_of, 0)], 0.0)
            whole = fold(dot(v[b, rows], g, NN))
            if k < 3:
                parts[k - 1, b // NX, b % NX, rows] = whole + pulled
            else:
                squares[b, rows] = p_now[b, rows] * whole + pulled
            return 0

        lax.fori_loop(0, UB, close_up, 0, unroll=16)

    def nothing():
        pass

    begin(0, 0)
    begin(0, 1)
    sum_first(0, 0)
    for k in range(3):
        sum_first(k, 1)
        for work in (sum_second, spread):
            work(k, 0)
            work(k, 1)
        if k == 0:
            load.wait()
        arrive(k, 0)
        compute(k + 1, 0, nothing)
        if k < 2:
            begin(k + 1, 0)
        arrive(k, 1)
        compute(k + 1, 1, functools.partial(sum_first, k + 1, 0) if k < 2 else nothing)
        if k < 2:
            begin(k + 1, 1)

    for b in range(UB):
        row_sums[b : b + 1] = jnp.sum(squares[b].T, axis=0, keepdims=True)
    for copy in [send(row_sums, land_x.at[i], peer) for i, peer in enumerate(along_x)]:
        copy.wait_recv()
    half[...] = row_sums[...] + land_x[0] + (land_x[1] + land_x[2])
    for copy in [send(half, land_z.at[i], peer) for i, peer in enumerate(along_z)]:
        copy.wait_recv()
    both = half[...] + land_z[0] + (land_z[1] + land_z[2])
    for b in range(UB):
        p, r = p_now[b], r_now[b]
        below = jnp.broadcast_to(both[b : b + 1], (BLOCK, BLOCK)).T + RIDGE * dots(p, p)
        out[b] = x_now[b] + dots(r, r) / (below + EPSILON) * p
    copies.finish()


def all_steps(order, part, start, yh, yl, th, tl, gram, weights):
    n = BLOCK // SUB
    copies = 3 * 12 * n + 6
    blocks = (UB, BLOCK, K)
    out = pl.pallas_call(
        cg_kernel,
        out_shape=jax.ShapeDtypeStruct(blocks, F32),
        in_specs=[SMEM] + [VMEM] * 7 + [ANY],
        out_specs=VMEM,
        scratch_shapes=[
            pltpu.VMEM((FAST, BLOCK, BLOCK), F32),
            pltpu.VMEM((UB, BLOCK, 2 * K), BF16),
            pltpu.VMEM(blocks, F32),
            pltpu.VMEM(blocks, F32),
            pltpu.VMEM(blocks, F32),
            pltpu.VMEM((2, FAST, 64, K), F32),
            pltpu.VMEM(blocks, F32),
            pltpu.VMEM((2, NZ, NX, BLOCK, K), F32),
            pltpu.VMEM((3, NZ, NX, BLOCK, K), F32),
            pltpu.VMEM((3, n, 3, 4, SUB, K), F32),
            pltpu.VMEM((3, n, 4, SUB, K), F32),
            pltpu.VMEM((3, n, 3, SUB, K), F32),
            pltpu.VMEM((UB, BLOCK), F32),
            pltpu.VMEM((3, UB, BLOCK), F32),
            pltpu.VMEM((3, UB, BLOCK), F32),
            pltpu.VMEM((UB, BLOCK), F32),
            pltpu.SemaphoreType.DMA((copies,)),
            pltpu.SemaphoreType.DMA((copies,)),
            pltpu.SemaphoreType.DMA,
        ],
        compiler_params=pltpu.CompilerParams(
            collective_id=3, has_side_effects=True, vmem_limit_bytes=WHOLE
        ),
        name="steps",
    )(order, part.reshape(NZ, NX, BLOCK, K), start.reshape(blocks), yh, yl, th, tl, gram, weights)
    return out.reshape(UB * BLOCK, K)


def step_by_step(order, part, start, yh, yl, th, tl, gram, weights):
    total = reduce(part)
    tail = [VMEM] * 5 + [ANY]
    part, residual = local(first_kernel, "first", (USERS,) * 2, [SMEM, VMEM, VMEM] + tail)(
        order, total, start, yh, yl, th, tl, gram, weights
    )
    total = reduce(part)
    part, iterate, residual, direction = local(
        second_kernel, "second", (USERS,) * 4, [SMEM] + [VMEM] * 3 + tail
    )(order, total, start, residual, yh, yl, th, tl, gram, weights)
    total = reduce(part)
    squares = jax.ShapeDtypeStruct((UB, BLOCK), F32)
    part, iterate, residual, direction = local(
        third_kernel,
        "third",
        (squares,) + (USERS,) * 3,
        [SMEM] + [VMEM] * 4 + tail,
        [pltpu.VMEM((UB * BLOCK, K), F32)],
    )(order, total, iterate, residual, direction, yh, yl, th, tl, gram, weights)
    squares = sum_scalars(part)
    return pl.pallas_call(
        last_kernel,
        out_shape=USERS,
        in_specs=[VMEM] * 4,
        out_specs=VMEM,
        compiler_params=pltpu.CompilerParams(vmem_limit_bytes=BIG),
        name="last",
    )(squares, iterate, residual, direction)


def shards(user_factors, item_factors, fetch_list, tile_user, tile_slot, er, ec, en, tile_count):
    yh, yl, th, tl, gram, ent, peak = gather(
        item_factors.reshape(IB, BLOCK, K),
        fetch_list.reshape(1, 128),
        tile_user.reshape(1, TILES),
        tile_slot.reshape(1, TILES),
        er.reshape(TILES, NNZ),
        ec.reshape(TILES, NNZ),
        en.reshape(TILES, NNZ),
        tile_count.reshape(1, 1),
    )
    part, weights, order = build(
        ent.reshape(COLS, STAGE, NNZ), yh, yl, th, tl, gram, user_factors
    )
    return lax.cond(
        peak[0, 0] <= FAST,
        all_steps,
        step_by_step,
        order, part, user_factors, yh, yl, th, tl, gram, weights,
    )


def solution(mesh):
    return jax.shard_map(
        shards,
        mesh=mesh,
        in_specs=(
            P("row", None),
            P(("row", "col"), None),
            P("row", "col", None, None),
            P("row", "col", None),
            P("row", "col", None),
            P("row", "col", None, None),
            P("row", "col", None, None),
            P("row", "col", None, None),
            P("row", "col"),
        ),
        out_specs=P("row", None),
        check_vma=False,
    )
```

```python
import functools

import jax
import jax.numpy as jnp
from jax import lax
from jax.experimental import pallas as pl
from jax.experimental.pallas import tpu as pltpu
from jax.sharding import PartitionSpec as P

K = 128
BLOCK = 128
UB = 16
IB = 8
TILES = 32
NNZ = 512
NZ = NX = 4
NY = 4
ROWS = 8
COLS = 16
ALL_TILES = COLS * TILES
LIST = 1024
LAST = 512
FAST = 36
STEP = 18
SUB = 32
UNROLL = 4
BUILD = 4
SLOTS = 2 * BUILD
GROUP = 4
HELD = 32
STAGE = 3 * TILES + 8
HALF = 56
SCALE = 40.0
RIDGE = 0.5
EPSILON = 1e-06
MESH = pl.DeviceIdType.MESH
F32 = jnp.float32
BF16 = jnp.bfloat16
NT = (((1,), (1,)), ((), ()))
NN = (((1,), (0,)), ((), ()))
ANY = pl.BlockSpec(memory_space=pl.ANY)
VMEM = pl.BlockSpec(memory_space=pltpu.VMEM)
SMEM = pl.BlockSpec(memory_space=pltpu.SMEM)
HBM = pl.BlockSpec(memory_space=pltpu.HBM)
BIG = 24 * 2**20
WHOLE = 40 * 2**20


def dot(a, b, dims):
    return lax.dot_general(a, b, dims, preferred_element_type=F32)


def split(a):
    high = a.astype(BF16)
    return high, (a - high.astype(F32)).astype(BF16)


def pair(a):
    return jnp.concatenate(split(a), axis=1)


def fold(wide):
    return wide[:, 0:128] + wide[:, 128:256]


def by_cols(high, low):
    both = jnp.concatenate([high, low], axis=1)
    return jnp.concatenate([both, both], axis=0)


def greet(peers):
    barrier = pltpu.get_barrier_semaphore()
    for peer in peers:
        pl.semaphore_signal(barrier, inc=1, device_id=peer, device_id_type=MESH)
    pl.semaphore_wait(barrier, len(peers))


class Copies:
    def __init__(self, send_sem, recv_sem):
        self.send_sem, self.recv_sem, self.made = send_sem, recv_sem, []

    def send(self, src, dst, peer):
        i = len(self.made)
        copy = pltpu.make_async_remote_copy(
            src_ref=src,
            dst_ref=dst,
            send_sem=self.send_sem.at[i],
            recv_sem=self.recv_sem.at[i],
            device_id=peer,
            device_id_type=MESH,
        )
        copy.start()
        self.made.append(copy)
        return copy

    def finish(self):
        for copy in self.made:
            copy.wait_send()


def col_place():
    c = lax.axis_index("col")
    z, x = c // NX, c % NX
    along_x = [{"col": z * NX + (x + d) % NX} for d in range(1, NX)]
    along_z = [{"col": ((z + d) % NZ) * NX + x} for d in range(1, NZ)]
    return c, z, x, along_x, along_z


def gather_kernel(
    items, fetch, user, slot, er, ec, en, count, yh, yl, th, tl, gram, ent, peak,
    stage, land, fetch_in, slot_in, user_in, small, keys, most, seen, send_sem, recv_sem, own_sem, in_sem,
):
    c, z, x, along_x, along_z = col_place()
    r = lax.axis_index("row")
    y, core = r // 2, r % 2
    right, left, across = (((y + d) % NY) * 2 + core for d in (1, 3, 2))
    other = y * 2 + 1 - core
    to_right, to_left, to_other = {"row": right}, {"row": left}, {"row": other}
    to_across = {"row": across}
    loads = [
        pltpu.make_async_copy(src, dst, in_sem.at[i])
        for i, (src, dst) in enumerate(
            (
                (er, stage.at[pl.ds(0, TILES)]),
                (ec, stage.at[pl.ds(TILES, TILES)]),
                (en, stage.at[pl.ds(2 * TILES, TILES)]),
                (items, land.at[r]),
                (fetch, fetch_in),
                (slot, slot_in),
                (user, user_in),
            )
        )
    ]
    for load in loads:
        load.start()
    greet(along_x + along_z + [to_right, to_left, to_across, to_other])
    copies = Copies(send_sem, recv_sem)
    send = copies.send
    half = [items.at[pl.ds(4 * i, 4)] for i in (0, 1)]
    there = [land.at[r, pl.ds(4 * i, 4)] for i in (0, 1)]
    from_left, from_right = [None, None], [None, None]
    for i in (0, 1):
        from_left[i] = send(half[i], there[i], to_right)
        from_right[1 - i] = send(half[1 - i], there[1 - i], to_left)
    between = [send(items, land.at[r], to_other)]

    for load in loads[4:]:
        load.wait()
    small[...] = jnp.zeros_like(small)
    small[0:1, 0:TILES] = slot_in[...]
    small[1:2, 0:TILES] = user_in[...]
    slots = small[0:1]
    table = jnp.broadcast_to(fetch_in[...].astype(F32), (128, 128)).T
    ids = lax.broadcasted_iota(jnp.int32, (128, 128), 0)
    local_id = jnp.sum(jnp.where(ids == slots, table, 0.0), axis=0, keepdims=True).astype(jnp.int32)
    lanes = lax.broadcasted_iota(jnp.int32, (1, 128), 1)
    last = 3 * TILES
    stage[last : last + 1, 0:128] = jnp.where(lanes < count[0, 0], slots & (COLS - 1), -1)
    stage[last + 1 : last + 2, 0:128] = ((slots >> 4) * IB + local_id) * UB + small[1:2]
    first_key = stage[last : last + 1, 0:128]
    keys[z, x] = jnp.broadcast_to(first_key, (8, 128))
    for load in loads[:3]:
        load.wait()
    own = pltpu.make_async_copy(stage, ent.at[z, x], own_sem)
    own.start()

    first, second = pl.ds(0, HALF), pl.ds(HALF, STAGE - HALF)
    parts = (pl.ds(0, 32), pl.ds(32, 24)), (pl.ds(56, 24), pl.ds(80, 24))
    ways = (
        (first, along_x, along_z, lambda d, e: ent.at[(z + e) % NZ, (x + d) % NX]),
        (second, along_z, along_x, lambda d, e: ent.at[(z + d) % NZ, (x + e) % NX]),
    )
    near = [[None] * 4, [None] * 4]
    up = [[None] * 4, [None] * 4]
    down = [[None] * 4, [None] * 4]

    def spread(w, d, source):
        rows, _, across_way, at = ways[w]
        to = at(-d, 0).at[rows]
        up[w][d] = send(source, to, across_way[0])
        down[w][d] = send(source, to, across_way[2])

    for w, (rows, along, _, at) in enumerate(ways):
        for d in (1, 3, 2):
            near[w][d] = send(stage.at[rows], at(0, 0).at[rows], along[d - 1])
        spread(w, 0, stage.at[rows])
    mine = keys.at[z, x]
    told_keys = [send(mine, mine, peer) for peer in along_x]

    far = []

    def pass_on(w, d):
        _, _, across_way, at = ways[w]
        up[w][d].wait_recv()
        piece = at(-d, -1).at[parts[w][0]]
        far.append(send(piece, piece, across_way[0]))
        down[w][d].wait_recv()
        piece = at(-d, 1).at[parts[w][1]]
        far.append(send(piece, piece, across_way[2]))

    def add(row, sums):
        def one(i, sums):
            high, low = split(land[row, i])
            high_t = high.T
            at = row * IB + i
            yh[at] = high
            yl[at] = low
            th[at] = high_t
            tl[at] = low.T
            return sums + dot(high_t, jnp.concatenate([high, low], axis=1), NN)

        return lax.fori_loop(0, IB, one, sums, unroll=4)

    loads[3].wait()
    sums = add(r, jnp.zeros((K, 2 * K), F32))
    for copy in told_keys:
        copy.wait_recv()
    mine = keys.at[z]
    told_keys = [send(mine, mine, peer) for peer in along_z]

    for d in (1, 3, 2):
        for w in (0, 1):
            near[w][d].wait_recv()
            rows, _, _, at = ways[w]
            spread(w, d, at(-d, 0).at[rows])
    for w in (0, 1):
        pass_on(w, 0)
    from_left[0].wait_recv()
    piece = land.at[left, pl.ds(0, 4)]
    round_y = [send(piece, piece, to_right)]
    from_right[1].wait_recv()
    piece = land.at[right, pl.ds(4, 4)]
    round_y.append(send(piece, piece, to_left))
    for copy in told_keys:
        copy.wait_recv()
    owners = keys[:, :, 0, :].reshape(COLS, 128)
    longest = jnp.zeros((1, 1), jnp.int32)
    for column in range(COLS):
        here = jnp.where(owners == column, 1, 0)
        here = jnp.sum(jnp.sum(here, axis=0, keepdims=True), axis=1, keepdims=True)
        longest = jnp.maximum(longest, here)
    most[0] = jnp.broadcast_to(longest, (8, 128))

    told = [
        send(most.at[0], seen.at[i], peer)
        for i, peer in enumerate((to_right, to_left, to_across))
    ]
    between[0].wait_recv()
    sums = add(other, sums)
    for d in (1, 3):
        for w in (0, 1):
            pass_on(w, d)
    from_left[1].wait_recv()
    between.append(send(land.at[left], land.at[left], to_other))
    from_right[0].wait_recv()
    between.append(send(land.at[right], land.at[right], to_other))
    for w in (0, 1):
        pass_on(w, 2)
    for copy in told:
        copy.wait_recv()
    most[1] = jnp.maximum(jnp.maximum(most[0], seen[0]), jnp.maximum(seen[1], seen[2]))
    told = send(most.at[1], seen.at[3], to_other)
    sums = add(left, sums)
    sums = add(right, sums)
    for copy in round_y:
        copy.wait_recv()
    between.append(send(land.at[across], land.at[across], to_other))
    sums = add(across, sums)
    for copy, d in zip(between[1:], (3, 1, 2)):
        copy.wait_recv()
        sums = add(((y + d) % NY) * 2 + 1 - core, sums)
    told.wait_recv()
    peak[...] = jnp.maximum(most[1], seen[3])
    for copy in far:
        copy.wait_recv()
    own.wait()
    mixed = sums[:, K:]
    gram[...] = sums[:, :K] + (mixed + mixed.T)
    copies.finish()


def gather(items, fetch, user, slot, er, ec, en, count):
    n = 6 + 4 + 2 * (3 + 8 + 8) + 10
    return pl.pallas_call(
        gather_kernel,
        out_shape=(
            *[jax.ShapeDtypeStruct((ROWS * IB, BLOCK, K), BF16)] * 4,
            jax.ShapeDtypeStruct((K, K), F32),
            jax.ShapeDtypeStruct((NZ, NX, STAGE, NNZ), jnp.int32),
            jax.ShapeDtypeStruct((8, 128), jnp.int32),
        ),
        in_specs=[HBM] * 7 + [SMEM],
        out_specs=(VMEM, VMEM, VMEM, VMEM, VMEM, ANY, VMEM),
        scratch_shapes=[
            pltpu.VMEM((STAGE, NNZ), jnp.int32),
            pltpu.VMEM((ROWS, IB, BLOCK, K), F32),
            pltpu.VMEM((1, 128), jnp.int32),
            pltpu.VMEM((1, TILES), jnp.int32),
            pltpu.VMEM((1, TILES), jnp.int32),
            pltpu.VMEM((8, 128), jnp.int32),
            pltpu.VMEM((NZ, NX, 8, 128), jnp.int32),
            pltpu.VMEM((2, 8, 128), jnp.int32),
            pltpu.VMEM((4, 8, 128), jnp.int32),
            pltpu.SemaphoreType.DMA((n,)),
            pltpu.SemaphoreType.DMA((n,)),
            pltpu.SemaphoreType.DMA,
            pltpu.SemaphoreType.DMA((7,)),
        ],
        compiler_params=pltpu.CompilerParams(
            collective_id=0, has_side_effects=True, vmem_limit_bytes=BIG
        ),
        name="gather",
    )(*[pltpu.with_memory_space_constraint(a, pltpu.HBM) for a in (items, fetch, user, slot, er, ec, en)], count)


def build_kernel(
    ent, yh, yl, th, tl, gram, start, out, weights, order, meta, found, place, held, v, sem, meta_sem
):
    fetched = pltpu.make_async_copy(
        ent.at[:, pl.ds(3 * TILES, 8), pl.ds(0, 128)], meta, meta_sem
    )
    fetched.start()
    g = by_cols(*split(gram[...]))

    def begin(b, _):
        at = rows_of(b)
        both = pair(start[at])
        v[at] = both
        out[at] = -fold(dot(both, g, NN))
        return 0

    lax.fori_loop(0, UB, begin, 0, unroll=UNROLL)
    fetched.wait()
    me = lax.axis_index("col")

    def scan(c, n):
        for t in range(TILES):
            found[n] = (c * TILES + t) * (64 * UB) + meta[c, 1, t]
            n = n + jnp.where(meta[c, 0, t] == me, 1, 0)
        return n

    n = lax.fori_loop(0, COLS, scan, 0)
    order[LIST - 1] = n

    for b in range(UB):
        place[b] = 0

    def count(j, _):
        b = found[j] & (UB - 1)
        place[b] = place[b] + 1
        return 0

    lax.fori_loop(0, n, count, 0)
    total = 0
    for b in range(UB):
        of_b = place[b]
        order[LAST + b] = jnp.where(of_b > 0, total + of_b - 1, -1)
        place[b] = total
        total = total + of_b

    def put(j, _):
        code = found[j]
        b = code & (UB - 1)
        to = place[b]
        order[to] = code
        place[b] = to + 1
        return 0

    lax.fori_loop(0, n, put, 0)
    ids = lax.broadcasted_iota(jnp.int32, (BLOCK, NNZ), 0)
    one, none = jnp.ones((), BF16), jnp.zeros((), BF16)

    def out_copy(j):
        slot = j % SLOTS
        return pltpu.make_async_copy(held.at[slot], weights.at[j], sem.at[slot])

    def group(q, _):
        for u in range(BUILD):
            j = q * BUILD + u

            @pl.when((j >= SLOTS) & (j - SLOTS < n))
            def _(j=j):
                out_copy(j - SLOTS).wait()

        made = []
        for u in range(BUILD):
            j = q * BUILD + u
            code = jnp.where(j < n, order[j], 0)
            b, block, at = code % UB, (code // UB) % 64, code // (64 * UB)
            c, t = at // TILES, at % TILES
            rows = jnp.where(j < n, ent[c, pl.ds(t, 1), :], BLOCK)
            cols = ent[c, pl.ds(TILES + t, 1), :]
            counts = ent[c, pl.ds(2 * TILES + t, 1), :].astype(F32)
            in_col = ids == cols
            once = jnp.where(in_col, 1.0, 0.0).astype(BF16)
            ones = jnp.where(ids == rows, 1.0, 0.0).astype(BF16)
            many = jnp.where(in_col, counts, 0.0).astype(BF16)
            both = dot(ones, jnp.concatenate([once, many], axis=0), NT)
            times, excess = both[:, :BLOCK], SCALE * both[:, BLOCK:]
            made.append((rows_of(b), block, times, excess))
        scores = [
            fold(dot(v[where], by_cols(th[block], tl[block]), NN)) for where, block, _, _ in made
        ]
        pulls = [
            fold(
                dot(pair(times + excess * (1.0 - score)), by_cols(yh[block], yl[block]), NN)
            )
            for (_, block, times, excess), score in zip(made, scores)
        ]
        for u, ((where, _, _, excess), pull) in enumerate(zip(made, pulls)):
            held[(q * BUILD + u) % SLOTS] = excess
            out[where] += pull
        for u in range(BUILD):
            j = q * BUILD + u

            @pl.when(j < n)
            def _(j=j):
                out_copy(j).start()

        return 0

    groups = (n + BUILD - 1) // BUILD
    lax.fori_loop(0, groups, group, 0)

    def drain(j, _):
        out_copy(j).wait()
        return 0

    lax.fori_loop(jnp.maximum(groups * BUILD - SLOTS, 0), n, drain, 0)


def build(ent, yh, yl, th, tl, gram, start):
    return pl.pallas_call(
        build_kernel,
        out_shape=(
            jax.ShapeDtypeStruct((UB * BLOCK, K), F32),
            jax.ShapeDtypeStruct((ALL_TILES, BLOCK, BLOCK), F32),
            jax.ShapeDtypeStruct((LIST,), jnp.int32),
        ),
        in_specs=[VMEM] * 7,
        out_specs=(VMEM, ANY, SMEM),
        scratch_shapes=[
            pltpu.SMEM((COLS, 8, 128), jnp.int32),
            pltpu.SMEM((LIST,), jnp.int32),
            pltpu.SMEM((UB,), jnp.int32),
            pltpu.VMEM((SLOTS, BLOCK, BLOCK), F32),
            pltpu.VMEM((UB * BLOCK, 2 * K), BF16),
            pltpu.SemaphoreType.DMA((SLOTS,)),
            pltpu.SemaphoreType.DMA,
        ],
        compiler_params=pltpu.CompilerParams(vmem_limit_bytes=BIG),
        name="build",
    )(ent, yh, yl, th, tl, gram, start)


def fetch_tiles(order, weights, held, sem, base):
    here = jnp.minimum(order[LIST - 1] - base, HELD)

    def begin(i, _):
        pltpu.make_async_copy(weights.at[base + i], held.at[i], sem.at[i]).start()
        return 0

    lax.fori_loop(0, here, begin, 0)
    return here


def each_tile(order, weights, held, sem, work):
    n = order[LIST - 1]

    def batch(k, _):
        base = k * HELD
        here = jnp.minimum(n - base, HELD)

        def group(q, _):
            for u in range(GROUP):
                i = q * GROUP + u

                @pl.when(i < here)
                def _(i=i):
                    pltpu.make_async_copy(weights.at[base + i], held.at[i], sem.at[i]).wait()

            for u in range(GROUP):
                i = q * GROUP + u
                live = i < here
                code = jnp.where(live, order[base + i], 0)
                w = jnp.where(live, held[i], 0.0)
                work(code % UB, (code // UB) % 64, w)
            return 0

        lax.fori_loop(0, (here + GROUP - 1) // GROUP, group, 0)

        @pl.when(n > base + HELD)
        def _():
            fetch_tiles(order, weights, held, sem, base + HELD)

        return 0

    lax.fori_loop(0, (n + HELD - 1) // HELD, batch, 0)


def rows_of(b):
    return pl.ds(pl.multiple_of(b * BLOCK, BLOCK), BLOCK)


def dots(a, b):
    return jnp.sum(a * b, axis=1, keepdims=True)


def pull_tiles(order, weights, held, sem, yh, yl, th, tl, v, out):
    def work(b, block, w):
        at = rows_of(b)
        scores = fold(dot(v[at], by_cols(th[block], tl[block]), NN))
        out[at] += fold(dot(pair(w * scores), by_cols(yh[block], yl[block]), NN))

    each_tile(order, weights, held, sem, work)


def first_kernel(order, total, start, yh, yl, th, tl, gram, weights, out, residual, v, held, sem):
    fetch_tiles(order, weights, held, sem, 0)
    g = by_cols(*split(gram[...]))

    def begin(b, _):
        at = rows_of(b)
        p = total[at] - RIDGE * start[at]
        residual[at] = p
        both = pair(p)
        v[at] = both
        out[at] = fold(dot(both, g, NN))
        return 0

    lax.fori_loop(0, UB, begin, 0, unroll=UNROLL)
    pull_tiles(order, weights, held, sem, yh, yl, th, tl, v, out)


def update(total, iterate, residual, direction):
    image = total + RIDGE * direction
    now = dots(residual, residual)
    alpha = now / (dots(direction, image) + EPSILON)
    iterate = iterate + alpha * direction
    residual = residual - alpha * image
    after = dots(residual, residual)
    direction = residual + after / (now + EPSILON) * direction
    return iterate, residual, direction


def second_kernel(
    order, total, iterate, residual, yh, yl, th, tl, gram, weights, out, new_x, new_r, new_p, v, held, sem
):
    fetch_tiles(order, weights, held, sem, 0)
    g = by_cols(*split(gram[...]))

    def begin(b, _):
        at = rows_of(b)
        r = residual[at]
        new_x[at], new_r[at], p = update(total[at], iterate[at], r, r)
        new_p[at] = p
        both = pair(p)
        v[at] = both
        out[at] = fold(dot(both, g, NN))
        return 0

    lax.fori_loop(0, UB, begin, 0, unroll=UNROLL)
    pull_tiles(order, weights, held, sem, yh, yl, th, tl, v, out)


def third_kernel(
    order, total, iterate, residual, direction, yh, yl, th, tl, gram, weights,
    squares, new_x, new_r, new_p, v, acc, held, sem,
):
    fetch_tiles(order, weights, held, sem, 0)
    g = by_cols(*split(gram[...]))

    def begin(b, _):
        at = rows_of(b)
        new_x[at], new_r[at], p = update(total[at], iterate[at], residual[at], direction[at])
        new_p[at] = p
        both = pair(p)
        v[at] = both
        acc[at] = p * fold(dot(both, g, NN))
        return 0

    lax.fori_loop(0, UB, begin, 0, unroll=UNROLL)

    def work(b, block, w):
        at = rows_of(b)
        scores = fold(dot(v[at], by_cols(th[block], tl[block]), NN))
        acc[at] += w * scores * scores

    each_tile(order, weights, held, sem, work)
    for b in range(UB):
        squares[b : b + 1] = jnp.sum(acc[b * BLOCK : (b + 1) * BLOCK].T, axis=0, keepdims=True)


def last_kernel(squares, iterate, residual, direction, out):
    sums = squares[...]
    for b in range(UB):
        at = pl.ds(b * BLOCK, BLOCK)
        p = direction[at]
        r = residual[at]
        below = jnp.broadcast_to(sums[b : b + 1], (BLOCK, BLOCK)).T + RIDGE * dots(p, p)
        out[at] = iterate[at] + dots(r, r) / (below + EPSILON) * p


USERS = jax.ShapeDtypeStruct((UB * BLOCK, K), F32)


def local(kernel, name, outs, specs, scratch=()):
    tiles = [
        pltpu.VMEM((UB * BLOCK, 2 * K), BF16),
        *scratch,
        pltpu.VMEM((HELD, BLOCK, BLOCK), F32),
        pltpu.SemaphoreType.DMA((HELD,)),
    ]
    return pl.pallas_call(
        kernel,
        out_shape=outs,
        in_specs=specs,
        out_specs=tuple(VMEM for _ in outs),
        scratch_shapes=tiles,
        compiler_params=pltpu.CompilerParams(vmem_limit_bytes=BIG),
        name=name,
    )


def reduce_kernel(part, out, land, sums, near, send_sem, recv_sem):
    c, z, x, along_x, along_z = col_place()
    greet(along_x + along_z)
    copies = Copies(send_sem, recv_sem)
    send = copies.send
    streams = [(pl.ds(SUB * i, SUB), i % 2 == 0) for i in range(BLOCK // SUB)]

    def line(ref, way, d, rows):
        return ref.at[:, (x + d) % NX, rows] if way else ref.at[(z + d) % NZ, :, rows]

    def axes(way):
        return (along_x, along_z, z) if way else (along_z, along_x, x)

    far = [
        [send(line(part, way, d, rows), land.at[i, d - 1], axes(way)[0][d - 1]) for d in (1, 2, 3)]
        for i, (rows, way) in enumerate(streams)
    ]
    close = []
    for i, (rows, way) in enumerate(streams):
        _, along, me = axes(way)
        for copy in far[i]:
            copy.wait_recv()
        mine = part[:, x, rows] if way else part[z, :, rows]
        sums[i] = mine + land[i, 0] + (land[i, 1] + land[i, 2])
        close.append(
            [send(sums.at[i, (me + d) % 4], near.at[i, d - 1], along[d - 1]) for d in (1, 2, 3)]
        )
    back = []
    for i, (rows, way) in enumerate(streams):
        _, along, me = axes(way)
        for copy in close[i]:
            copy.wait_recv()
        out[z, x, rows] = sums[i, me] + near[i, 0] + (near[i, 1] + near[i, 2])
        here = out.at[z, x, rows]
        back.append([send(here, here, peer) for peer in along])
    end = []
    for i, (rows, way) in enumerate(streams):
        for copy in back[i]:
            copy.wait_recv()
        here = line(out, way, 0, rows)
        end += [send(here, here, peer) for peer in axes(way)[0]]
    for copy in end:
        copy.wait_recv()
    copies.finish()


def reduce(part):
    n = BLOCK // SUB
    out = pl.pallas_call(
        reduce_kernel,
        out_shape=jax.ShapeDtypeStruct((NZ, NX, BLOCK, K), F32),
        in_specs=[VMEM],
        out_specs=VMEM,
        scratch_shapes=[
            pltpu.VMEM((n, 3, 4, SUB, K), F32),
            pltpu.VMEM((n, 4, SUB, K), F32),
            pltpu.VMEM((n, 3, SUB, K), F32),
            pltpu.SemaphoreType.DMA((12 * n,)),
            pltpu.SemaphoreType.DMA((12 * n,)),
        ],
        compiler_params=pltpu.CompilerParams(
            collective_id=1, has_side_effects=True, vmem_limit_bytes=BIG
        ),
        name="reduce",
    )(part.reshape(NZ, NX, BLOCK, K))
    return out.reshape(UB * BLOCK, K)


def scalars_kernel(mine, out, land_x, land_z, half, send_sem, recv_sem):
    _, _, _, along_x, along_z = col_place()
    greet(along_x + along_z)
    copies = Copies(send_sem, recv_sem)
    for copy in [copies.send(mine, land_x.at[i], peer) for i, peer in enumerate(along_x)]:
        copy.wait_recv()
    half[...] = mine[...] + land_x[0] + (land_x[1] + land_x[2])
    for copy in [copies.send(half, land_z.at[i], peer) for i, peer in enumerate(along_z)]:
        copy.wait_recv()
    out[...] = half[...] + land_z[0] + (land_z[1] + land_z[2])
    copies.finish()


def sum_scalars(mine):
    return pl.pallas_call(
        scalars_kernel,
        out_shape=jax.ShapeDtypeStruct((UB, BLOCK), F32),
        in_specs=[VMEM],
        out_specs=VMEM,
        scratch_shapes=[
            pltpu.VMEM((3, UB, BLOCK), F32),
            pltpu.VMEM((3, UB, BLOCK), F32),
            pltpu.VMEM((UB, BLOCK), F32),
            pltpu.SemaphoreType.DMA((6,)),
            pltpu.SemaphoreType.DMA((6,)),
        ],
        compiler_params=pltpu.CompilerParams(collective_id=2, has_side_effects=True, vmem_limit_bytes=BIG),
        name="scalars",
    )(mine)


def cg_kernel(
    order, part, start, yh, yl, th, tl, gram, weights, out,
    held, v, x_now, r_now, p_now, pulls, squares, parts, tot, land, sums, near,
    row_sums, land_x, land_z, half, send_sem, recv_sem, w_sem,
):
    _, z, x, along_x, along_z = col_place()
    load = pltpu.make_async_copy(weights.at[pl.ds(0, FAST)], held, w_sem)
    load.start()
    greet(along_x + along_z)
    copies = Copies(send_sem, recv_sem)
    send = copies.send
    far, close, back, end = {}, {}, {}, {}
    rounds = (part, parts.at[0], parts.at[1])

    def streams(s):
        for i in (2 * s, 2 * s + 1):
            way = i % 2 == 0
            first, second, me = (along_x, along_z, z) if way else (along_z, along_x, x)
            yield i, pl.ds(SUB * i, SUB), way, first, second, me

    def line(ref, way, d, rows):
        return ref.at[:, (x + d) % NX, rows] if way else ref.at[(z + d) % NZ, :, rows]

    def begin(k, s):
        for i, rows, way, first, _, _ in streams(s):
            far[k, i] = [
                send(line(rounds[k], way, d, rows), land.at[k, i, d - 1], first[d - 1])
                for d in (1, 2, 3)
            ]

    def sum_first(k, s):
        for i, rows, way, _, second, me in streams(s):
            for copy in far[k, i]:
                copy.wait_recv()
            mine = rounds[k][:, x, rows] if way else rounds[k][z, :, rows]
            sums[k, i] = mine + land[k, i, 0] + (land[k, i, 1] + land[k, i, 2])
            close[k, i] = [
                send(sums.at[k, i, (me + d) % 4], near.at[k, i, d - 1], second[d - 1])
                for d in (1, 2, 3)
            ]

    def sum_second(k, s):
        for i, rows, _, _, second, me in streams(s):
            for copy in close[k, i]:
                copy.wait_recv()
            tot[k, z, x, rows] = sums[k, i, me] + near[k, i, 0] + (near[k, i, 1] + near[k, i, 2])
            here = tot.at[k, z, x, rows]
            back[k, i] = [send(here, here, peer) for peer in second]

    def spread(k, s):
        for i, rows, way, first, _, _ in streams(s):
            for copy in back[k, i]:
                copy.wait_recv()
            here = line(tot.at[k], way, 0, rows)
            end[k, i] = [send(here, here, peer) for peer in first]

    def arrive(k, s):
        for i in (2 * s, 2 * s + 1):
            for copy in end[k, i]:
                copy.wait_recv()

    g = by_cols(*split(gram[...]))
    n = order[LIST - 1]

    def compute(k, s, before_end):
        rows = pl.ds(64 * s, 64)

        def step(b, _):
            total = tot[k - 1, b // NX, b % NX, rows]
            if k == 1:
                p = total - RIDGE * start[b, rows]
                r_now[b, rows] = p
            else:
                before = start[b, rows] if k == 2 else x_now[b, rows]
                r = r_now[b, rows]
                old = r if k == 2 else p_now[b, rows]
                x_now[b, rows], r_now[b, rows], p = update(total, before, r, old)
            p_now[b, rows] = p
            v[b, rows] = pair(p)
            return 0

        lax.fori_loop(0, UB, step, 0, unroll=16)

        def some(q, acc):
            last_b, acc = acc
            for u in range(STEP):
                j = q * STEP + u
                code = order[j]
                b, block = code & (UB - 1), (code >> 4) & 63
                w = jnp.where(j < n, held[j, rows], 0.0)
                scores = fold(dot(v[b, rows], by_cols(th[block], tl[block]), NN))
                if k < 3:
                    pull = fold(dot(pair(w * scores), by_cols(yh[block], yl[block]), NN))
                else:
                    pull = w * scores * scores
                acc = jnp.where(b == last_b, acc, 0.0) + pull
                last_b = b
                pulls[s, j] = acc
            return last_b, acc

        lax.fori_loop(0, FAST // STEP, some, (jnp.int32(-1), jnp.zeros((64, K), F32)))
        before_end()

        def close_up(b, _):
            end_of = order[LAST + b]
            pulled = jnp.where(end_of >= 0, pulls[s, jnp.maximum(end_of, 0)], 0.0)
            whole = fold(dot(v[b, rows], g, NN))
            if k < 3:
                parts[k - 1, b // NX, b % NX, rows] = whole + pulled
            else:
                squares[b, rows] = p_now[b, rows] * whole + pulled
            return 0

        lax.fori_loop(0, UB, close_up, 0, unroll=16)

    def nothing():
        pass

    begin(0, 0)
    begin(0, 1)
    sum_first(0, 0)
    for k in range(3):
        sum_first(k, 1)
        for work in (sum_second, spread):
            work(k, 0)
            work(k, 1)
        if k == 0:
            load.wait()
        arrive(k, 0)
        compute(k + 1, 0, nothing)
        if k < 2:
            begin(k + 1, 0)
        arrive(k, 1)
        compute(k + 1, 1, functools.partial(sum_first, k + 1, 0) if k < 2 else nothing)
        if k < 2:
            begin(k + 1, 1)

    for b in range(UB):
        row_sums[b : b + 1] = jnp.sum(squares[b].T, axis=0, keepdims=True)
    for copy in [send(row_sums, land_x.at[i], peer) for i, peer in enumerate(along_x)]:
        copy.wait_recv()
    half[...] = row_sums[...] + land_x[0] + (land_x[1] + land_x[2])
    for copy in [send(half, land_z.at[i], peer) for i, peer in enumerate(along_z)]:
        copy.wait_recv()
    both = half[...] + land_z[0] + (land_z[1] + land_z[2])
    for b in range(UB):
        p, r = p_now[b], r_now[b]
        below = jnp.broadcast_to(both[b : b + 1], (BLOCK, BLOCK)).T + RIDGE * dots(p, p)
        out[b] = x_now[b] + dots(r, r) / (below + EPSILON) * p
    copies.finish()


def all_steps(order, part, start, yh, yl, th, tl, gram, weights):
    n = BLOCK // SUB
    copies = 3 * 12 * n + 6
    blocks = (UB, BLOCK, K)
    out = pl.pallas_call(
        cg_kernel,
        out_shape=jax.ShapeDtypeStruct(blocks, F32),
        in_specs=[SMEM] + [VMEM] * 7 + [ANY],
        out_specs=VMEM,
        scratch_shapes=[
            pltpu.VMEM((FAST, BLOCK, BLOCK), F32),
            pltpu.VMEM((UB, BLOCK, 2 * K), BF16),
            pltpu.VMEM(blocks, F32),
            pltpu.VMEM(blocks, F32),
            pltpu.VMEM(blocks, F32),
            pltpu.VMEM((2, FAST, 64, K), F32),
            pltpu.VMEM(blocks, F32),
            pltpu.VMEM((2, NZ, NX, BLOCK, K), F32),
            pltpu.VMEM((3, NZ, NX, BLOCK, K), F32),
            pltpu.VMEM((3, n, 3, 4, SUB, K), F32),
            pltpu.VMEM((3, n, 4, SUB, K), F32),
            pltpu.VMEM((3, n, 3, SUB, K), F32),
            pltpu.VMEM((UB, BLOCK), F32),
            pltpu.VMEM((3, UB, BLOCK), F32),
            pltpu.VMEM((3, UB, BLOCK), F32),
            pltpu.VMEM((UB, BLOCK), F32),
            pltpu.SemaphoreType.DMA((copies,)),
            pltpu.SemaphoreType.DMA((copies,)),
            pltpu.SemaphoreType.DMA,
        ],
        compiler_params=pltpu.CompilerParams(
            collective_id=3, has_side_effects=True, vmem_limit_bytes=WHOLE
        ),
        name="steps",
    )(order, part.reshape(NZ, NX, BLOCK, K), start.reshape(blocks), yh, yl, th, tl, gram, weights)
    return out.reshape(UB * BLOCK, K)


def step_by_step(order, part, start, yh, yl, th, tl, gram, weights):
    total = reduce(part)
    tail = [VMEM] * 5 + [ANY]
    part, residual = local(first_kernel, "first", (USERS,) * 2, [SMEM, VMEM, VMEM] + tail)(
        order, total, start, yh, yl, th, tl, gram, weights
    )
    total = reduce(part)
    part, iterate, residual, direction = local(
        second_kernel, "second", (USERS,) * 4, [SMEM] + [VMEM] * 3 + tail
    )(order, total, start, residual, yh, yl, th, tl, gram, weights)
    total = reduce(part)
    squares = jax.ShapeDtypeStruct((UB, BLOCK), F32)
    part, iterate, residual, direction = local(
        third_kernel,
        "third",
        (squares,) + (USERS,) * 3,
        [SMEM] + [VMEM] * 4 + tail,
        [pltpu.VMEM((UB * BLOCK, K), F32)],
    )(order, total, iterate, residual, direction, yh, yl, th, tl, gram, weights)
    squares = sum_scalars(part)
    return pl.pallas_call(
        last_kernel,
        out_shape=USERS,
        in_specs=[VMEM] * 4,
        out_specs=VMEM,
        compiler_params=pltpu.CompilerParams(vmem_limit_bytes=BIG),
        name="last",
    )(squares, iterate, residual, direction)


def shards(user_factors, item_factors, fetch_list, tile_user, tile_slot, er, ec, en, tile_count):
    yh, yl, th, tl, gram, ent, peak = gather(
        item_factors.reshape(IB, BLOCK, K),
        fetch_list.reshape(1, 128),
        tile_user.reshape(1, TILES),
        tile_slot.reshape(1, TILES),
        er.reshape(TILES, NNZ),
        ec.reshape(TILES, NNZ),
        en.reshape(TILES, NNZ),
        tile_count.reshape(1, 1),
    )
    part, weights, order = build(
        ent.reshape(COLS, STAGE, NNZ), yh, yl, th, tl, gram, user_factors
    )
    return lax.cond(
        peak[0, 0] <= FAST,
        all_steps,
        step_by_step,
        order, part, user_factors, yh, yl, th, tl, gram, weights,
    )


def solution(mesh):
    return jax.shard_map(
        shards,
        mesh=mesh,
        in_specs=(
            P("row", None),
            P(("row", "col"), None),
            P("row", "col", None, None),
            P("row", "col", None),
            P("row", "col", None),
            P("row", "col", None, None),
            P("row", "col", None, None),
            P("row", "col", None, None),
            P("row", "col"),
        ),
        out_specs=P("row", None),
        check_vma=False,
    )
```

```python
import functools

import jax
import jax.numpy as jnp
from jax import lax
from jax.experimental import pallas as pl
from jax.experimental.pallas import tpu as pltpu
from jax.sharding import PartitionSpec as P

K = 128
BLOCK = 128
UB = 16
IB = 8
TILES = 32
NNZ = 512
NZ = NX = 4
NY = 4
ROWS = 8
COLS = 16
ALL_TILES = COLS * TILES
LIST = 1024
LAST = 512
FAST = 36
STEP = 18
SUB = 32
UNROLL = 4
BUILD = 4
SLOTS = 2 * BUILD
GROUP = 4
HELD = 32
STAGE = 3 * TILES + 8
HALF = 56
SCALE = 40.0
RIDGE = 0.5
EPSILON = 1e-06
MESH = pl.DeviceIdType.MESH
F32 = jnp.float32
BF16 = jnp.bfloat16
NT = (((1,), (1,)), ((), ()))
NN = (((1,), (0,)), ((), ()))
ANY = pl.BlockSpec(memory_space=pl.ANY)
VMEM = pl.BlockSpec(memory_space=pltpu.VMEM)
SMEM = pl.BlockSpec(memory_space=pltpu.SMEM)
HBM = pl.BlockSpec(memory_space=pltpu.HBM)
BIG = 24 * 2**20
WHOLE = 40 * 2**20


def dot(a, b, dims):
    return lax.dot_general(a, b, dims, preferred_element_type=F32)


def split(a):
    high = a.astype(BF16)
    return high, (a - high.astype(F32)).astype(BF16)


def pair(a):
    return jnp.concatenate(split(a), axis=1)


def fold(wide):
    return wide[:, 0:128] + wide[:, 128:256]


def by_cols(high, low):
    both = jnp.concatenate([high, low], axis=1)
    return jnp.concatenate([both, both], axis=0)


def greet(peers):
    barrier = pltpu.get_barrier_semaphore()
    for peer in peers:
        pl.semaphore_signal(barrier, inc=1, device_id=peer, device_id_type=MESH)
    pl.semaphore_wait(barrier, len(peers))


class Copies:
    def __init__(self, send_sem, recv_sem):
        self.send_sem, self.recv_sem, self.made = send_sem, recv_sem, []

    def send(self, src, dst, peer):
        i = len(self.made)
        copy = pltpu.make_async_remote_copy(
            src_ref=src,
            dst_ref=dst,
            send_sem=self.send_sem.at[i],
            recv_sem=self.recv_sem.at[i],
            device_id=peer,
            device_id_type=MESH,
        )
        copy.start()
        self.made.append(copy)
        return copy

    def finish(self):
        for copy in self.made:
            copy.wait_send()


def col_place():
    c = lax.axis_index("col")
    z, x = c // NX, c % NX
    along_x = [{"col": z * NX + (x + d) % NX} for d in range(1, NX)]
    along_z = [{"col": ((z + d) % NZ) * NX + x} for d in range(1, NZ)]
    return c, z, x, along_x, along_z


def gather_kernel(
    items, fetch, user, slot, er, ec, en, count, yh, yl, th, tl, gram, ent, peak,
    stage, land, fetch_in, slot_in, user_in, small, keys, most, seen, send_sem, recv_sem, own_sem, in_sem,
):
    c, z, x, along_x, along_z = col_place()
    r = lax.axis_index("row")
    y, core = r // 2, r % 2
    right, left, across = (((y + d) % NY) * 2 + core for d in (1, 3, 2))
    other = y * 2 + 1 - core
    to_right, to_left, to_other = {"row": right}, {"row": left}, {"row": other}
    to_across = {"row": across}
    loads = [
        pltpu.make_async_copy(src, dst, in_sem.at[i])
        for i, (src, dst) in enumerate(
            (
                (er, stage.at[pl.ds(0, TILES)]),
                (ec, stage.at[pl.ds(TILES, TILES)]),
                (en, stage.at[pl.ds(2 * TILES, TILES)]),
                (items, land.at[r]),
                (fetch, fetch_in),
                (slot, slot_in),
                (user, user_in),
            )
        )
    ]
    for load in loads:
        load.start()
    greet(along_x + along_z + [to_right, to_left, to_across, to_other])
    copies = Copies(send_sem, recv_sem)
    send = copies.send
    half = [items.at[pl.ds(4 * i, 4)] for i in (0, 1)]
    there = [land.at[r, pl.ds(4 * i, 4)] for i in (0, 1)]
    from_left, from_right = [None, None], [None, None]
    for i in (0, 1):
        from_left[i] = send(half[i], there[i], to_right)
        from_right[1 - i] = send(half[1 - i], there[1 - i], to_left)
    between = [send(items, land.at[r], to_other)]

    for load in loads[4:]:
        load.wait()
    small[...] = jnp.zeros_like(small)
    small[0:1, 0:TILES] = slot_in[...]
    small[1:2, 0:TILES] = user_in[...]
    slots = small[0:1]
    table = jnp.broadcast_to(fetch_in[...].astype(F32), (128, 128)).T
    ids = lax.broadcasted_iota(jnp.int32, (128, 128), 0)
    local_id = jnp.sum(jnp.where(ids == slots, table, 0.0), axis=0, keepdims=True).astype(jnp.int32)
    lanes = lax.broadcasted_iota(jnp.int32, (1, 128), 1)
    last = 3 * TILES
    stage[last : last + 1, 0:128] = jnp.where(lanes < count[0, 0], slots & (COLS - 1), -1)
    stage[last + 1 : last + 2, 0:128] = ((slots >> 4) * IB + local_id) * UB + small[1:2]
    first_key = stage[last : last + 1, 0:128]
    keys[z, x] = jnp.broadcast_to(first_key, (8, 128))
    for load in loads[:3]:
        load.wait()
    own = pltpu.make_async_copy(stage, ent.at[z, x], own_sem)
    own.start()

    first, second = pl.ds(0, HALF), pl.ds(HALF, STAGE - HALF)
    parts = (pl.ds(0, 32), pl.ds(32, 24)), (pl.ds(56, 24), pl.ds(80, 24))
    ways = (
        (first, along_x, along_z, lambda d, e: ent.at[(z + e) % NZ, (x + d) % NX]),
        (second, along_z, along_x, lambda d, e: ent.at[(z + d) % NZ, (x + e) % NX]),
    )
    near = [[None] * 4, [None] * 4]
    up = [[None] * 4, [None] * 4]
    down = [[None] * 4, [None] * 4]

    def spread(w, d, source):
        rows, _, across_way, at = ways[w]
        to = at(-d, 0).at[rows]
        up[w][d] = send(source, to, across_way[0])
        down[w][d] = send(source, to, across_way[2])

    for w, (rows, along, _, at) in enumerate(ways):
        for d in (1, 3, 2):
            near[w][d] = send(stage.at[rows], at(0, 0).at[rows], along[d - 1])
        spread(w, 0, stage.at[rows])
    mine = keys.at[z, x]
    told_keys = [send(mine, mine, peer) for peer in along_x]

    far = []

    def pass_on(w, d):
        _, _, across_way, at = ways[w]
        up[w][d].wait_recv()
        piece = at(-d, -1).at[parts[w][0]]
        far.append(send(piece, piece, across_way[0]))
        down[w][d].wait_recv()
        piece = at(-d, 1).at[parts[w][1]]
        far.append(send(piece, piece, across_way[2]))

    def add(row, sums):
        def one(i, sums):
            high, low = split(land[row, i])
            high_t = high.T
            at = row * IB + i
            yh[at] = high
            yl[at] = low
            th[at] = high_t
            tl[at] = low.T
            return sums + dot(high_t, jnp.concatenate([high, low], axis=1), NN)

        return lax.fori_loop(0, IB, one, sums, unroll=4)

    loads[3].wait()
    sums = add(r, jnp.zeros((K, 2 * K), F32))
    for copy in told_keys:
        copy.wait_recv()
    mine = keys.at[z]
    told_keys = [send(mine, mine, peer) for peer in along_z]

    for d in (1, 3, 2):
        for w in (0, 1):
            near[w][d].wait_recv()
            rows, _, _, at = ways[w]
            spread(w, d, at(-d, 0).at[rows])
    for w in (0, 1):
        pass_on(w, 0)
    from_left[0].wait_recv()
    piece = land.at[left, pl.ds(0, 4)]
    round_y = [send(piece, piece, to_right)]
    from_right[1].wait_recv()
    piece = land.at[right, pl.ds(4, 4)]
    round_y.append(send(piece, piece, to_left))
    for copy in told_keys:
        copy.wait_recv()
    owners = keys[:, :, 0, :].reshape(COLS, 128)
    counted = [
        jnp.sum(jnp.where(owners == column, 1.0, 0.0), axis=0, keepdims=True)
        for column in range(COLS)
    ]
    counted = jnp.sum(jnp.concatenate(counted, axis=0), axis=1, keepdims=True)
    longest = jnp.max(counted, axis=0, keepdims=True).astype(jnp.int32)
    most[0] = jnp.broadcast_to(longest, (8, 128))

    told = [
        send(most.at[0], seen.at[i], peer)
        for i, peer in enumerate((to_right, to_left, to_across))
    ]
    between[0].wait_recv()
    sums = add(other, sums)
    for d in (1, 3):
        for w in (0, 1):
            pass_on(w, d)
    from_left[1].wait_recv()
    between.append(send(land.at[left], land.at[left], to_other))
    from_right[0].wait_recv()
    between.append(send(land.at[right], land.at[right], to_other))
    for w in (0, 1):
        pass_on(w, 2)
    for copy in told:
        copy.wait_recv()
    most[1] = jnp.maximum(jnp.maximum(most[0], seen[0]), jnp.maximum(seen[1], seen[2]))
    told = send(most.at[1], seen.at[3], to_other)
    sums = add(left, sums)
    sums = add(right, sums)
    for copy in round_y:
        copy.wait_recv()
    between.append(send(land.at[across], land.at[across], to_other))
    sums = add(across, sums)
    for copy, d in zip(between[1:], (3, 1, 2)):
        copy.wait_recv()
        sums = add(((y + d) % NY) * 2 + 1 - core, sums)
    told.wait_recv()
    peak[...] = jnp.maximum(most[1], seen[3])
    for copy in far:
        copy.wait_recv()
    own.wait()
    mixed = sums[:, K:]
    gram[...] = sums[:, :K] + (mixed + mixed.T)
    copies.finish()


def gather(items, fetch, user, slot, er, ec, en, count):
    n = 6 + 4 + 2 * (3 + 8 + 8) + 10
    return pl.pallas_call(
        gather_kernel,
        out_shape=(
            *[jax.ShapeDtypeStruct((ROWS * IB, BLOCK, K), BF16)] * 4,
            jax.ShapeDtypeStruct((K, K), F32),
            jax.ShapeDtypeStruct((NZ, NX, STAGE, NNZ), jnp.int32),
            jax.ShapeDtypeStruct((8, 128), jnp.int32),
        ),
        in_specs=[HBM] * 7 + [SMEM],
        out_specs=(VMEM, VMEM, VMEM, VMEM, VMEM, ANY, VMEM),
        scratch_shapes=[
            pltpu.VMEM((STAGE, NNZ), jnp.int32),
            pltpu.VMEM((ROWS, IB, BLOCK, K), F32),
            pltpu.VMEM((1, 128), jnp.int32),
            pltpu.VMEM((1, TILES), jnp.int32),
            pltpu.VMEM((1, TILES), jnp.int32),
            pltpu.VMEM((8, 128), jnp.int32),
            pltpu.VMEM((NZ, NX, 8, 128), jnp.int32),
            pltpu.VMEM((2, 8, 128), jnp.int32),
            pltpu.VMEM((4, 8, 128), jnp.int32),
            pltpu.SemaphoreType.DMA((n,)),
            pltpu.SemaphoreType.DMA((n,)),
            pltpu.SemaphoreType.DMA,
            pltpu.SemaphoreType.DMA((7,)),
        ],
        compiler_params=pltpu.CompilerParams(
            collective_id=0, has_side_effects=True, vmem_limit_bytes=BIG
        ),
        name="gather",
    )(*[pltpu.with_memory_space_constraint(a, pltpu.HBM) for a in (items, fetch, user, slot, er, ec, en)], count)


def build_kernel(
    ent, yh, yl, th, tl, gram, start, out, weights, order, meta, found, place, held, v, sem, meta_sem
):
    fetched = pltpu.make_async_copy(
        ent.at[:, pl.ds(3 * TILES, 8), pl.ds(0, 128)], meta, meta_sem
    )
    fetched.start()
    g = by_cols(*split(gram[...]))

    def begin(b, _):
        at = rows_of(b)
        both = pair(start[at])
        v[at] = both
        out[at] = -fold(dot(both, g, NN))
        return 0

    lax.fori_loop(0, UB, begin, 0, unroll=UNROLL)
    fetched.wait()
    me = lax.axis_index("col")

    def scan(c, n):
        for t in range(TILES):
            found[n] = (c * TILES + t) * (64 * UB) + meta[c, 1, t]
            n = n + jnp.where(meta[c, 0, t] == me, 1, 0)
        return n

    n = lax.fori_loop(0, COLS, scan, 0)
    order[LIST - 1] = n

    for b in range(UB):
        place[b] = 0

    def count(j, _):
        b = found[j] & (UB - 1)
        place[b] = place[b] + 1
        return 0

    lax.fori_loop(0, n, count, 0)
    total = 0
    for b in range(UB):
        of_b = place[b]
        order[LAST + b] = jnp.where(of_b > 0, total + of_b - 1, -1)
        place[b] = total
        total = total + of_b

    def put(j, _):
        code = found[j]
        b = code & (UB - 1)
        to = place[b]
        order[to] = code
        place[b] = to + 1
        return 0

    lax.fori_loop(0, n, put, 0)
    ids = lax.broadcasted_iota(jnp.int32, (BLOCK, NNZ), 0)
    one, none = jnp.ones((), BF16), jnp.zeros((), BF16)

    def out_copy(j):
        slot = j % SLOTS
        return pltpu.make_async_copy(held.at[slot], weights.at[j], sem.at[slot])

    def group(q, _):
        for u in range(BUILD):
            j = q * BUILD + u

            @pl.when((j >= SLOTS) & (j - SLOTS < n))
            def _(j=j):
                out_copy(j - SLOTS).wait()

        made = []
        for u in range(BUILD):
            j = q * BUILD + u
            code = jnp.where(j < n, order[j], 0)
            b, block, at = code % UB, (code // UB) % 64, code // (64 * UB)
            c, t = at // TILES, at % TILES
            rows = jnp.where(j < n, ent[c, pl.ds(t, 1), :], BLOCK)
            cols = ent[c, pl.ds(TILES + t, 1), :]
            counts = ent[c, pl.ds(2 * TILES + t, 1), :].astype(F32)
            in_col = ids == cols
            once = jnp.where(in_col, 1.0, 0.0).astype(BF16)
            ones = jnp.where(ids == rows, 1.0, 0.0).astype(BF16)
            many = jnp.where(in_col, counts, 0.0).astype(BF16)
            both = dot(ones, jnp.concatenate([once, many], axis=0), NT)
            times, excess = both[:, :BLOCK], SCALE * both[:, BLOCK:]
            made.append((rows_of(b), block, times, excess))
        scores = [
            fold(dot(v[where], by_cols(th[block], tl[block]), NN)) for where, block, _, _ in made
        ]
        pulls = [
            fold(
                dot(pair(times + excess * (1.0 - score)), by_cols(yh[block], yl[block]), NN)
            )
            for (_, block, times, excess), score in zip(made, scores)
        ]
        for u, ((where, _, _, excess), pull) in enumerate(zip(made, pulls)):
            held[(q * BUILD + u) % SLOTS] = excess
            out[where] += pull
        for u in range(BUILD):
            j = q * BUILD + u

            @pl.when(j < n)
            def _(j=j):
                out_copy(j).start()

        return 0

    groups = (n + BUILD - 1) // BUILD
    lax.fori_loop(0, groups, group, 0)

    def drain(j, _):
        out_copy(j).wait()
        return 0

    lax.fori_loop(jnp.maximum(groups * BUILD - SLOTS, 0), n, drain, 0)


def build(ent, yh, yl, th, tl, gram, start):
    return pl.pallas_call(
        build_kernel,
        out_shape=(
            jax.ShapeDtypeStruct((UB * BLOCK, K), F32),
            jax.ShapeDtypeStruct((ALL_TILES, BLOCK, BLOCK), F32),
            jax.ShapeDtypeStruct((LIST,), jnp.int32),
        ),
        in_specs=[VMEM] * 7,
        out_specs=(VMEM, ANY, SMEM),
        scratch_shapes=[
            pltpu.SMEM((COLS, 8, 128), jnp.int32),
            pltpu.SMEM((LIST,), jnp.int32),
            pltpu.SMEM((UB,), jnp.int32),
            pltpu.VMEM((SLOTS, BLOCK, BLOCK), F32),
            pltpu.VMEM((UB * BLOCK, 2 * K), BF16),
            pltpu.SemaphoreType.DMA((SLOTS,)),
            pltpu.SemaphoreType.DMA,
        ],
        compiler_params=pltpu.CompilerParams(vmem_limit_bytes=BIG),
        name="build",
    )(ent, yh, yl, th, tl, gram, start)


def fetch_tiles(order, weights, held, sem, base):
    here = jnp.minimum(order[LIST - 1] - base, HELD)

    def begin(i, _):
        pltpu.make_async_copy(weights.at[base + i], held.at[i], sem.at[i]).start()
        return 0

    lax.fori_loop(0, here, begin, 0)
    return here


def each_tile(order, weights, held, sem, work):
    n = order[LIST - 1]

    def batch(k, _):
        base = k * HELD
        here = jnp.minimum(n - base, HELD)

        def group(q, _):
            for u in range(GROUP):
                i = q * GROUP + u

                @pl.when(i < here)
                def _(i=i):
                    pltpu.make_async_copy(weights.at[base + i], held.at[i], sem.at[i]).wait()

            for u in range(GROUP):
                i = q * GROUP + u
                live = i < here
                code = jnp.where(live, order[base + i], 0)
                w = jnp.where(live, held[i], 0.0)
                work(code % UB, (code // UB) % 64, w)
            return 0

        lax.fori_loop(0, (here + GROUP - 1) // GROUP, group, 0)

        @pl.when(n > base + HELD)
        def _():
            fetch_tiles(order, weights, held, sem, base + HELD)

        return 0

    lax.fori_loop(0, (n + HELD - 1) // HELD, batch, 0)


def rows_of(b):
    return pl.ds(pl.multiple_of(b * BLOCK, BLOCK), BLOCK)


def dots(a, b):
    return jnp.sum(a * b, axis=1, keepdims=True)


def pull_tiles(order, weights, held, sem, yh, yl, th, tl, v, out):
    def work(b, block, w):
        at = rows_of(b)
        scores = fold(dot(v[at], by_cols(th[block], tl[block]), NN))
        out[at] += fold(dot(pair(w * scores), by_cols(yh[block], yl[block]), NN))

    each_tile(order, weights, held, sem, work)


def first_kernel(order, total, start, yh, yl, th, tl, gram, weights, out, residual, v, held, sem):
    fetch_tiles(order, weights, held, sem, 0)
    g = by_cols(*split(gram[...]))

    def begin(b, _):
        at = rows_of(b)
        p = total[at] - RIDGE * start[at]
        residual[at] = p
        both = pair(p)
        v[at] = both
        out[at] = fold(dot(both, g, NN))
        return 0

    lax.fori_loop(0, UB, begin, 0, unroll=UNROLL)
    pull_tiles(order, weights, held, sem, yh, yl, th, tl, v, out)


def update(total, iterate, residual, direction):
    image = total + RIDGE * direction
    now = dots(residual, residual)
    alpha = now / (dots(direction, image) + EPSILON)
    iterate = iterate + alpha * direction
    residual = residual - alpha * image
    after = dots(residual, residual)
    direction = residual + after / (now + EPSILON) * direction
    return iterate, residual, direction


def second_kernel(
    order, total, iterate, residual, yh, yl, th, tl, gram, weights, out, new_x, new_r, new_p, v, held, sem
):
    fetch_tiles(order, weights, held, sem, 0)
    g = by_cols(*split(gram[...]))

    def begin(b, _):
        at = rows_of(b)
        r = residual[at]
        new_x[at], new_r[at], p = update(total[at], iterate[at], r, r)
        new_p[at] = p
        both = pair(p)
        v[at] = both
        out[at] = fold(dot(both, g, NN))
        return 0

    lax.fori_loop(0, UB, begin, 0, unroll=UNROLL)
    pull_tiles(order, weights, held, sem, yh, yl, th, tl, v, out)


def third_kernel(
    order, total, iterate, residual, direction, yh, yl, th, tl, gram, weights,
    squares, new_x, new_r, new_p, v, acc, held, sem,
):
    fetch_tiles(order, weights, held, sem, 0)
    g = by_cols(*split(gram[...]))

    def begin(b, _):
        at = rows_of(b)
        new_x[at], new_r[at], p = update(total[at], iterate[at], residual[at], direction[at])
        new_p[at] = p
        both = pair(p)
        v[at] = both
        acc[at] = p * fold(dot(both, g, NN))
        return 0

    lax.fori_loop(0, UB, begin, 0, unroll=UNROLL)

    def work(b, block, w):
        at = rows_of(b)
        scores = fold(dot(v[at], by_cols(th[block], tl[block]), NN))
        acc[at] += w * scores * scores

    each_tile(order, weights, held, sem, work)
    for b in range(UB):
        squares[b : b + 1] = jnp.sum(acc[b * BLOCK : (b + 1) * BLOCK].T, axis=0, keepdims=True)


def last_kernel(squares, iterate, residual, direction, out):
    sums = squares[...]
    for b in range(UB):
        at = pl.ds(b * BLOCK, BLOCK)
        p = direction[at]
        r = residual[at]
        below = jnp.broadcast_to(sums[b : b + 1], (BLOCK, BLOCK)).T + RIDGE * dots(p, p)
        out[at] = iterate[at] + dots(r, r) / (below + EPSILON) * p


USERS = jax.ShapeDtypeStruct((UB * BLOCK, K), F32)


def local(kernel, name, outs, specs, scratch=()):
    tiles = [
        pltpu.VMEM((UB * BLOCK, 2 * K), BF16),
        *scratch,
        pltpu.VMEM((HELD, BLOCK, BLOCK), F32),
        pltpu.SemaphoreType.DMA((HELD,)),
    ]
    return pl.pallas_call(
        kernel,
        out_shape=outs,
        in_specs=specs,
        out_specs=tuple(VMEM for _ in outs),
        scratch_shapes=tiles,
        compiler_params=pltpu.CompilerParams(vmem_limit_bytes=BIG),
        name=name,
    )


def reduce_kernel(part, out, land, sums, near, send_sem, recv_sem):
    c, z, x, along_x, along_z = col_place()
    greet(along_x + along_z)
    copies = Copies(send_sem, recv_sem)
    send = copies.send
    streams = [(pl.ds(SUB * i, SUB), i % 2 == 0) for i in range(BLOCK // SUB)]

    def line(ref, way, d, rows):
        return ref.at[:, (x + d) % NX, rows] if way else ref.at[(z + d) % NZ, :, rows]

    def axes(way):
        return (along_x, along_z, z) if way else (along_z, along_x, x)

    far = [
        [send(line(part, way, d, rows), land.at[i, d - 1], axes(way)[0][d - 1]) for d in (1, 2, 3)]
        for i, (rows, way) in enumerate(streams)
    ]
    close = []
    for i, (rows, way) in enumerate(streams):
        _, along, me = axes(way)
        for copy in far[i]:
            copy.wait_recv()
        mine = part[:, x, rows] if way else part[z, :, rows]
        sums[i] = mine + land[i, 0] + (land[i, 1] + land[i, 2])
        close.append(
            [send(sums.at[i, (me + d) % 4], near.at[i, d - 1], along[d - 1]) for d in (1, 2, 3)]
        )
    back = []
    for i, (rows, way) in enumerate(streams):
        _, along, me = axes(way)
        for copy in close[i]:
            copy.wait_recv()
        out[z, x, rows] = sums[i, me] + near[i, 0] + (near[i, 1] + near[i, 2])
        here = out.at[z, x, rows]
        back.append([send(here, here, peer) for peer in along])
    end = []
    for i, (rows, way) in enumerate(streams):
        for copy in back[i]:
            copy.wait_recv()
        here = line(out, way, 0, rows)
        end += [send(here, here, peer) for peer in axes(way)[0]]
    for copy in end:
        copy.wait_recv()
    copies.finish()


def reduce(part):
    n = BLOCK // SUB
    out = pl.pallas_call(
        reduce_kernel,
        out_shape=jax.ShapeDtypeStruct((NZ, NX, BLOCK, K), F32),
        in_specs=[VMEM],
        out_specs=VMEM,
        scratch_shapes=[
            pltpu.VMEM((n, 3, 4, SUB, K), F32),
            pltpu.VMEM((n, 4, SUB, K), F32),
            pltpu.VMEM((n, 3, SUB, K), F32),
            pltpu.SemaphoreType.DMA((12 * n,)),
            pltpu.SemaphoreType.DMA((12 * n,)),
        ],
        compiler_params=pltpu.CompilerParams(
            collective_id=1, has_side_effects=True, vmem_limit_bytes=BIG
        ),
        name="reduce",
    )(part.reshape(NZ, NX, BLOCK, K))
    return out.reshape(UB * BLOCK, K)


def scalars_kernel(mine, out, land_x, land_z, half, send_sem, recv_sem):
    _, _, _, along_x, along_z = col_place()
    greet(along_x + along_z)
    copies = Copies(send_sem, recv_sem)
    for copy in [copies.send(mine, land_x.at[i], peer) for i, peer in enumerate(along_x)]:
        copy.wait_recv()
    half[...] = mine[...] + land_x[0] + (land_x[1] + land_x[2])
    for copy in [copies.send(half, land_z.at[i], peer) for i, peer in enumerate(along_z)]:
        copy.wait_recv()
    out[...] = half[...] + land_z[0] + (land_z[1] + land_z[2])
    copies.finish()


def sum_scalars(mine):
    return pl.pallas_call(
        scalars_kernel,
        out_shape=jax.ShapeDtypeStruct((UB, BLOCK), F32),
        in_specs=[VMEM],
        out_specs=VMEM,
        scratch_shapes=[
            pltpu.VMEM((3, UB, BLOCK), F32),
            pltpu.VMEM((3, UB, BLOCK), F32),
            pltpu.VMEM((UB, BLOCK), F32),
            pltpu.SemaphoreType.DMA((6,)),
            pltpu.SemaphoreType.DMA((6,)),
        ],
        compiler_params=pltpu.CompilerParams(collective_id=2, has_side_effects=True, vmem_limit_bytes=BIG),
        name="scalars",
    )(mine)


def cg_kernel(
    order, part, start, yh, yl, th, tl, gram, weights, out,
    held, v, x_now, r_now, p_now, pulls, squares, parts, tot, land, sums, near,
    row_sums, land_x, land_z, half, send_sem, recv_sem, w_sem,
):
    _, z, x, along_x, along_z = col_place()
    load = pltpu.make_async_copy(weights.at[pl.ds(0, FAST)], held, w_sem)
    load.start()
    greet(along_x + along_z)
    copies = Copies(send_sem, recv_sem)
    send = copies.send
    far, close, back, end = {}, {}, {}, {}
    rounds = (part, parts.at[0], parts.at[1])

    def streams(s):
        for i in (2 * s, 2 * s + 1):
            way = i % 2 == 0
            first, second, me = (along_x, along_z, z) if way else (along_z, along_x, x)
            yield i, pl.ds(SUB * i, SUB), way, first, second, me

    def line(ref, way, d, rows):
        return ref.at[:, (x + d) % NX, rows] if way else ref.at[(z + d) % NZ, :, rows]

    def begin(k, s):
        for i, rows, way, first, _, _ in streams(s):
            far[k, i] = [
                send(line(rounds[k], way, d, rows), land.at[k, i, d - 1], first[d - 1])
                for d in (2, 1, 3)
            ]

    def sum_first(k, s):
        for i, rows, way, _, second, me in streams(s):
            for copy in far[k, i]:
                copy.wait_recv()
            mine = rounds[k][:, x, rows] if way else rounds[k][z, :, rows]
            sums[k, i] = mine + land[k, i, 0] + (land[k, i, 1] + land[k, i, 2])
            close[k, i] = [
                send(sums.at[k, i, (me + d) % 4], near.at[k, i, d - 1], second[d - 1])
                for d in (2, 1, 3)
            ]

    def sum_second(k, s):
        for i, rows, _, _, second, me in streams(s):
            for copy in close[k, i]:
                copy.wait_recv()
            tot[k, z, x, rows] = sums[k, i, me] + near[k, i, 0] + (near[k, i, 1] + near[k, i, 2])
            here = tot.at[k, z, x, rows]
            back[k, i] = [send(here, here, second[d]) for d in (1, 0, 2)]

    def spread(k, s):
        for i, rows, way, first, _, _ in streams(s):
            for copy in back[k, i]:
                copy.wait_recv()
            here = line(tot.at[k], way, 0, rows)
            end[k, i] = [send(here, here, first[d]) for d in (1, 0, 2)]

    def arrive(k, s):
        for i in (2 * s, 2 * s + 1):
            for copy in end[k, i]:
                copy.wait_recv()

    g = by_cols(*split(gram[...]))
    n = order[LIST - 1]

    def compute(k, s, before_end):
        rows = pl.ds(64 * s, 64)

        def step(b, _):
            total = tot[k - 1, b // NX, b % NX, rows]
            if k == 1:
                p = total - RIDGE * start[b, rows]
                r_now[b, rows] = p
            else:
                before = start[b, rows] if k == 2 else x_now[b, rows]
                r = r_now[b, rows]
                old = r if k == 2 else p_now[b, rows]
                x_now[b, rows], r_now[b, rows], p = update(total, before, r, old)
            p_now[b, rows] = p
            v[b, rows] = pair(p)
            return 0

        lax.fori_loop(0, UB, step, 0, unroll=16)

        def some(q, acc):
            last_b, acc = acc
            for u in range(STEP):
                j = q * STEP + u
                code = order[j]
                b, block = code & (UB - 1), (code >> 4) & 63
                w = jnp.where(j < n, held[j, rows], 0.0)
                scores = fold(dot(v[b, rows], by_cols(th[block], tl[block]), NN))
                if k < 3:
                    pull = fold(dot(pair(w * scores), by_cols(yh[block], yl[block]), NN))
                else:
                    pull = w * scores * scores
                acc = jnp.where(b == last_b, acc, 0.0) + pull
                last_b = b
                pulls[s, j] = acc
            return last_b, acc

        lax.fori_loop(0, FAST // STEP, some, (jnp.int32(-1), jnp.zeros((64, K), F32)))
        before_end()

        def close_up(b, _):
            end_of = order[LAST + b]
            pulled = jnp.where(end_of >= 0, pulls[s, jnp.maximum(end_of, 0)], 0.0)
            whole = fold(dot(v[b, rows], g, NN))
            if k < 3:
                parts[k - 1, b // NX, b % NX, rows] = whole + pulled
            else:
                squares[b, rows] = p_now[b, rows] * whole + pulled
            return 0

        lax.fori_loop(0, UB, close_up, 0, unroll=16)
        if k == 3:
            for b in range(UB):
                row_sums[b : b + 1, 64 * s : 64 * s + 64] = jnp.sum(
                    squares[b, rows].T, axis=0, keepdims=True
                )

    def nothing():
        pass

    begin(0, 0)
    begin(0, 1)
    sum_first(0, 0)
    for k in range(3):
        sum_first(k, 1)
        for work in (sum_second, spread):
            work(k, 0)
            work(k, 1)
        if k == 0:
            load.wait()
        arrive(k, 0)
        compute(k + 1, 0, nothing)
        if k < 2:
            begin(k + 1, 0)
        arrive(k, 1)
        compute(k + 1, 1, functools.partial(sum_first, k + 1, 0) if k < 2 else nothing)
        if k < 2:
            begin(k + 1, 1)

    told = [send(row_sums, land_x.at[i], peer) for i, peer in enumerate(along_x)]
    for b in range(UB):
        p, r = p_now[b], r_now[b]
        rest = jnp.broadcast_to(RIDGE * dots(p, p) + EPSILON, (BLOCK, K))
        pulls[0, b] = rest[:64]
        pulls[1, b] = rest[64:]
        squares[b] = jnp.broadcast_to(dots(r, r), (BLOCK, K))
    for copy in told:
        copy.wait_recv()
    half[...] = row_sums[...] + land_x[0] + (land_x[1] + land_x[2])
    for copy in [send(half, land_z.at[i], peer) for i, peer in enumerate(along_z)]:
        copy.wait_recv()
    both = half[...] + land_z[0] + (land_z[1] + land_z[2])
    for b in range(UB):
        below = jnp.broadcast_to(both[b : b + 1], (BLOCK, BLOCK)).T
        rest = jnp.concatenate([pulls[0, b], pulls[1, b]], axis=0)
        out[b] = x_now[b] + squares[b] / (below + rest) * p_now[b]
    copies.finish()


def all_steps(order, part, start, yh, yl, th, tl, gram, weights):
    n = BLOCK // SUB
    copies = 3 * 12 * n + 6
    blocks = (UB, BLOCK, K)
    out = pl.pallas_call(
        cg_kernel,
        out_shape=jax.ShapeDtypeStruct(blocks, F32),
        in_specs=[SMEM] + [VMEM] * 7 + [ANY],
        out_specs=VMEM,
        scratch_shapes=[
            pltpu.VMEM((FAST, BLOCK, BLOCK), F32),
            pltpu.VMEM((UB, BLOCK, 2 * K), BF16),
            pltpu.VMEM(blocks, F32),
            pltpu.VMEM(blocks, F32),
            pltpu.VMEM(blocks, F32),
            pltpu.VMEM((2, FAST, 64, K), F32),
            pltpu.VMEM(blocks, F32),
            pltpu.VMEM((2, NZ, NX, BLOCK, K), F32),
            pltpu.VMEM((3, NZ, NX, BLOCK, K), F32),
            pltpu.VMEM((3, n, 3, 4, SUB, K), F32),
            pltpu.VMEM((3, n, 4, SUB, K), F32),
            pltpu.VMEM((3, n, 3, SUB, K), F32),
            pltpu.VMEM((UB, BLOCK), F32),
            pltpu.VMEM((3, UB, BLOCK), F32),
            pltpu.VMEM((3, UB, BLOCK), F32),
            pltpu.VMEM((UB, BLOCK), F32),
            pltpu.SemaphoreType.DMA((copies,)),
            pltpu.SemaphoreType.DMA((copies,)),
            pltpu.SemaphoreType.DMA,
        ],
        compiler_params=pltpu.CompilerParams(
            collective_id=3, has_side_effects=True, vmem_limit_bytes=WHOLE
        ),
        name="steps",
    )(order, part.reshape(NZ, NX, BLOCK, K), start.reshape(blocks), yh, yl, th, tl, gram, weights)
    return out.reshape(UB * BLOCK, K)


def step_by_step(order, part, start, yh, yl, th, tl, gram, weights):
    total = reduce(part)
    tail = [VMEM] * 5 + [ANY]
    part, residual = local(first_kernel, "first", (USERS,) * 2, [SMEM, VMEM, VMEM] + tail)(
        order, total, start, yh, yl, th, tl, gram, weights
    )
    total = reduce(part)
    part, iterate, residual, direction = local(
        second_kernel, "second", (USERS,) * 4, [SMEM] + [VMEM] * 3 + tail
    )(order, total, start, residual, yh, yl, th, tl, gram, weights)
    total = reduce(part)
    squares = jax.ShapeDtypeStruct((UB, BLOCK), F32)
    part, iterate, residual, direction = local(
        third_kernel,
        "third",
        (squares,) + (USERS,) * 3,
        [SMEM] + [VMEM] * 4 + tail,
        [pltpu.VMEM((UB * BLOCK, K), F32)],
    )(order, total, iterate, residual, direction, yh, yl, th, tl, gram, weights)
    squares = sum_scalars(part)
    return pl.pallas_call(
        last_kernel,
        out_shape=USERS,
        in_specs=[VMEM] * 4,
        out_specs=VMEM,
        compiler_params=pltpu.CompilerParams(vmem_limit_bytes=BIG),
        name="last",
    )(squares, iterate, residual, direction)


def shards(user_factors, item_factors, fetch_list, tile_user, tile_slot, er, ec, en, tile_count):
    yh, yl, th, tl, gram, ent, peak = gather(
        item_factors.reshape(IB, BLOCK, K),
        fetch_list.reshape(1, 128),
        tile_user.reshape(1, TILES),
        tile_slot.reshape(1, TILES),
        er.reshape(TILES, NNZ),
        ec.reshape(TILES, NNZ),
        en.reshape(TILES, NNZ),
        tile_count.reshape(1, 1),
    )
    part, weights, order = build(
        ent.reshape(COLS, STAGE, NNZ), yh, yl, th, tl, gram, user_factors
    )
    return lax.cond(
        peak[0, 0] <= FAST,
        all_steps,
        step_by_step,
        order, part, user_factors, yh, yl, th, tl, gram, weights,
    )


def solution(mesh):
    return jax.shard_map(
        shards,
        mesh=mesh,
        in_specs=(
            P("row", None),
            P(("row", "col"), None),
            P("row", "col", None, None),
            P("row", "col", None),
            P("row", "col", None),
            P("row", "col", None, None),
            P("row", "col", None, None),
            P("row", "col", None, None),
            P("row", "col"),
        ),
        out_specs=P("row", None),
        check_vma=False,
    )
```

```python
import functools

import jax
import jax.numpy as jnp
from jax import lax
from jax.experimental import pallas as pl
from jax.experimental.pallas import tpu as pltpu
from jax.sharding import PartitionSpec as P

K = 128
BLOCK = 128
UB = 16
IB = 8
TILES = 32
NNZ = 512
NZ = NX = 4
NY = 4
ROWS = 8
COLS = 16
ALL_TILES = COLS * TILES
LIST = 1024
LAST = 512
FAST = 36
STEP = 18
SUB = 32
THIN = 16
UNROLL = 4
BUILD = 4
SLOTS = 2 * BUILD
GROUP = 4
HELD = 32
STAGE = 3 * TILES + 8
HALF = 56
SCALE = 40.0
RIDGE = 0.5
EPSILON = 1e-06
MESH = pl.DeviceIdType.MESH
F32 = jnp.float32
BF16 = jnp.bfloat16
NT = (((1,), (1,)), ((), ()))
NN = (((1,), (0,)), ((), ()))
ANY = pl.BlockSpec(memory_space=pl.ANY)
VMEM = pl.BlockSpec(memory_space=pltpu.VMEM)
SMEM = pl.BlockSpec(memory_space=pltpu.SMEM)
HBM = pl.BlockSpec(memory_space=pltpu.HBM)
BIG = 24 * 2**20
WHOLE = 40 * 2**20


def dot(a, b, dims):
    return lax.dot_general(a, b, dims, preferred_element_type=F32)


def split(a):
    high = a.astype(BF16)
    return high, (a - high.astype(F32)).astype(BF16)


def pair(a):
    return jnp.concatenate(split(a), axis=1)


def fold(wide):
    return wide[:, 0:128] + wide[:, 128:256]


def by_cols(high, low):
    both = jnp.concatenate([high, low], axis=1)
    return jnp.concatenate([both, both], axis=0)


def greet(peers):
    barrier = pltpu.get_barrier_semaphore()
    for peer in peers:
        pl.semaphore_signal(barrier, inc=1, device_id=peer, device_id_type=MESH)
    pl.semaphore_wait(barrier, len(peers))


class Copies:
    def __init__(self, send_sem, recv_sem):
        self.send_sem, self.recv_sem, self.made = send_sem, recv_sem, []

    def send(self, src, dst, peer):
        i = len(self.made)
        copy = pltpu.make_async_remote_copy(
            src_ref=src,
            dst_ref=dst,
            send_sem=self.send_sem.at[i],
            recv_sem=self.recv_sem.at[i],
            device_id=peer,
            device_id_type=MESH,
        )
        copy.start()
        self.made.append(copy)
        return copy

    def finish(self):
        for copy in self.made:
            copy.wait_send()


def col_place():
    c = lax.axis_index("col")
    z, x = c // NX, c % NX
    along_x = [{"col": z * NX + (x + d) % NX} for d in range(1, NX)]
    along_z = [{"col": ((z + d) % NZ) * NX + x} for d in range(1, NZ)]
    return c, z, x, along_x, along_z


def gather_kernel(
    items, fetch, user, slot, er, ec, en, count, yh, yl, th, tl, gram, ent, peak,
    stage, land, fetch_in, slot_in, user_in, small, keys, most, seen, send_sem, recv_sem, own_sem, in_sem,
):
    c, z, x, along_x, along_z = col_place()
    r = lax.axis_index("row")
    y, core = r // 2, r % 2
    right, left, across = (((y + d) % NY) * 2 + core for d in (1, 3, 2))
    other = y * 2 + 1 - core
    to_right, to_left, to_other = {"row": right}, {"row": left}, {"row": other}
    to_across = {"row": across}
    loads = [
        pltpu.make_async_copy(src, dst, in_sem.at[i])
        for i, (src, dst) in enumerate(
            (
                (er, stage.at[pl.ds(0, TILES)]),
                (ec, stage.at[pl.ds(TILES, TILES)]),
                (en, stage.at[pl.ds(2 * TILES, TILES)]),
                (items, land.at[r]),
                (fetch, fetch_in),
                (slot, slot_in),
                (user, user_in),
            )
        )
    ]
    for load in loads:
        load.start()
    greet(along_x + along_z + [to_right, to_left, to_across, to_other])
    copies = Copies(send_sem, recv_sem)
    send = copies.send
    half = [items.at[pl.ds(4 * i, 4)] for i in (0, 1)]
    there = [land.at[r, pl.ds(4 * i, 4)] for i in (0, 1)]
    from_left, from_right = [None, None], [None, None]
    for i in (0, 1):
        from_left[i] = send(half[i], there[i], to_right)
        from_right[1 - i] = send(half[1 - i], there[1 - i], to_left)
    between = [send(items, land.at[r], to_other)]

    for load in loads[4:]:
        load.wait()
    small[...] = jnp.zeros_like(small)
    small[0:1, 0:TILES] = slot_in[...]
    small[1:2, 0:TILES] = user_in[...]
    slots = small[0:1]
    table = jnp.broadcast_to(fetch_in[...].astype(F32), (128, 128)).T
    ids = lax.broadcasted_iota(jnp.int32, (128, 128), 0)
    local_id = jnp.sum(jnp.where(ids == slots, table, 0.0), axis=0, keepdims=True).astype(jnp.int32)
    lanes = lax.broadcasted_iota(jnp.int32, (1, 128), 1)
    last = 3 * TILES
    stage[last : last + 1, 0:128] = jnp.where(lanes < count[0, 0], slots & (COLS - 1), -1)
    stage[last + 1 : last + 2, 0:128] = ((slots >> 4) * IB + local_id) * UB + small[1:2]
    first_key = stage[last : last + 1, 0:128]
    keys[z, x] = jnp.broadcast_to(first_key, (8, 128))
    for load in loads[:3]:
        load.wait()
    own = pltpu.make_async_copy(stage, ent.at[z, x], own_sem)
    own.start()

    first, second = pl.ds(0, HALF), pl.ds(HALF, STAGE - HALF)
    parts = (pl.ds(0, 32), pl.ds(32, 24)), (pl.ds(56, 24), pl.ds(80, 24))
    ways = (
        (first, along_x, along_z, lambda d, e: ent.at[(z + e) % NZ, (x + d) % NX]),
        (second, along_z, along_x, lambda d, e: ent.at[(z + d) % NZ, (x + e) % NX]),
    )
    near = [[None] * 4, [None] * 4]
    up = [[None] * 4, [None] * 4]
    down = [[None] * 4, [None] * 4]

    def spread(w, d, source):
        rows, _, across_way, at = ways[w]
        to = at(-d, 0).at[rows]
        up[w][d] = send(source, to, across_way[0])
        down[w][d] = send(source, to, across_way[2])

    for w, (rows, along, _, at) in enumerate(ways):
        for d in (1, 3, 2):
            near[w][d] = send(stage.at[rows], at(0, 0).at[rows], along[d - 1])
        spread(w, 0, stage.at[rows])
    mine = keys.at[z, x]
    told_keys = [send(mine, mine, peer) for peer in along_x]

    far = []

    def pass_on(w, d):
        _, _, across_way, at = ways[w]
        up[w][d].wait_recv()
        piece = at(-d, -1).at[parts[w][0]]
        far.append(send(piece, piece, across_way[0]))
        down[w][d].wait_recv()
        piece = at(-d, 1).at[parts[w][1]]
        far.append(send(piece, piece, across_way[2]))

    def add(row, sums):
        def one(i, sums):
            high, low = split(land[row, i])
            high_t = high.T
            at = row * IB + i
            yh[at] = high
            yl[at] = low
            th[at] = high_t
            tl[at] = low.T
            return sums + dot(high_t, jnp.concatenate([high, low], axis=1), NN)

        return lax.fori_loop(0, IB, one, sums, unroll=4)

    loads[3].wait()
    sums = add(r, jnp.zeros((K, 2 * K), F32))
    for copy in told_keys:
        copy.wait_recv()
    mine = keys.at[z]
    told_keys = [send(mine, mine, peer) for peer in along_z]

    for d in (1, 3, 2):
        for w in (0, 1):
            near[w][d].wait_recv()
            rows, _, _, at = ways[w]
            spread(w, d, at(-d, 0).at[rows])
    for w in (0, 1):
        pass_on(w, 0)
    from_left[0].wait_recv()
    piece = land.at[left, pl.ds(0, 4)]
    round_y = [send(piece, piece, to_right)]
    from_right[1].wait_recv()
    piece = land.at[right, pl.ds(4, 4)]
    round_y.append(send(piece, piece, to_left))
    for copy in told_keys:
        copy.wait_recv()
    owners = keys[:, :, 0, :].reshape(COLS, 128)
    counted = [
        jnp.sum(jnp.where(owners == column, 1.0, 0.0), axis=0, keepdims=True)
        for column in range(COLS)
    ]
    counted = jnp.sum(jnp.concatenate(counted, axis=0), axis=1, keepdims=True)
    longest = jnp.max(counted, axis=0, keepdims=True).astype(jnp.int32)
    most[0] = jnp.broadcast_to(longest, (8, 128))

    told = [
        send(most.at[0], seen.at[i], peer)
        for i, peer in enumerate((to_right, to_left, to_across))
    ]
    between[0].wait_recv()
    sums = add(other, sums)
    for d in (1, 3):
        for w in (0, 1):
            pass_on(w, d)
    from_left[1].wait_recv()
    between.append(send(land.at[left], land.at[left], to_other))
    from_right[0].wait_recv()
    between.append(send(land.at[right], land.at[right], to_other))
    for w in (0, 1):
        pass_on(w, 2)
    for copy in told:
        copy.wait_recv()
    most[1] = jnp.maximum(jnp.maximum(most[0], seen[0]), jnp.maximum(seen[1], seen[2]))
    told = send(most.at[1], seen.at[3], to_other)
    sums = add(left, sums)
    sums = add(right, sums)
    for copy in round_y:
        copy.wait_recv()
    between.append(send(land.at[across], land.at[across], to_other))
    sums = add(across, sums)
    for copy, d in zip(between[1:], (3, 1, 2)):
        copy.wait_recv()
        sums = add(((y + d) % NY) * 2 + 1 - core, sums)
    told.wait_recv()
    peak[...] = jnp.maximum(most[1], seen[3])
    for copy in far:
        copy.wait_recv()
    own.wait()
    mixed = sums[:, K:]
    gram[...] = sums[:, :K] + (mixed + mixed.T)
    copies.finish()


def gather(items, fetch, user, slot, er, ec, en, count):
    n = 6 + 4 + 2 * (3 + 8 + 8) + 10
    return pl.pallas_call(
        gather_kernel,
        out_shape=(
            *[jax.ShapeDtypeStruct((ROWS * IB, BLOCK, K), BF16)] * 4,
            jax.ShapeDtypeStruct((K, K), F32),
            jax.ShapeDtypeStruct((NZ, NX, STAGE, NNZ), jnp.int32),
            jax.ShapeDtypeStruct((8, 128), jnp.int32),
        ),
        in_specs=[HBM] * 7 + [SMEM],
        out_specs=(VMEM, VMEM, VMEM, VMEM, VMEM, ANY, VMEM),
        scratch_shapes=[
            pltpu.VMEM((STAGE, NNZ), jnp.int32),
            pltpu.VMEM((ROWS, IB, BLOCK, K), F32),
            pltpu.VMEM((1, 128), jnp.int32),
            pltpu.VMEM((1, TILES), jnp.int32),
            pltpu.VMEM((1, TILES), jnp.int32),
            pltpu.VMEM((8, 128), jnp.int32),
            pltpu.VMEM((NZ, NX, 8, 128), jnp.int32),
            pltpu.VMEM((2, 8, 128), jnp.int32),
            pltpu.VMEM((4, 8, 128), jnp.int32),
            pltpu.SemaphoreType.DMA((n,)),
            pltpu.SemaphoreType.DMA((n,)),
            pltpu.SemaphoreType.DMA,
            pltpu.SemaphoreType.DMA((7,)),
        ],
        compiler_params=pltpu.CompilerParams(
            collective_id=0, has_side_effects=True, vmem_limit_bytes=BIG
        ),
        name="gather",
    )(*[pltpu.with_memory_space_constraint(a, pltpu.HBM) for a in (items, fetch, user, slot, er, ec, en)], count)


def build_kernel(
    ent, yh, yl, th, tl, gram, start, peak, out, weights, order, fits, meta, found, place, held, v, sem, meta_sem
):
    fetched = pltpu.make_async_copy(
        ent.at[:, pl.ds(3 * TILES, 8), pl.ds(0, 128)], meta, meta_sem
    )
    fetched.start()
    g = by_cols(*split(gram[...]))

    def begin(b, _):
        at = rows_of(b)
        both = pair(start[at])
        v[at] = both
        out[at] = -fold(dot(both, g, NN))
        return 0

    lax.fori_loop(0, UB, begin, 0, unroll=UNROLL)
    fits[0] = jnp.where(jnp.max(peak[...].astype(F32)) <= FAST, 1, 0)
    fetched.wait()
    me = lax.axis_index("col")

    def scan(c, n):
        for t in range(TILES):
            found[n] = (c * TILES + t) * (64 * UB) + meta[c, 1, t]
            n = n + jnp.where(meta[c, 0, t] == me, 1, 0)
        return n

    n = lax.fori_loop(0, COLS, scan, 0)
    order[LIST - 1] = n

    for b in range(UB):
        place[b] = 0

    def count(j, _):
        b = found[j] & (UB - 1)
        place[b] = place[b] + 1
        return 0

    lax.fori_loop(0, n, count, 0)
    total = 0
    for b in range(UB):
        of_b = place[b]
        order[LAST + b] = jnp.where(of_b > 0, total + of_b - 1, -1)
        place[b] = total
        total = total + of_b

    def put(j, _):
        code = found[j]
        b = code & (UB - 1)
        to = place[b]
        order[to] = code
        place[b] = to + 1
        return 0

    lax.fori_loop(0, n, put, 0)
    ids = lax.broadcasted_iota(jnp.int32, (BLOCK, NNZ), 0)
    one, none = jnp.ones((), BF16), jnp.zeros((), BF16)

    def out_copy(j):
        slot = j % SLOTS
        return pltpu.make_async_copy(held.at[slot], weights.at[j], sem.at[slot])

    def group(q, _):
        for u in range(BUILD):
            j = q * BUILD + u

            @pl.when((j >= SLOTS) & (j - SLOTS < n))
            def _(j=j):
                out_copy(j - SLOTS).wait()

        made = []
        for u in range(BUILD):
            j = q * BUILD + u
            code = jnp.where(j < n, order[j], 0)
            b, block, at = code % UB, (code // UB) % 64, code // (64 * UB)
            c, t = at // TILES, at % TILES
            rows = jnp.where(j < n, ent[c, pl.ds(t, 1), :], BLOCK)
            cols = ent[c, pl.ds(TILES + t, 1), :]
            counts = ent[c, pl.ds(2 * TILES + t, 1), :].astype(F32)
            in_col = ids == cols
            once = jnp.where(in_col, 1.0, 0.0).astype(BF16)
            ones = jnp.where(ids == rows, 1.0, 0.0).astype(BF16)
            many = jnp.where(in_col, counts, 0.0).astype(BF16)
            both = dot(ones, jnp.concatenate([once, many], axis=0), NT)
            times, excess = both[:, :BLOCK], SCALE * both[:, BLOCK:]
            made.append((rows_of(b), block, times, excess))
        scores = [
            fold(dot(v[where], by_cols(th[block], tl[block]), NN)) for where, block, _, _ in made
        ]
        pulls = [
            fold(
                dot(pair(times + excess * (1.0 - score)), by_cols(yh[block], yl[block]), NN)
            )
            for (_, block, times, excess), score in zip(made, scores)
        ]
        for u, ((where, _, _, excess), pull) in enumerate(zip(made, pulls)):
            held[(q * BUILD + u) % SLOTS] = excess
            out[where] += pull
        for u in range(BUILD):
            j = q * BUILD + u

            @pl.when(j < n)
            def _(j=j):
                out_copy(j).start()

        return 0

    groups = (n + BUILD - 1) // BUILD
    lax.fori_loop(0, groups, group, 0)

    def drain(j, _):
        out_copy(j).wait()
        return 0

    lax.fori_loop(jnp.maximum(groups * BUILD - SLOTS, 0), n, drain, 0)


def build(ent, yh, yl, th, tl, gram, start, peak):
    return pl.pallas_call(
        build_kernel,
        out_shape=(
            jax.ShapeDtypeStruct((UB * BLOCK, K), F32),
            jax.ShapeDtypeStruct((ALL_TILES, BLOCK, BLOCK), F32),
            jax.ShapeDtypeStruct((LIST,), jnp.int32),
            jax.ShapeDtypeStruct((1,), jnp.int32),
        ),
        in_specs=[VMEM] * 8,
        out_specs=(VMEM, ANY, SMEM, SMEM),
        scratch_shapes=[
            pltpu.SMEM((COLS, 8, 128), jnp.int32),
            pltpu.SMEM((LIST,), jnp.int32),
            pltpu.SMEM((UB,), jnp.int32),
            pltpu.VMEM((SLOTS, BLOCK, BLOCK), F32),
            pltpu.VMEM((UB * BLOCK, 2 * K), BF16),
            pltpu.SemaphoreType.DMA((SLOTS,)),
            pltpu.SemaphoreType.DMA,
        ],
        compiler_params=pltpu.CompilerParams(vmem_limit_bytes=BIG),
        name="build",
    )(ent, yh, yl, th, tl, gram, start, peak)


def fetch_tiles(order, weights, held, sem, base):
    here = jnp.minimum(order[LIST - 1] - base, HELD)

    def begin(i, _):
        pltpu.make_async_copy(weights.at[base + i], held.at[i], sem.at[i]).start()
        return 0

    lax.fori_loop(0, here, begin, 0)
    return here


def each_tile(order, weights, held, sem, work):
    n = order[LIST - 1]

    def batch(k, _):
        base = k * HELD
        here = jnp.minimum(n - base, HELD)

        def group(q, _):
            for u in range(GROUP):
                i = q * GROUP + u

                @pl.when(i < here)
                def _(i=i):
                    pltpu.make_async_copy(weights.at[base + i], held.at[i], sem.at[i]).wait()

            for u in range(GROUP):
                i = q * GROUP + u
                live = i < here
                code = jnp.where(live, order[base + i], 0)
                w = jnp.where(live, held[i], 0.0)
                work(code % UB, (code // UB) % 64, w)
            return 0

        lax.fori_loop(0, (here + GROUP - 1) // GROUP, group, 0)

        @pl.when(n > base + HELD)
        def _():
            fetch_tiles(order, weights, held, sem, base + HELD)

        return 0

    lax.fori_loop(0, (n + HELD - 1) // HELD, batch, 0)


def rows_of(b):
    return pl.ds(pl.multiple_of(b * BLOCK, BLOCK), BLOCK)


def dots(a, b):
    return jnp.sum(a * b, axis=1, keepdims=True)


def pull_tiles(order, weights, held, sem, yh, yl, th, tl, v, out):
    def work(b, block, w):
        at = rows_of(b)
        scores = fold(dot(v[at], by_cols(th[block], tl[block]), NN))
        out[at] += fold(dot(pair(w * scores), by_cols(yh[block], yl[block]), NN))

    each_tile(order, weights, held, sem, work)


def first_kernel(order, total, start, yh, yl, th, tl, gram, weights, out, residual, v, held, sem):
    fetch_tiles(order, weights, held, sem, 0)
    g = by_cols(*split(gram[...]))

    def begin(b, _):
        at = rows_of(b)
        p = total[at] - RIDGE * start[at]
        residual[at] = p
        both = pair(p)
        v[at] = both
        out[at] = fold(dot(both, g, NN))
        return 0

    lax.fori_loop(0, UB, begin, 0, unroll=UNROLL)
    pull_tiles(order, weights, held, sem, yh, yl, th, tl, v, out)


def update(total, iterate, residual, direction):
    image = total + RIDGE * direction
    now = dots(residual, residual)
    alpha = now / (dots(direction, image) + EPSILON)
    iterate = iterate + alpha * direction
    residual = residual - alpha * image
    after = dots(residual, residual)
    direction = residual + after / (now + EPSILON) * direction
    return iterate, residual, direction


def second_kernel(
    order, total, iterate, residual, yh, yl, th, tl, gram, weights, out, new_x, new_r, new_p, v, held, sem
):
    fetch_tiles(order, weights, held, sem, 0)
    g = by_cols(*split(gram[...]))

    def begin(b, _):
        at = rows_of(b)
        r = residual[at]
        new_x[at], new_r[at], p = update(total[at], iterate[at], r, r)
        new_p[at] = p
        both = pair(p)
        v[at] = both
        out[at] = fold(dot(both, g, NN))
        return 0

    lax.fori_loop(0, UB, begin, 0, unroll=UNROLL)
    pull_tiles(order, weights, held, sem, yh, yl, th, tl, v, out)


def third_kernel(
    order, total, iterate, residual, direction, yh, yl, th, tl, gram, weights,
    squares, new_x, new_r, new_p, v, acc, held, sem,
):
    fetch_tiles(order, weights, held, sem, 0)
    g = by_cols(*split(gram[...]))

    def begin(b, _):
        at = rows_of(b)
        new_x[at], new_r[at], p = update(total[at], iterate[at], residual[at], direction[at])
        new_p[at] = p
        both = pair(p)
        v[at] = both
        acc[at] = p * fold(dot(both, g, NN))
        return 0

    lax.fori_loop(0, UB, begin, 0, unroll=UNROLL)

    def work(b, block, w):
        at = rows_of(b)
        scores = fold(dot(v[at], by_cols(th[block], tl[block]), NN))
        acc[at] += w * scores * scores

    each_tile(order, weights, held, sem, work)
    for b in range(UB):
        squares[b : b + 1] = jnp.sum(acc[b * BLOCK : (b + 1) * BLOCK].T, axis=0, keepdims=True)


def last_kernel(squares, iterate, residual, direction, out):
    sums = squares[...]
    for b in range(UB):
        at = pl.ds(b * BLOCK, BLOCK)
        p = direction[at]
        r = residual[at]
        below = jnp.broadcast_to(sums[b : b + 1], (BLOCK, BLOCK)).T + RIDGE * dots(p, p)
        out[at] = iterate[at] + dots(r, r) / (below + EPSILON) * p


USERS = jax.ShapeDtypeStruct((UB * BLOCK, K), F32)


def local(kernel, name, outs, specs, scratch=()):
    tiles = [
        pltpu.VMEM((UB * BLOCK, 2 * K), BF16),
        *scratch,
        pltpu.VMEM((HELD, BLOCK, BLOCK), F32),
        pltpu.SemaphoreType.DMA((HELD,)),
    ]
    return pl.pallas_call(
        kernel,
        out_shape=outs,
        in_specs=specs,
        out_specs=tuple(VMEM for _ in outs),
        scratch_shapes=tiles,
        compiler_params=pltpu.CompilerParams(vmem_limit_bytes=BIG),
        name=name,
    )


def reduce_kernel(part, out, land, sums, near, send_sem, recv_sem):
    c, z, x, along_x, along_z = col_place()
    greet(along_x + along_z)
    copies = Copies(send_sem, recv_sem)
    send = copies.send
    streams = [(pl.ds(SUB * i, SUB), i % 2 == 0) for i in range(BLOCK // SUB)]

    def line(ref, way, d, rows):
        return ref.at[:, (x + d) % NX, rows] if way else ref.at[(z + d) % NZ, :, rows]

    def axes(way):
        return (along_x, along_z, z) if way else (along_z, along_x, x)

    far = [
        [send(line(part, way, d, rows), land.at[i, d - 1], axes(way)[0][d - 1]) for d in (1, 2, 3)]
        for i, (rows, way) in enumerate(streams)
    ]
    close = []
    for i, (rows, way) in enumerate(streams):
        _, along, me = axes(way)
        for copy in far[i]:
            copy.wait_recv()
        mine = part[:, x, rows] if way else part[z, :, rows]
        sums[i] = mine + land[i, 0] + (land[i, 1] + land[i, 2])
        close.append(
            [send(sums.at[i, (me + d) % 4], near.at[i, d - 1], along[d - 1]) for d in (1, 2, 3)]
        )
    back = []
    for i, (rows, way) in enumerate(streams):
        _, along, me = axes(way)
        for copy in close[i]:
            copy.wait_recv()
        out[z, x, rows] = sums[i, me] + near[i, 0] + (near[i, 1] + near[i, 2])
        here = out.at[z, x, rows]
        back.append([send(here, here, peer) for peer in along])
    end = []
    for i, (rows, way) in enumerate(streams):
        for copy in back[i]:
            copy.wait_recv()
        here = line(out, way, 0, rows)
        end += [send(here, here, peer) for peer in axes(way)[0]]
    for copy in end:
        copy.wait_recv()
    copies.finish()


def reduce(part):
    n = BLOCK // SUB
    out = pl.pallas_call(
        reduce_kernel,
        out_shape=jax.ShapeDtypeStruct((NZ, NX, BLOCK, K), F32),
        in_specs=[VMEM],
        out_specs=VMEM,
        scratch_shapes=[
            pltpu.VMEM((n, 3, 4, SUB, K), F32),
            pltpu.VMEM((n, 4, SUB, K), F32),
            pltpu.VMEM((n, 3, SUB, K), F32),
            pltpu.SemaphoreType.DMA((12 * n,)),
            pltpu.SemaphoreType.DMA((12 * n,)),
        ],
        compiler_params=pltpu.CompilerParams(
            collective_id=1, has_side_effects=True, vmem_limit_bytes=BIG
        ),
        name="reduce",
    )(part.reshape(NZ, NX, BLOCK, K))
    return out.reshape(UB * BLOCK, K)


def scalars_kernel(mine, out, land_x, land_z, half, send_sem, recv_sem):
    _, _, _, along_x, along_z = col_place()
    greet(along_x + along_z)
    copies = Copies(send_sem, recv_sem)
    for copy in [copies.send(mine, land_x.at[i], peer) for i, peer in enumerate(along_x)]:
        copy.wait_recv()
    half[...] = mine[...] + land_x[0] + (land_x[1] + land_x[2])
    for copy in [copies.send(half, land_z.at[i], peer) for i, peer in enumerate(along_z)]:
        copy.wait_recv()
    out[...] = half[...] + land_z[0] + (land_z[1] + land_z[2])
    copies.finish()


def sum_scalars(mine):
    return pl.pallas_call(
        scalars_kernel,
        out_shape=jax.ShapeDtypeStruct((UB, BLOCK), F32),
        in_specs=[VMEM],
        out_specs=VMEM,
        scratch_shapes=[
            pltpu.VMEM((3, UB, BLOCK), F32),
            pltpu.VMEM((3, UB, BLOCK), F32),
            pltpu.VMEM((UB, BLOCK), F32),
            pltpu.SemaphoreType.DMA((6,)),
            pltpu.SemaphoreType.DMA((6,)),
        ],
        compiler_params=pltpu.CompilerParams(collective_id=2, has_side_effects=True, vmem_limit_bytes=BIG),
        name="scalars",
    )(mine)


def cg_kernel(
    order, part, start, yh, yl, th, tl, gram, weights, out,
    held, v, x_now, r_now, p_now, pulls, squares, parts, tot, land, sums, near,
    row_sums, land_x, land_z, half, send_sem, recv_sem, w_sem,
):
    _, z, x, along_x, along_z = col_place()
    load = pltpu.make_async_copy(weights.at[pl.ds(0, FAST)], held, w_sem)
    load.start()
    greet(along_x + along_z)
    copies = Copies(send_sem, recv_sem)
    send = copies.send
    far, close, back, end = {}, {}, {}, {}
    rounds = (part, parts.at[0], parts.at[1])

    def streams(s):
        for i in range(4 * s, 4 * s + 4):
            way = i % 2 == 0
            first, second, me = (along_x, along_z, z) if way else (along_z, along_x, x)
            yield i, pl.ds(THIN * i, THIN), way, first, second, me

    def line(ref, way, d, rows):
        return ref.at[:, (x + d) % NX, rows] if way else ref.at[(z + d) % NZ, :, rows]

    def begin(k, s):
        for i, rows, way, first, _, _ in streams(s):
            far[k, i] = [
                send(line(rounds[k], way, d, rows), land.at[k, i, d - 1], first[d - 1])
                for d in (2, 1, 3)
            ]

    def sum_first(k, s):
        for i, rows, way, _, second, me in streams(s):
            for copy in far[k, i]:
                copy.wait_recv()
            mine = rounds[k][:, x, rows] if way else rounds[k][z, :, rows]
            sums[k, i] = mine + land[k, i, 0] + (land[k, i, 1] + land[k, i, 2])
            close[k, i] = [
                send(sums.at[k, i, (me + d) % 4], near.at[k, i, d - 1], second[d - 1])
                for d in (2, 1, 3)
            ]

    def sum_second(k, s):
        for i, rows, _, _, second, me in streams(s):
            for copy in close[k, i]:
                copy.wait_recv()
            tot[k, z, x, rows] = sums[k, i, me] + near[k, i, 0] + (near[k, i, 1] + near[k, i, 2])
            here = tot.at[k, z, x, rows]
            back[k, i] = [send(here, here, second[d]) for d in (1, 0, 2)]

    def spread(k, s):
        for i, rows, way, first, _, _ in streams(s):
            for copy in back[k, i]:
                copy.wait_recv()
            here = line(tot.at[k], way, 0, rows)
            end[k, i] = [send(here, here, first[d]) for d in (1, 0, 2)]

    def arrive(k, s):
        for i in range(4 * s, 4 * s + 4):
            for copy in end[k, i]:
                copy.wait_recv()

    g = by_cols(*split(gram[...]))
    n = order[LIST - 1]

    def compute(k, s, before_end):
        rows = pl.ds(64 * s, 64)

        def step(b, _):
            total = tot[k - 1, b // NX, b % NX, rows]
            if k == 1:
                p = total - RIDGE * start[b, rows]
                r_now[b, rows] = p
            else:
                before = start[b, rows] if k == 2 else x_now[b, rows]
                r = r_now[b, rows]
                old = r if k == 2 else p_now[b, rows]
                x_now[b, rows], r_now[b, rows], p = update(total, before, r, old)
            p_now[b, rows] = p
            v[b, rows] = pair(p)
            return 0

        lax.fori_loop(0, UB, step, 0, unroll=16)

        def some(q, acc):
            last_b, acc = acc
            for u in range(STEP):
                j = q * STEP + u
                code = order[j]
                b, block = code & (UB - 1), (code >> 4) & 63
                w = jnp.where(j < n, held[j, rows], 0.0)
                scores = fold(dot(v[b, rows], by_cols(th[block], tl[block]), NN))
                if k < 3:
                    pull = fold(dot(pair(w * scores), by_cols(yh[block], yl[block]), NN))
                else:
                    pull = w * scores * scores
                acc = jnp.where(b == last_b, acc, 0.0) + pull
                last_b = b
                pulls[s, j] = acc
            return last_b, acc

        lax.fori_loop(0, FAST // STEP, some, (jnp.int32(-1), jnp.zeros((64, K), F32)))
        before_end()

        def close_up(b, _):
            end_of = order[LAST + b]
            pulled = jnp.where(end_of >= 0, pulls[s, jnp.maximum(end_of, 0)], 0.0)
            whole = fold(dot(v[b, rows], g, NN))
            if k < 3:
                parts[k - 1, b // NX, b % NX, rows] = whole + pulled
            else:
                squares[b, rows] = p_now[b, rows] * whole + pulled
            return 0

        lax.fori_loop(0, UB, close_up, 0, unroll=16)
        if k == 3:
            for b in range(UB):
                row_sums[b : b + 1, 64 * s : 64 * s + 64] = jnp.sum(
                    squares[b, rows].T, axis=0, keepdims=True
                )

    def nothing():
        pass

    begin(0, 0)
    begin(0, 1)
    sum_first(0, 0)
    for k in range(3):
        sum_first(k, 1)
        for work in (sum_second, spread):
            work(k, 0)
            work(k, 1)
        if k == 0:
            load.wait()
        arrive(k, 0)
        compute(k + 1, 0, nothing)
        if k < 2:
            begin(k + 1, 0)
        arrive(k, 1)
        compute(k + 1, 1, functools.partial(sum_first, k + 1, 0) if k < 2 else nothing)
        if k < 2:
            begin(k + 1, 1)

    told = [send(row_sums, land_x.at[i], peer) for i, peer in enumerate(along_x)]
    for b in range(UB):
        p, r = p_now[b], r_now[b]
        rest = jnp.broadcast_to(RIDGE * dots(p, p) + EPSILON, (BLOCK, K))
        pulls[0, b] = rest[:64]
        pulls[1, b] = rest[64:]
        squares[b] = jnp.broadcast_to(dots(r, r), (BLOCK, K))
    for copy in told:
        copy.wait_recv()
    half[...] = row_sums[...] + land_x[0] + (land_x[1] + land_x[2])
    for copy in [send(half, land_z.at[i], peer) for i, peer in enumerate(along_z)]:
        copy.wait_recv()
    both = half[...] + land_z[0] + (land_z[1] + land_z[2])
    for b in range(UB):
        below = jnp.broadcast_to(both[b : b + 1], (BLOCK, BLOCK)).T
        rest = jnp.concatenate([pulls[0, b], pulls[1, b]], axis=0)
        out[b] = x_now[b] + squares[b] / (below + rest) * p_now[b]
    copies.finish()


def all_steps(order, part, start, yh, yl, th, tl, gram, weights):
    n = BLOCK // THIN
    copies = 3 * 12 * n + 6
    blocks = (UB, BLOCK, K)
    out = pl.pallas_call(
        cg_kernel,
        out_shape=jax.ShapeDtypeStruct(blocks, F32),
        in_specs=[SMEM] + [VMEM] * 7 + [ANY],
        out_specs=VMEM,
        scratch_shapes=[
            pltpu.VMEM((FAST, BLOCK, BLOCK), F32),
            pltpu.VMEM((UB, BLOCK, 2 * K), BF16),
            pltpu.VMEM(blocks, F32),
            pltpu.VMEM(blocks, F32),
            pltpu.VMEM(blocks, F32),
            pltpu.VMEM((2, FAST, 64, K), F32),
            pltpu.VMEM(blocks, F32),
            pltpu.VMEM((2, NZ, NX, BLOCK, K), F32),
            pltpu.VMEM((3, NZ, NX, BLOCK, K), F32),
            pltpu.VMEM((3, n, 3, 4, THIN, K), F32),
            pltpu.VMEM((3, n, 4, THIN, K), F32),
            pltpu.VMEM((3, n, 3, THIN, K), F32),
            pltpu.VMEM((UB, BLOCK), F32),
            pltpu.VMEM((3, UB, BLOCK), F32),
            pltpu.VMEM((3, UB, BLOCK), F32),
            pltpu.VMEM((UB, BLOCK), F32),
            pltpu.SemaphoreType.DMA((copies,)),
            pltpu.SemaphoreType.DMA((copies,)),
            pltpu.SemaphoreType.DMA,
        ],
        compiler_params=pltpu.CompilerParams(
            collective_id=3, has_side_effects=True, vmem_limit_bytes=WHOLE
        ),
        name="steps",
    )(order, part.reshape(NZ, NX, BLOCK, K), start.reshape(blocks), yh, yl, th, tl, gram, weights)
    return out.reshape(UB * BLOCK, K)


def step_by_step(order, part, start, yh, yl, th, tl, gram, weights):
    total = reduce(part)
    tail = [VMEM] * 5 + [ANY]
    part, residual = local(first_kernel, "first", (USERS,) * 2, [SMEM, VMEM, VMEM] + tail)(
        order, total, start, yh, yl, th, tl, gram, weights
    )
    total = reduce(part)
    part, iterate, residual, direction = local(
        second_kernel, "second", (USERS,) * 4, [SMEM] + [VMEM] * 3 + tail
    )(order, total, start, residual, yh, yl, th, tl, gram, weights)
    total = reduce(part)
    squares = jax.ShapeDtypeStruct((UB, BLOCK), F32)
    part, iterate, residual, direction = local(
        third_kernel,
        "third",
        (squares,) + (USERS,) * 3,
        [SMEM] + [VMEM] * 4 + tail,
        [pltpu.VMEM((UB * BLOCK, K), F32)],
    )(order, total, iterate, residual, direction, yh, yl, th, tl, gram, weights)
    squares = sum_scalars(part)
    return pl.pallas_call(
        last_kernel,
        out_shape=USERS,
        in_specs=[VMEM] * 4,
        out_specs=VMEM,
        compiler_params=pltpu.CompilerParams(vmem_limit_bytes=BIG),
        name="last",
    )(squares, iterate, residual, direction)


def shards(user_factors, item_factors, fetch_list, tile_user, tile_slot, er, ec, en, tile_count):
    yh, yl, th, tl, gram, ent, peak = gather(
        item_factors.reshape(IB, BLOCK, K),
        fetch_list.reshape(1, 128),
        tile_user.reshape(1, TILES),
        tile_slot.reshape(1, TILES),
        er.reshape(TILES, NNZ),
        ec.reshape(TILES, NNZ),
        en.reshape(TILES, NNZ),
        tile_count.reshape(1, 1),
    )
    part, weights, order, fits = build(
        ent.reshape(COLS, STAGE, NNZ), yh, yl, th, tl, gram, user_factors, peak
    )
    return lax.cond(
        fits[0] > 0,
        all_steps,
        step_by_step,
        order, part, user_factors, yh, yl, th, tl, gram, weights,
    )


def solution(mesh):
    return jax.shard_map(
        shards,
        mesh=mesh,
        in_specs=(
            P("row", None),
            P(("row", "col"), None),
            P("row", "col", None, None),
            P("row", "col", None),
            P("row", "col", None),
            P("row", "col", None, None),
            P("row", "col", None, None),
            P("row", "col", None, None),
            P("row", "col"),
        ),
        out_specs=P("row", None),
        check_vma=False,
    )
```

```python
import functools

import jax
import jax.numpy as jnp
from jax import lax
from jax.experimental import pallas as pl
from jax.experimental.pallas import tpu as pltpu
from jax.sharding import PartitionSpec as P

K = 128
BLOCK = 128
UB = 16
IB = 8
TILES = 32
NNZ = 512
NZ = NX = 4
NY = 4
ROWS = 8
COLS = 16
ALL_TILES = COLS * TILES
LIST = 1024
LAST = 512
FAST = 36
STEP = 36
SUB = 32
THIN = 16
UNROLL = 4
BUILD = 4
SLOTS = 2 * BUILD
GROUP = 4
HELD = 32
STAGE = 3 * TILES + 8
HALF = 56
SCALE = 40.0
RIDGE = 0.5
EPSILON = 1e-06
MESH = pl.DeviceIdType.MESH
F32 = jnp.float32
BF16 = jnp.bfloat16
NT = (((1,), (1,)), ((), ()))
NN = (((1,), (0,)), ((), ()))
ANY = pl.BlockSpec(memory_space=pl.ANY)
VMEM = pl.BlockSpec(memory_space=pltpu.VMEM)
SMEM = pl.BlockSpec(memory_space=pltpu.SMEM)
HBM = pl.BlockSpec(memory_space=pltpu.HBM)
BIG = 24 * 2**20
WHOLE = 40 * 2**20


def dot(a, b, dims):
    return lax.dot_general(a, b, dims, preferred_element_type=F32)


def split(a):
    high = a.astype(BF16)
    return high, (a - high.astype(F32)).astype(BF16)


def pair(a):
    return jnp.concatenate(split(a), axis=1)


def fold(wide):
    return wide[:, 0:128] + wide[:, 128:256]


def by_cols(high, low):
    both = jnp.concatenate([high, low], axis=1)
    return jnp.concatenate([both, both], axis=0)


def greet(peers):
    barrier = pltpu.get_barrier_semaphore()
    for peer in peers:
        pl.semaphore_signal(barrier, inc=1, device_id=peer, device_id_type=MESH)
    pl.semaphore_wait(barrier, len(peers))


class Copies:
    def __init__(self, send_sem, recv_sem):
        self.send_sem, self.recv_sem, self.made = send_sem, recv_sem, []

    def send(self, src, dst, peer):
        i = len(self.made)
        copy = pltpu.make_async_remote_copy(
            src_ref=src,
            dst_ref=dst,
            send_sem=self.send_sem.at[i],
            recv_sem=self.recv_sem.at[i],
            device_id=peer,
            device_id_type=MESH,
        )
        copy.start()
        self.made.append(copy)
        return copy

    def finish(self):
        for copy in self.made:
            copy.wait_send()


def col_place():
    c = lax.axis_index("col")
    z, x = c // NX, c % NX
    along_x = [{"col": z * NX + (x + d) % NX} for d in range(1, NX)]
    along_z = [{"col": ((z + d) % NZ) * NX + x} for d in range(1, NZ)]
    return c, z, x, along_x, along_z


def gather_kernel(
    items, fetch, user, slot, er, ec, en, count, yh, yl, th, tl, gram, ent, peak,
    stage, land, fetch_in, slot_in, user_in, small, keys, most, seen, send_sem, recv_sem, own_sem, in_sem,
):
    c, z, x, along_x, along_z = col_place()
    r = lax.axis_index("row")
    y, core = r // 2, r % 2
    right, left, across = (((y + d) % NY) * 2 + core for d in (1, 3, 2))
    other = y * 2 + 1 - core
    to_right, to_left, to_other = {"row": right}, {"row": left}, {"row": other}
    to_across = {"row": across}
    loads = [
        pltpu.make_async_copy(src, dst, in_sem.at[i])
        for i, (src, dst) in enumerate(
            (
                (er, stage.at[pl.ds(0, TILES)]),
                (ec, stage.at[pl.ds(TILES, TILES)]),
                (en, stage.at[pl.ds(2 * TILES, TILES)]),
                (items, land.at[r]),
                (fetch, fetch_in),
                (slot, slot_in),
                (user, user_in),
            )
        )
    ]
    for load in loads:
        load.start()
    greet(along_x + along_z + [to_right, to_left, to_across, to_other])
    copies = Copies(send_sem, recv_sem)
    send = copies.send
    half = [items.at[pl.ds(4 * i, 4)] for i in (0, 1)]
    there = [land.at[r, pl.ds(4 * i, 4)] for i in (0, 1)]
    from_left, from_right = [None, None], [None, None]
    for i in (0, 1):
        from_left[i] = send(half[i], there[i], to_right)
        from_right[1 - i] = send(half[1 - i], there[1 - i], to_left)
    between = [send(items, land.at[r], to_other)]

    for load in loads[4:]:
        load.wait()
    small[...] = jnp.zeros_like(small)
    small[0:1, 0:TILES] = slot_in[...]
    small[1:2, 0:TILES] = user_in[...]
    slots = small[0:1]
    table = jnp.broadcast_to(fetch_in[...].astype(F32), (128, 128)).T
    ids = lax.broadcasted_iota(jnp.int32, (128, 128), 0)
    local_id = jnp.sum(jnp.where(ids == slots, table, 0.0), axis=0, keepdims=True).astype(jnp.int32)
    lanes = lax.broadcasted_iota(jnp.int32, (1, 128), 1)
    last = 3 * TILES
    stage[last : last + 1, 0:128] = jnp.where(lanes < count[0, 0], slots & (COLS - 1), -1)
    stage[last + 1 : last + 2, 0:128] = ((slots >> 4) * IB + local_id) * UB + small[1:2]
    first_key = stage[last : last + 1, 0:128]
    keys[z, x] = jnp.broadcast_to(first_key, (8, 128))
    for load in loads[:3]:
        load.wait()
    own = pltpu.make_async_copy(stage, ent.at[z, x], own_sem)
    own.start()

    first, second = pl.ds(0, HALF), pl.ds(HALF, STAGE - HALF)
    parts = (pl.ds(0, 32), pl.ds(32, 24)), (pl.ds(56, 24), pl.ds(80, 24))
    ways = (
        (first, along_x, along_z, lambda d, e: ent.at[(z + e) % NZ, (x + d) % NX]),
        (second, along_z, along_x, lambda d, e: ent.at[(z + d) % NZ, (x + e) % NX]),
    )
    near = [[None] * 4, [None] * 4]
    up = [[None] * 4, [None] * 4]
    down = [[None] * 4, [None] * 4]

    def spread(w, d, source):
        rows, _, across_way, at = ways[w]
        to = at(-d, 0).at[rows]
        up[w][d] = send(source, to, across_way[0])
        down[w][d] = send(source, to, across_way[2])

    for w, (rows, along, _, at) in enumerate(ways):
        for d in (1, 3, 2):
            near[w][d] = send(stage.at[rows], at(0, 0).at[rows], along[d - 1])
        spread(w, 0, stage.at[rows])
    mine = keys.at[z, x]
    told_keys = [send(mine, mine, peer) for peer in along_x]

    far = []

    def pass_on(w, d):
        _, _, across_way, at = ways[w]
        up[w][d].wait_recv()
        piece = at(-d, -1).at[parts[w][0]]
        far.append(send(piece, piece, across_way[0]))
        down[w][d].wait_recv()
        piece = at(-d, 1).at[parts[w][1]]
        far.append(send(piece, piece, across_way[2]))

    def add(row, sums):
        def one(i, sums):
            high, low = split(land[row, i])
            high_t = high.T
            at = row * IB + i
            yh[at] = high
            yl[at] = low
            th[at] = high_t
            tl[at] = low.T
            return sums + dot(high_t, jnp.concatenate([high, low], axis=1), NN)

        return lax.fori_loop(0, IB, one, sums, unroll=4)

    loads[3].wait()
    sums = add(r, jnp.zeros((K, 2 * K), F32))
    for copy in told_keys:
        copy.wait_recv()
    mine = keys.at[z]
    told_keys = [send(mine, mine, peer) for peer in along_z]

    for d in (1, 3, 2):
        for w in (0, 1):
            near[w][d].wait_recv()
            rows, _, _, at = ways[w]
            spread(w, d, at(-d, 0).at[rows])
    for w in (0, 1):
        pass_on(w, 0)
    from_left[0].wait_recv()
    piece = land.at[left, pl.ds(0, 4)]
    round_y = [send(piece, piece, to_right)]
    from_right[1].wait_recv()
    piece = land.at[right, pl.ds(4, 4)]
    round_y.append(send(piece, piece, to_left))
    for copy in told_keys:
        copy.wait_recv()
    owners = keys[:, :, 0, :].reshape(COLS, 128)
    counted = [
        jnp.sum(jnp.where(owners == column, 1.0, 0.0), axis=0, keepdims=True)
        for column in range(COLS)
    ]
    counted = jnp.sum(jnp.concatenate(counted, axis=0), axis=1, keepdims=True)
    longest = jnp.max(counted, axis=0, keepdims=True).astype(jnp.int32)
    most[0] = jnp.broadcast_to(longest, (8, 128))

    told = [
        send(most.at[0], seen.at[i], peer)
        for i, peer in enumerate((to_right, to_left, to_across))
    ]
    between[0].wait_recv()
    sums = add(other, sums)
    for d in (1, 3):
        for w in (0, 1):
            pass_on(w, d)
    from_left[1].wait_recv()
    between.append(send(land.at[left], land.at[left], to_other))
    from_right[0].wait_recv()
    between.append(send(land.at[right], land.at[right], to_other))
    for w in (0, 1):
        pass_on(w, 2)
    for copy in told:
        copy.wait_recv()
    most[1] = jnp.maximum(jnp.maximum(most[0], seen[0]), jnp.maximum(seen[1], seen[2]))
    told = send(most.at[1], seen.at[3], to_other)
    sums = add(left, sums)
    sums = add(right, sums)
    for copy in round_y:
        copy.wait_recv()
    between.append(send(land.at[across], land.at[across], to_other))
    sums = add(across, sums)
    for copy, d in zip(between[1:], (3, 1, 2)):
        copy.wait_recv()
        sums = add(((y + d) % NY) * 2 + 1 - core, sums)
    told.wait_recv()
    peak[...] = jnp.maximum(most[1], seen[3])
    for copy in far:
        copy.wait_recv()
    own.wait()
    mixed = sums[:, K:]
    gram[...] = sums[:, :K] + (mixed + mixed.T)
    copies.finish()


def gather(items, fetch, user, slot, er, ec, en, count):
    n = 6 + 4 + 2 * (3 + 8 + 8) + 10
    return pl.pallas_call(
        gather_kernel,
        out_shape=(
            *[jax.ShapeDtypeStruct((ROWS * IB, BLOCK, K), BF16)] * 4,
            jax.ShapeDtypeStruct((K, K), F32),
            jax.ShapeDtypeStruct((NZ, NX, STAGE, NNZ), jnp.int32),
            jax.ShapeDtypeStruct((8, 128), jnp.int32),
        ),
        in_specs=[HBM] * 7 + [SMEM],
        out_specs=(VMEM, VMEM, VMEM, VMEM, VMEM, ANY, VMEM),
        scratch_shapes=[
            pltpu.VMEM((STAGE, NNZ), jnp.int32),
            pltpu.VMEM((ROWS, IB, BLOCK, K), F32),
            pltpu.VMEM((1, 128), jnp.int32),
            pltpu.VMEM((1, TILES), jnp.int32),
            pltpu.VMEM((1, TILES), jnp.int32),
            pltpu.VMEM((8, 128), jnp.int32),
            pltpu.VMEM((NZ, NX, 8, 128), jnp.int32),
            pltpu.VMEM((2, 8, 128), jnp.int32),
            pltpu.VMEM((4, 8, 128), jnp.int32),
            pltpu.SemaphoreType.DMA((n,)),
            pltpu.SemaphoreType.DMA((n,)),
            pltpu.SemaphoreType.DMA,
            pltpu.SemaphoreType.DMA((7,)),
        ],
        compiler_params=pltpu.CompilerParams(
            collective_id=0, has_side_effects=True, vmem_limit_bytes=BIG
        ),
        name="gather",
    )(*[pltpu.with_memory_space_constraint(a, pltpu.HBM) for a in (items, fetch, user, slot, er, ec, en)], count)


def build_kernel(
    ent, yh, yl, th, tl, gram, start, peak, out, weights, order, fits, meta, found, place, held, v, sem, meta_sem
):
    fetched = pltpu.make_async_copy(
        ent.at[:, pl.ds(3 * TILES, 8), pl.ds(0, 128)], meta, meta_sem
    )
    fetched.start()
    g = by_cols(*split(gram[...]))

    def begin(b, _):
        at = rows_of(b)
        both = pair(start[at])
        v[at] = both
        out[at] = -fold(dot(both, g, NN))
        return 0

    lax.fori_loop(0, UB, begin, 0, unroll=UNROLL)
    fits[0] = jnp.where(jnp.max(peak[...].astype(F32)) <= FAST, 1, 0)
    fetched.wait()
    me = lax.axis_index("col")

    def scan(c, n):
        for t in range(TILES):
            found[n] = (c * TILES + t) * (64 * UB) + meta[c, 1, t]
            n = n + jnp.where(meta[c, 0, t] == me, 1, 0)
        return n

    n = lax.fori_loop(0, COLS, scan, 0)
    order[LIST - 1] = n

    for b in range(UB):
        place[b] = 0

    def count(j, _):
        b = found[j] & (UB - 1)
        place[b] = place[b] + 1
        return 0

    lax.fori_loop(0, n, count, 0)
    total = 0
    for b in range(UB):
        of_b = place[b]
        order[LAST + b] = jnp.where(of_b > 0, total + of_b - 1, -1)
        place[b] = total
        total = total + of_b

    def put(j, _):
        code = found[j]
        b = code & (UB - 1)
        to = place[b]
        order[to] = code
        place[b] = to + 1
        return 0

    lax.fori_loop(0, n, put, 0)
    ids = lax.broadcasted_iota(jnp.int32, (BLOCK, NNZ), 0)
    one, none = jnp.ones((), BF16), jnp.zeros((), BF16)

    def out_copy(j):
        slot = j % SLOTS
        return pltpu.make_async_copy(held.at[slot], weights.at[j], sem.at[slot])

    def group(q, _):
        for u in range(BUILD):
            j = q * BUILD + u

            @pl.when((j >= SLOTS) & (j - SLOTS < n))
            def _(j=j):
                out_copy(j - SLOTS).wait()

        made = []
        for u in range(BUILD):
            j = q * BUILD + u
            code = jnp.where(j < n, order[j], 0)
            b, block, at = code % UB, (code // UB) % 64, code // (64 * UB)
            c, t = at // TILES, at % TILES
            rows = jnp.where(j < n, ent[c, pl.ds(t, 1), :], BLOCK)
            cols = ent[c, pl.ds(TILES + t, 1), :]
            counts = ent[c, pl.ds(2 * TILES + t, 1), :].astype(F32)
            in_col = ids == cols
            once = jnp.where(in_col, 1.0, 0.0).astype(BF16)
            ones = jnp.where(ids == rows, 1.0, 0.0).astype(BF16)
            many = jnp.where(in_col, counts, 0.0).astype(BF16)
            both = dot(ones, jnp.concatenate([once, many], axis=0), NT)
            times, excess = both[:, :BLOCK], SCALE * both[:, BLOCK:]
            made.append((rows_of(b), block, times, excess))
        scores = [
            fold(dot(v[where], by_cols(th[block], tl[block]), NN)) for where, block, _, _ in made
        ]
        pulls = [
            fold(
                dot(pair(times + excess * (1.0 - score)), by_cols(yh[block], yl[block]), NN)
            )
            for (_, block, times, excess), score in zip(made, scores)
        ]
        for u, ((where, _, _, excess), pull) in enumerate(zip(made, pulls)):
            held[(q * BUILD + u) % SLOTS] = excess
            out[where] += pull
        for u in range(BUILD):
            j = q * BUILD + u

            @pl.when(j < n)
            def _(j=j):
                out_copy(j).start()

        return 0

    groups = (n + BUILD - 1) // BUILD
    lax.fori_loop(0, groups, group, 0)

    def drain(j, _):
        out_copy(j).wait()
        return 0

    lax.fori_loop(jnp.maximum(groups * BUILD - SLOTS, 0), n, drain, 0)


def build(ent, yh, yl, th, tl, gram, start, peak):
    return pl.pallas_call(
        build_kernel,
        out_shape=(
            jax.ShapeDtypeStruct((UB * BLOCK, K), F32),
            jax.ShapeDtypeStruct((ALL_TILES, BLOCK, BLOCK), F32),
            jax.ShapeDtypeStruct((LIST,), jnp.int32),
            jax.ShapeDtypeStruct((1,), jnp.int32),
        ),
        in_specs=[VMEM] * 8,
        out_specs=(VMEM, ANY, SMEM, SMEM),
        scratch_shapes=[
            pltpu.SMEM((COLS, 8, 128), jnp.int32),
            pltpu.SMEM((LIST,), jnp.int32),
            pltpu.SMEM((UB,), jnp.int32),
            pltpu.VMEM((SLOTS, BLOCK, BLOCK), F32),
            pltpu.VMEM((UB * BLOCK, 2 * K), BF16),
            pltpu.SemaphoreType.DMA((SLOTS,)),
            pltpu.SemaphoreType.DMA,
        ],
        compiler_params=pltpu.CompilerParams(vmem_limit_bytes=BIG),
        name="build",
    )(ent, yh, yl, th, tl, gram, start, peak)


def fetch_tiles(order, weights, held, sem, base):
    here = jnp.minimum(order[LIST - 1] - base, HELD)

    def begin(i, _):
        pltpu.make_async_copy(weights.at[base + i], held.at[i], sem.at[i]).start()
        return 0

    lax.fori_loop(0, here, begin, 0)
    return here


def each_tile(order, weights, held, sem, work):
    n = order[LIST - 1]

    def batch(k, _):
        base = k * HELD
        here = jnp.minimum(n - base, HELD)

        def group(q, _):
            for u in range(GROUP):
                i = q * GROUP + u

                @pl.when(i < here)
                def _(i=i):
                    pltpu.make_async_copy(weights.at[base + i], held.at[i], sem.at[i]).wait()

            for u in range(GROUP):
                i = q * GROUP + u
                live = i < here
                code = jnp.where(live, order[base + i], 0)
                w = jnp.where(live, held[i], 0.0)
                work(code % UB, (code // UB) % 64, w)
            return 0

        lax.fori_loop(0, (here + GROUP - 1) // GROUP, group, 0)

        @pl.when(n > base + HELD)
        def _():
            fetch_tiles(order, weights, held, sem, base + HELD)

        return 0

    lax.fori_loop(0, (n + HELD - 1) // HELD, batch, 0)


def rows_of(b):
    return pl.ds(pl.multiple_of(b * BLOCK, BLOCK), BLOCK)


def dots(a, b):
    return jnp.sum(a * b, axis=1, keepdims=True)


def pull_tiles(order, weights, held, sem, yh, yl, th, tl, v, out):
    def work(b, block, w):
        at = rows_of(b)
        scores = fold(dot(v[at], by_cols(th[block], tl[block]), NN))
        out[at] += fold(dot(pair(w * scores), by_cols(yh[block], yl[block]), NN))

    each_tile(order, weights, held, sem, work)


def first_kernel(order, total, start, yh, yl, th, tl, gram, weights, out, residual, v, held, sem):
    fetch_tiles(order, weights, held, sem, 0)
    g = by_cols(*split(gram[...]))

    def begin(b, _):
        at = rows_of(b)
        p = total[at] - RIDGE * start[at]
        residual[at] = p
        both = pair(p)
        v[at] = both
        out[at] = fold(dot(both, g, NN))
        return 0

    lax.fori_loop(0, UB, begin, 0, unroll=UNROLL)
    pull_tiles(order, weights, held, sem, yh, yl, th, tl, v, out)


def update(total, iterate, residual, direction):
    image = total + RIDGE * direction
    now = dots(residual, residual)
    alpha = now / (dots(direction, image) + EPSILON)
    iterate = iterate + alpha * direction
    residual = residual - alpha * image
    after = dots(residual, residual)
    direction = residual + after / (now + EPSILON) * direction
    return iterate, residual, direction


def second_kernel(
    order, total, iterate, residual, yh, yl, th, tl, gram, weights, out, new_x, new_r, new_p, v, held, sem
):
    fetch_tiles(order, weights, held, sem, 0)
    g = by_cols(*split(gram[...]))

    def begin(b, _):
        at = rows_of(b)
        r = residual[at]
        new_x[at], new_r[at], p = update(total[at], iterate[at], r, r)
        new_p[at] = p
        both = pair(p)
        v[at] = both
        out[at] = fold(dot(both, g, NN))
        return 0

    lax.fori_loop(0, UB, begin, 0, unroll=UNROLL)
    pull_tiles(order, weights, held, sem, yh, yl, th, tl, v, out)


def third_kernel(
    order, total, iterate, residual, direction, yh, yl, th, tl, gram, weights,
    squares, new_x, new_r, new_p, v, acc, held, sem,
):
    fetch_tiles(order, weights, held, sem, 0)
    g = by_cols(*split(gram[...]))

    def begin(b, _):
        at = rows_of(b)
        new_x[at], new_r[at], p = update(total[at], iterate[at], residual[at], direction[at])
        new_p[at] = p
        both = pair(p)
        v[at] = both
        acc[at] = p * fold(dot(both, g, NN))
        return 0

    lax.fori_loop(0, UB, begin, 0, unroll=UNROLL)

    def work(b, block, w):
        at = rows_of(b)
        scores = fold(dot(v[at], by_cols(th[block], tl[block]), NN))
        acc[at] += w * scores * scores

    each_tile(order, weights, held, sem, work)
    for b in range(UB):
        squares[b : b + 1] = jnp.sum(acc[b * BLOCK : (b + 1) * BLOCK].T, axis=0, keepdims=True)


def last_kernel(squares, iterate, residual, direction, out):
    sums = squares[...]
    for b in range(UB):
        at = pl.ds(b * BLOCK, BLOCK)
        p = direction[at]
        r = residual[at]
        below = jnp.broadcast_to(sums[b : b + 1], (BLOCK, BLOCK)).T + RIDGE * dots(p, p)
        out[at] = iterate[at] + dots(r, r) / (below + EPSILON) * p


USERS = jax.ShapeDtypeStruct((UB * BLOCK, K), F32)


def local(kernel, name, outs, specs, scratch=()):
    tiles = [
        pltpu.VMEM((UB * BLOCK, 2 * K), BF16),
        *scratch,
        pltpu.VMEM((HELD, BLOCK, BLOCK), F32),
        pltpu.SemaphoreType.DMA((HELD,)),
    ]
    return pl.pallas_call(
        kernel,
        out_shape=outs,
        in_specs=specs,
        out_specs=tuple(VMEM for _ in outs),
        scratch_shapes=tiles,
        compiler_params=pltpu.CompilerParams(vmem_limit_bytes=BIG),
        name=name,
    )


def reduce_kernel(part, out, land, sums, near, send_sem, recv_sem):
    c, z, x, along_x, along_z = col_place()
    greet(along_x + along_z)
    copies = Copies(send_sem, recv_sem)
    send = copies.send
    streams = [(pl.ds(SUB * i, SUB), i % 2 == 0) for i in range(BLOCK // SUB)]

    def line(ref, way, d, rows):
        return ref.at[:, (x + d) % NX, rows] if way else ref.at[(z + d) % NZ, :, rows]

    def axes(way):
        return (along_x, along_z, z) if way else (along_z, along_x, x)

    far = [
        [send(line(part, way, d, rows), land.at[i, d - 1], axes(way)[0][d - 1]) for d in (1, 2, 3)]
        for i, (rows, way) in enumerate(streams)
    ]
    close = []
    for i, (rows, way) in enumerate(streams):
        _, along, me = axes(way)
        for copy in far[i]:
            copy.wait_recv()
        mine = part[:, x, rows] if way else part[z, :, rows]
        sums[i] = mine + land[i, 0] + (land[i, 1] + land[i, 2])
        close.append(
            [send(sums.at[i, (me + d) % 4], near.at[i, d - 1], along[d - 1]) for d in (1, 2, 3)]
        )
    back = []
    for i, (rows, way) in enumerate(streams):
        _, along, me = axes(way)
        for copy in close[i]:
            copy.wait_recv()
        out[z, x, rows] = sums[i, me] + near[i, 0] + (near[i, 1] + near[i, 2])
        here = out.at[z, x, rows]
        back.append([send(here, here, peer) for peer in along])
    end = []
    for i, (rows, way) in enumerate(streams):
        for copy in back[i]:
            copy.wait_recv()
        here = line(out, way, 0, rows)
        end += [send(here, here, peer) for peer in axes(way)[0]]
    for copy in end:
        copy.wait_recv()
    copies.finish()


def reduce(part):
    n = BLOCK // SUB
    out = pl.pallas_call(
        reduce_kernel,
        out_shape=jax.ShapeDtypeStruct((NZ, NX, BLOCK, K), F32),
        in_specs=[VMEM],
        out_specs=VMEM,
        scratch_shapes=[
            pltpu.VMEM((n, 3, 4, SUB, K), F32),
            pltpu.VMEM((n, 4, SUB, K), F32),
            pltpu.VMEM((n, 3, SUB, K), F32),
            pltpu.SemaphoreType.DMA((12 * n,)),
            pltpu.SemaphoreType.DMA((12 * n,)),
        ],
        compiler_params=pltpu.CompilerParams(
            collective_id=1, has_side_effects=True, vmem_limit_bytes=BIG
        ),
        name="reduce",
    )(part.reshape(NZ, NX, BLOCK, K))
    return out.reshape(UB * BLOCK, K)


def scalars_kernel(mine, out, land_x, land_z, half, send_sem, recv_sem):
    _, _, _, along_x, along_z = col_place()
    greet(along_x + along_z)
    copies = Copies(send_sem, recv_sem)
    for copy in [copies.send(mine, land_x.at[i], peer) for i, peer in enumerate(along_x)]:
        copy.wait_recv()
    half[...] = mine[...] + land_x[0] + (land_x[1] + land_x[2])
    for copy in [copies.send(half, land_z.at[i], peer) for i, peer in enumerate(along_z)]:
        copy.wait_recv()
    out[...] = half[...] + land_z[0] + (land_z[1] + land_z[2])
    copies.finish()


def sum_scalars(mine):
    return pl.pallas_call(
        scalars_kernel,
        out_shape=jax.ShapeDtypeStruct((UB, BLOCK), F32),
        in_specs=[VMEM],
        out_specs=VMEM,
        scratch_shapes=[
            pltpu.VMEM((3, UB, BLOCK), F32),
            pltpu.VMEM((3, UB, BLOCK), F32),
            pltpu.VMEM((UB, BLOCK), F32),
            pltpu.SemaphoreType.DMA((6,)),
            pltpu.SemaphoreType.DMA((6,)),
        ],
        compiler_params=pltpu.CompilerParams(collective_id=2, has_side_effects=True, vmem_limit_bytes=BIG),
        name="scalars",
    )(mine)


def cg_kernel(
    order, part, start, yh, yl, th, tl, gram, weights, out,
    held, v, x_now, r_now, p_now, pulls, squares, parts, tot, land, sums, near,
    row_sums, land_x, land_z, half, send_sem, recv_sem, w_sem,
):
    _, z, x, along_x, along_z = col_place()
    load = pltpu.make_async_copy(weights.at[pl.ds(0, FAST)], held, w_sem)
    load.start()
    greet(along_x + along_z)
    copies = Copies(send_sem, recv_sem)
    send = copies.send
    far, close, back, end = {}, {}, {}, {}
    rounds = (part, parts.at[0], parts.at[1])

    def streams(s):
        for i in range(4 * s, 4 * s + 4):
            way = i % 2 == 0
            first, second, me = (along_x, along_z, z) if way else (along_z, along_x, x)
            yield i, pl.ds(THIN * i, THIN), way, first, second, me

    def line(ref, way, d, rows):
        return ref.at[:, (x + d) % NX, rows] if way else ref.at[(z + d) % NZ, :, rows]

    def begin(k, s):
        for i, rows, way, first, _, _ in streams(s):
            far[k, i] = [
                send(line(rounds[k], way, d, rows), land.at[k, i, d - 1], first[d - 1])
                for d in (2, 1, 3)
            ]

    def sum_first(k, s):
        for i, rows, way, _, second, me in streams(s):
            for copy in far[k, i]:
                copy.wait_recv()
            mine = rounds[k][:, x, rows] if way else rounds[k][z, :, rows]
            sums[k, i] = mine + land[k, i, 0] + (land[k, i, 1] + land[k, i, 2])
            close[k, i] = [
                send(sums.at[k, i, (me + d) % 4], near.at[k, i, d - 1], second[d - 1])
                for d in (2, 1, 3)
            ]

    def sum_second(k, s):
        for i, rows, _, _, second, me in streams(s):
            for copy in close[k, i]:
                copy.wait_recv()
            tot[k, z, x, rows] = sums[k, i, me] + near[k, i, 0] + (near[k, i, 1] + near[k, i, 2])
            here = tot.at[k, z, x, rows]
            back[k, i] = [send(here, here, second[d]) for d in (1, 0, 2)]

    def spread(k, s):
        for i, rows, way, first, _, _ in streams(s):
            for copy in back[k, i]:
                copy.wait_recv()
            here = line(tot.at[k], way, 0, rows)
            end[k, i] = [send(here, here, first[d]) for d in (1, 0, 2)]

    def arrive(k, s):
        for i in range(4 * s, 4 * s + 4):
            for copy in end[k, i]:
                copy.wait_recv()

    g = by_cols(*split(gram[...]))
    n = order[LIST - 1]

    def compute(k, s, before_end):
        rows = pl.ds(64 * s, 64)

        def step(b, _):
            total = tot[k - 1, b // NX, b % NX, rows]
            if k == 1:
                p = total - RIDGE * start[b, rows]
                r_now[b, rows] = p
            else:
                before = start[b, rows] if k == 2 else x_now[b, rows]
                r = r_now[b, rows]
                old = r if k == 2 else p_now[b, rows]
                x_now[b, rows], r_now[b, rows], p = update(total, before, r, old)
            p_now[b, rows] = p
            v[b, rows] = pair(p)
            return 0

        lax.fori_loop(0, UB, step, 0, unroll=16)

        def some(q, acc):
            last_b, acc = acc
            for u in range(STEP):
                j = q * STEP + u
                code = order[j]
                b, block = code & (UB - 1), (code >> 4) & 63
                w = jnp.where(j < n, held[j, rows], 0.0)
                scores = fold(dot(v[b, rows], by_cols(th[block], tl[block]), NN))
                if k < 3:
                    pull = fold(dot(pair(w * scores), by_cols(yh[block], yl[block]), NN))
                else:
                    pull = w * scores * scores
                acc = jnp.where(b == last_b, acc, 0.0) + pull
                last_b = b
                pulls[s, j] = acc
            return last_b, acc

        lax.fori_loop(0, FAST // STEP, some, (jnp.int32(-1), jnp.zeros((64, K), F32)))
        before_end()

        def close_up(b, _):
            end_of = order[LAST + b]
            pulled = jnp.where(end_of >= 0, pulls[s, jnp.maximum(end_of, 0)], 0.0)
            whole = fold(dot(v[b, rows], g, NN))
            if k < 3:
                parts[k - 1, b // NX, b % NX, rows] = whole + pulled
            else:
                squares[b, rows] = p_now[b, rows] * whole + pulled
            return 0

        lax.fori_loop(0, UB, close_up, 0, unroll=16)
        if k == 3:
            for b in range(UB):
                row_sums[b : b + 1, 64 * s : 64 * s + 64] = jnp.sum(
                    squares[b, rows].T, axis=0, keepdims=True
                )

    def nothing():
        pass

    begin(0, 0)
    begin(0, 1)
    sum_first(0, 0)
    for k in range(3):
        sum_first(k, 1)
        for work in (sum_second, spread):
            work(k, 0)
            work(k, 1)
        if k == 0:
            load.wait()
        arrive(k, 0)
        compute(k + 1, 0, nothing)
        if k < 2:
            begin(k + 1, 0)
        arrive(k, 1)
        compute(k + 1, 1, functools.partial(sum_first, k + 1, 0) if k < 2 else nothing)
        if k < 2:
            begin(k + 1, 1)

    told = [send(row_sums, land_x.at[i], peer) for i, peer in enumerate(along_x)]
    for b in range(UB):
        p, r = p_now[b], r_now[b]
        rest = jnp.broadcast_to(RIDGE * dots(p, p) + EPSILON, (BLOCK, K))
        pulls[0, b] = rest[:64]
        pulls[1, b] = rest[64:]
        squares[b] = jnp.broadcast_to(dots(r, r), (BLOCK, K))
    for copy in told:
        copy.wait_recv()
    half[...] = row_sums[...] + land_x[0] + (land_x[1] + land_x[2])
    for copy in [send(half, land_z.at[i], peer) for i, peer in enumerate(along_z)]:
        copy.wait_recv()
    both = half[...] + land_z[0] + (land_z[1] + land_z[2])
    for b in range(UB):
        below = jnp.broadcast_to(both[b : b + 1], (BLOCK, BLOCK)).T
        rest = jnp.concatenate([pulls[0, b], pulls[1, b]], axis=0)
        out[b] = x_now[b] + squares[b] / (below + rest) * p_now[b]
    copies.finish()


def all_steps(order, part, start, yh, yl, th, tl, gram, weights):
    n = BLOCK // THIN
    copies = 3 * 12 * n + 6
    blocks = (UB, BLOCK, K)
    out = pl.pallas_call(
        cg_kernel,
        out_shape=jax.ShapeDtypeStruct(blocks, F32),
        in_specs=[SMEM] + [VMEM] * 7 + [ANY],
        out_specs=VMEM,
        scratch_shapes=[
            pltpu.VMEM((FAST, BLOCK, BLOCK), F32),
            pltpu.VMEM((UB, BLOCK, 2 * K), BF16),
            pltpu.VMEM(blocks, F32),
            pltpu.VMEM(blocks, F32),
            pltpu.VMEM(blocks, F32),
            pltpu.VMEM((2, FAST, 64, K), F32),
            pltpu.VMEM(blocks, F32),
            pltpu.VMEM((2, NZ, NX, BLOCK, K), F32),
            pltpu.VMEM((3, NZ, NX, BLOCK, K), F32),
            pltpu.VMEM((3, n, 3, 4, THIN, K), F32),
            pltpu.VMEM((3, n, 4, THIN, K), F32),
            pltpu.VMEM((3, n, 3, THIN, K), F32),
            pltpu.VMEM((UB, BLOCK), F32),
            pltpu.VMEM((3, UB, BLOCK), F32),
            pltpu.VMEM((3, UB, BLOCK), F32),
            pltpu.VMEM((UB, BLOCK), F32),
            pltpu.SemaphoreType.DMA((copies,)),
            pltpu.SemaphoreType.DMA((copies,)),
            pltpu.SemaphoreType.DMA,
        ],
        compiler_params=pltpu.CompilerParams(
            collective_id=3, has_side_effects=True, vmem_limit_bytes=WHOLE
        ),
        name="steps",
    )(order, part.reshape(NZ, NX, BLOCK, K), start.reshape(blocks), yh, yl, th, tl, gram, weights)
    return out.reshape(UB * BLOCK, K)


def step_by_step(order, part, start, yh, yl, th, tl, gram, weights):
    total = reduce(part)
    tail = [VMEM] * 5 + [ANY]
    part, residual = local(first_kernel, "first", (USERS,) * 2, [SMEM, VMEM, VMEM] + tail)(
        order, total, start, yh, yl, th, tl, gram, weights
    )
    total = reduce(part)
    part, iterate, residual, direction = local(
        second_kernel, "second", (USERS,) * 4, [SMEM] + [VMEM] * 3 + tail
    )(order, total, start, residual, yh, yl, th, tl, gram, weights)
    total = reduce(part)
    squares = jax.ShapeDtypeStruct((UB, BLOCK), F32)
    part, iterate, residual, direction = local(
        third_kernel,
        "third",
        (squares,) + (USERS,) * 3,
        [SMEM] + [VMEM] * 4 + tail,
        [pltpu.VMEM((UB * BLOCK, K), F32)],
    )(order, total, iterate, residual, direction, yh, yl, th, tl, gram, weights)
    squares = sum_scalars(part)
    return pl.pallas_call(
        last_kernel,
        out_shape=USERS,
        in_specs=[VMEM] * 4,
        out_specs=VMEM,
        compiler_params=pltpu.CompilerParams(vmem_limit_bytes=BIG),
        name="last",
    )(squares, iterate, residual, direction)


def shards(user_factors, item_factors, fetch_list, tile_user, tile_slot, er, ec, en, tile_count):
    yh, yl, th, tl, gram, ent, peak = gather(
        item_factors.reshape(IB, BLOCK, K),
        fetch_list.reshape(1, 128),
        tile_user.reshape(1, TILES),
        tile_slot.reshape(1, TILES),
        er.reshape(TILES, NNZ),
        ec.reshape(TILES, NNZ),
        en.reshape(TILES, NNZ),
        tile_count.reshape(1, 1),
    )
    part, weights, order, fits = build(
        ent.reshape(COLS, STAGE, NNZ), yh, yl, th, tl, gram, user_factors, peak
    )
    return lax.cond(
        fits[0] > 0,
        all_steps,
        step_by_step,
        order, part, user_factors, yh, yl, th, tl, gram, weights,
    )


def solution(mesh):
    return jax.shard_map(
        shards,
        mesh=mesh,
        in_specs=(
            P("row", None),
            P(("row", "col"), None),
            P("row", "col", None, None),
            P("row", "col", None),
            P("row", "col", None),
            P("row", "col", None, None),
            P("row", "col", None, None),
            P("row", "col", None, None),
            P("row", "col"),
        ),
        out_specs=P("row", None),
        check_vma=False,
    )
```

```python
import functools

import jax
import jax.numpy as jnp
from jax import lax
from jax.experimental import pallas as pl
from jax.experimental.pallas import tpu as pltpu
from jax.sharding import PartitionSpec as P

K = 128
BLOCK = 128
UB = 16
IB = 8
TILES = 32
NNZ = 512
NZ = NX = 4
NY = 4
ROWS = 8
COLS = 16
ALL_TILES = COLS * TILES
LIST = 1024
LAST = 512
FAST = 36
STEP = 36
SUB = 32
THIN = 16
UNROLL = 4
BUILD = 4
SLOTS = 2 * BUILD
GROUP = 4
HELD = 32
STAGE = 3 * TILES + 8
HALF = 56
SCALE = 40.0
RIDGE = 0.5
EPSILON = 1e-06
MESH = pl.DeviceIdType.MESH
F32 = jnp.float32
BF16 = jnp.bfloat16
NT = (((1,), (1,)), ((), ()))
NN = (((1,), (0,)), ((), ()))
ANY = pl.BlockSpec(memory_space=pl.ANY)
VMEM = pl.BlockSpec(memory_space=pltpu.VMEM)
SMEM = pl.BlockSpec(memory_space=pltpu.SMEM)
HBM = pl.BlockSpec(memory_space=pltpu.HBM)
BIG = 24 * 2**20
WHOLE = 40 * 2**20


def dot(a, b, dims):
    return lax.dot_general(a, b, dims, preferred_element_type=F32)


def split(a):
    high = a.astype(BF16)
    return high, (a - high.astype(F32)).astype(BF16)


def pair(a):
    return jnp.concatenate(split(a), axis=1)


def fold(wide):
    return wide[:, 0:128] + wide[:, 128:256]


def by_cols(high, low):
    both = jnp.concatenate([high, low], axis=1)
    return jnp.concatenate([both, both], axis=0)


def greet(peers):
    barrier = pltpu.get_barrier_semaphore()
    for peer in peers:
        pl.semaphore_signal(barrier, inc=1, device_id=peer, device_id_type=MESH)
    pl.semaphore_wait(barrier, len(peers))


class Copies:
    def __init__(self, send_sem, recv_sem):
        self.send_sem, self.recv_sem, self.made = send_sem, recv_sem, []

    def send(self, src, dst, peer):
        i = len(self.made)
        copy = pltpu.make_async_remote_copy(
            src_ref=src,
            dst_ref=dst,
            send_sem=self.send_sem.at[i],
            recv_sem=self.recv_sem.at[i],
            device_id=peer,
            device_id_type=MESH,
        )
        copy.start()
        self.made.append(copy)
        return copy

    def finish(self):
        for copy in self.made:
            copy.wait_send()


def col_place():
    c = lax.axis_index("col")
    z, x = c // NX, c % NX
    along_x = [{"col": z * NX + (x + d) % NX} for d in range(1, NX)]
    along_z = [{"col": ((z + d) % NZ) * NX + x} for d in range(1, NZ)]
    return c, z, x, along_x, along_z


def gather_kernel(
    items, fetch, user, slot, er, ec, en, count, yh, yl, th, tl, gram, ent, peak,
    stage, land, fetch_in, slot_in, user_in, small, keys, most, seen, send_sem, recv_sem, own_sem, in_sem,
):
    c, z, x, along_x, along_z = col_place()
    r = lax.axis_index("row")
    y, core = r // 2, r % 2
    right, left, across = (((y + d) % NY) * 2 + core for d in (1, 3, 2))
    other = y * 2 + 1 - core
    to_right, to_left, to_other = {"row": right}, {"row": left}, {"row": other}
    to_across = {"row": across}
    loads = [
        pltpu.make_async_copy(src, dst, in_sem.at[i])
        for i, (src, dst) in enumerate(
            (
                (er, stage.at[pl.ds(0, TILES)]),
                (ec, stage.at[pl.ds(TILES, TILES)]),
                (en, stage.at[pl.ds(2 * TILES, TILES)]),
                (items, land.at[r]),
                (fetch, fetch_in),
                (slot, slot_in),
                (user, user_in),
            )
        )
    ]
    for load in loads:
        load.start()
    greet(along_x + along_z + [to_right, to_left, to_across, to_other])
    copies = Copies(send_sem, recv_sem)
    send = copies.send
    half = [items.at[pl.ds(4 * i, 4)] for i in (0, 1)]
    there = [land.at[r, pl.ds(4 * i, 4)] for i in (0, 1)]
    from_left, from_right = [None, None], [None, None]
    for i in (0, 1):
        from_left[i] = send(half[i], there[i], to_right)
        from_right[1 - i] = send(half[1 - i], there[1 - i], to_left)
    between = [send(items, land.at[r], to_other)]

    for load in loads[4:]:
        load.wait()
    small[...] = jnp.zeros_like(small)
    small[0:1, 0:TILES] = slot_in[...]
    small[1:2, 0:TILES] = user_in[...]
    slots = small[0:1]
    table = jnp.broadcast_to(fetch_in[...].astype(F32), (128, 128)).T
    ids = lax.broadcasted_iota(jnp.int32, (128, 128), 0)
    local_id = jnp.sum(jnp.where(ids == slots, table, 0.0), axis=0, keepdims=True).astype(jnp.int32)
    lanes = lax.broadcasted_iota(jnp.int32, (1, 128), 1)
    last = 3 * TILES
    stage[last : last + 1, 0:128] = jnp.where(lanes < count[0, 0], slots & (COLS - 1), -1)
    stage[last + 1 : last + 2, 0:128] = ((slots >> 4) * IB + local_id) * UB + small[1:2]
    first_key = stage[last : last + 1, 0:128]
    keys[z, x] = jnp.broadcast_to(first_key, (8, 128))
    for load in loads[:3]:
        load.wait()
    own = pltpu.make_async_copy(stage, ent.at[z, x], own_sem)
    own.start()

    first, second = pl.ds(0, HALF), pl.ds(HALF, STAGE - HALF)
    parts = (pl.ds(0, 32), pl.ds(32, 24)), (pl.ds(56, 24), pl.ds(80, 24))
    ways = (
        (first, along_x, along_z, lambda d, e: ent.at[(z + e) % NZ, (x + d) % NX]),
        (second, along_z, along_x, lambda d, e: ent.at[(z + d) % NZ, (x + e) % NX]),
    )
    near = [[None] * 4, [None] * 4]
    up = [[None] * 4, [None] * 4]
    down = [[None] * 4, [None] * 4]

    def spread(w, d, source):
        rows, _, across_way, at = ways[w]
        to = at(-d, 0).at[rows]
        up[w][d] = send(source, to, across_way[0])
        down[w][d] = send(source, to, across_way[2])

    for w, (rows, along, _, at) in enumerate(ways):
        for d in (1, 3, 2):
            near[w][d] = send(stage.at[rows], at(0, 0).at[rows], along[d - 1])
        spread(w, 0, stage.at[rows])
    mine = keys.at[z, x]
    told_keys = [send(mine, mine, peer) for peer in along_x]

    far = []

    def pass_on(w, d):
        _, _, across_way, at = ways[w]
        up[w][d].wait_recv()
        piece = at(-d, -1).at[parts[w][0]]
        far.append(send(piece, piece, across_way[0]))
        down[w][d].wait_recv()
        piece = at(-d, 1).at[parts[w][1]]
        far.append(send(piece, piece, across_way[2]))

    def add(row, sums):
        def one(i, sums):
            high, low = split(land[row, i])
            high_t = high.T
            at = row * IB + i
            yh[at] = high
            yl[at] = low
            th[at] = high_t
            tl[at] = low.T
            return sums + dot(high_t, jnp.concatenate([high, low], axis=1), NN)

        return lax.fori_loop(0, IB, one, sums, unroll=8)

    loads[3].wait()
    sums = add(r, jnp.zeros((K, 2 * K), F32))
    for d in (1, 3, 2):
        for w in (0, 1):
            near[w][d].wait_recv()
            rows, _, _, at = ways[w]
            spread(w, d, at(-d, 0).at[rows])
    for copy in told_keys:
        copy.wait_recv()
    mine = keys.at[z]
    told_keys = [send(mine, mine, peer) for peer in along_z]
    for w in (0, 1):
        pass_on(w, 0)
    from_left[0].wait_recv()
    piece = land.at[left, pl.ds(0, 4)]
    round_y = [send(piece, piece, to_right)]
    from_right[1].wait_recv()
    piece = land.at[right, pl.ds(4, 4)]
    round_y.append(send(piece, piece, to_left))
    between[0].wait_recv()
    sums = add(other, sums)
    for d in (1, 3):
        for w in (0, 1):
            pass_on(w, d)
    from_left[1].wait_recv()
    between.append(send(land.at[left], land.at[left], to_other))
    from_right[0].wait_recv()
    between.append(send(land.at[right], land.at[right], to_other))
    for w in (0, 1):
        pass_on(w, 2)
    for copy in told_keys:
        copy.wait_recv()
    owners = keys[:, :, 0, :].reshape(COLS, 128)
    counted = [
        jnp.sum(jnp.where(owners == column, 1.0, 0.0), axis=0, keepdims=True)
        for column in range(COLS)
    ]
    counted = jnp.sum(jnp.concatenate(counted, axis=0), axis=1, keepdims=True)
    longest = jnp.max(counted, axis=0, keepdims=True).astype(jnp.int32)
    most[0] = jnp.broadcast_to(longest, (8, 128))

    told = [
        send(most.at[0], seen.at[i], peer)
        for i, peer in enumerate((to_right, to_left, to_across))
    ]
    sums = add(left, sums)
    sums = add(right, sums)
    for copy in told:
        copy.wait_recv()
    most[1] = jnp.maximum(jnp.maximum(most[0], seen[0]), jnp.maximum(seen[1], seen[2]))
    told = send(most.at[1], seen.at[3], to_other)
    for copy in round_y:
        copy.wait_recv()
    between.append(send(land.at[across], land.at[across], to_other))
    sums = add(across, sums)
    for copy, d in zip(between[1:], (3, 1, 2)):
        copy.wait_recv()
        sums = add(((y + d) % NY) * 2 + 1 - core, sums)
    told.wait_recv()
    peak[...] = jnp.maximum(most[1], seen[3])
    for copy in far:
        copy.wait_recv()
    own.wait()
    mixed = sums[:, K:]
    gram[...] = sums[:, :K] + (mixed + mixed.T)
    copies.finish()


def gather(items, fetch, user, slot, er, ec, en, count):
    n = 6 + 4 + 2 * (3 + 8 + 8) + 10
    return pl.pallas_call(
        gather_kernel,
        out_shape=(
            *[jax.ShapeDtypeStruct((ROWS * IB, BLOCK, K), BF16)] * 4,
            jax.ShapeDtypeStruct((K, K), F32),
            jax.ShapeDtypeStruct((NZ, NX, STAGE, NNZ), jnp.int32),
            jax.ShapeDtypeStruct((8, 128), jnp.int32),
        ),
        in_specs=[HBM] * 7 + [SMEM],
        out_specs=(VMEM, VMEM, VMEM, VMEM, VMEM, ANY, VMEM),
        scratch_shapes=[
            pltpu.VMEM((STAGE, NNZ), jnp.int32),
            pltpu.VMEM((ROWS, IB, BLOCK, K), F32),
            pltpu.VMEM((1, 128), jnp.int32),
            pltpu.VMEM((1, TILES), jnp.int32),
            pltpu.VMEM((1, TILES), jnp.int32),
            pltpu.VMEM((8, 128), jnp.int32),
            pltpu.VMEM((NZ, NX, 8, 128), jnp.int32),
            pltpu.VMEM((2, 8, 128), jnp.int32),
            pltpu.VMEM((4, 8, 128), jnp.int32),
            pltpu.SemaphoreType.DMA((n,)),
            pltpu.SemaphoreType.DMA((n,)),
            pltpu.SemaphoreType.DMA,
            pltpu.SemaphoreType.DMA((7,)),
        ],
        compiler_params=pltpu.CompilerParams(
            collective_id=0, has_side_effects=True, vmem_limit_bytes=BIG
        ),
        name="gather",
    )(*[pltpu.with_memory_space_constraint(a, pltpu.HBM) for a in (items, fetch, user, slot, er, ec, en)], count)


def build_kernel(
    ent, yh, yl, th, tl, gram, start, peak, out, weights, order, fits, meta, found, place, held, v, sem, meta_sem
):
    fetched = pltpu.make_async_copy(
        ent.at[:, pl.ds(3 * TILES, 8), pl.ds(0, 128)], meta, meta_sem
    )
    fetched.start()
    g = by_cols(*split(gram[...]))

    def begin(b, _):
        at = rows_of(b)
        both = pair(start[at])
        v[at] = both
        out[at] = -fold(dot(both, g, NN))
        return 0

    lax.fori_loop(0, UB, begin, 0, unroll=UNROLL)
    fits[0] = jnp.where(jnp.max(peak[...].astype(F32)) <= FAST, 1, 0)
    fetched.wait()
    me = lax.axis_index("col")

    def scan(c, n):
        for t in range(TILES):
            found[n] = (c * TILES + t) * (64 * UB) + meta[c, 1, t]
            n = n + jnp.where(meta[c, 0, t] == me, 1, 0)
        return n

    n = lax.fori_loop(0, COLS, scan, 0)
    order[LIST - 1] = n

    for b in range(UB):
        place[b] = 0

    def count(j, _):
        b = found[j] & (UB - 1)
        place[b] = place[b] + 1
        return 0

    lax.fori_loop(0, n, count, 0)
    total = 0
    for b in range(UB):
        of_b = place[b]
        order[LAST + b] = jnp.where(of_b > 0, total + of_b - 1, -1)
        place[b] = total
        total = total + of_b

    def put(j, _):
        code = found[j]
        b = code & (UB - 1)
        to = place[b]
        order[to] = code
        place[b] = to + 1
        return 0

    lax.fori_loop(0, n, put, 0)
    ids = lax.broadcasted_iota(jnp.int32, (BLOCK, NNZ), 0)
    one, none = jnp.ones((), BF16), jnp.zeros((), BF16)

    def out_copy(j):
        slot = j % SLOTS
        return pltpu.make_async_copy(held.at[slot], weights.at[j], sem.at[slot])

    def group(q, _):
        for u in range(BUILD):
            j = q * BUILD + u

            @pl.when((j >= SLOTS) & (j - SLOTS < n))
            def _(j=j):
                out_copy(j - SLOTS).wait()

        made = []
        for u in range(BUILD):
            j = q * BUILD + u
            code = jnp.where(j < n, order[j], 0)
            b, block, at = code % UB, (code // UB) % 64, code // (64 * UB)
            c, t = at // TILES, at % TILES
            rows = jnp.where(j < n, ent[c, pl.ds(t, 1), :], BLOCK)
            cols = ent[c, pl.ds(TILES + t, 1), :]
            counts = ent[c, pl.ds(2 * TILES + t, 1), :].astype(F32)
            in_col = ids == cols
            once = jnp.where(in_col, 1.0, 0.0).astype(BF16)
            ones = jnp.where(ids == rows, 1.0, 0.0).astype(BF16)
            many = jnp.where(in_col, counts, 0.0).astype(BF16)
            both = dot(ones, jnp.concatenate([once, many], axis=0), NT)
            times, excess = both[:, :BLOCK], SCALE * both[:, BLOCK:]
            made.append((rows_of(b), block, times, excess))
        scores = [
            fold(dot(v[where], by_cols(th[block], tl[block]), NN)) for where, block, _, _ in made
        ]
        pulls = [
            fold(
                dot(pair(times + excess * (1.0 - score)), by_cols(yh[block], yl[block]), NN)
            )
            for (_, block, times, excess), score in zip(made, scores)
        ]
        for u, ((where, _, _, excess), pull) in enumerate(zip(made, pulls)):
            held[(q * BUILD + u) % SLOTS] = excess
            out[where] += pull
        for u in range(BUILD):
            j = q * BUILD + u

            @pl.when(j < n)
            def _(j=j):
                out_copy(j).start()

        return 0

    groups = (n + BUILD - 1) // BUILD
    lax.fori_loop(0, groups, group, 0)

    def drain(j, _):
        out_copy(j).wait()
        return 0

    lax.fori_loop(jnp.maximum(groups * BUILD - SLOTS, 0), n, drain, 0)


def build(ent, yh, yl, th, tl, gram, start, peak):
    return pl.pallas_call(
        build_kernel,
        out_shape=(
            jax.ShapeDtypeStruct((UB * BLOCK, K), F32),
            jax.ShapeDtypeStruct((ALL_TILES, BLOCK, BLOCK), F32),
            jax.ShapeDtypeStruct((LIST,), jnp.int32),
            jax.ShapeDtypeStruct((1,), jnp.int32),
        ),
        in_specs=[VMEM] * 8,
        out_specs=(VMEM, ANY, SMEM, SMEM),
        scratch_shapes=[
            pltpu.SMEM((COLS, 8, 128), jnp.int32),
            pltpu.SMEM((LIST,), jnp.int32),
            pltpu.SMEM((UB,), jnp.int32),
            pltpu.VMEM((SLOTS, BLOCK, BLOCK), F32),
            pltpu.VMEM((UB * BLOCK, 2 * K), BF16),
            pltpu.SemaphoreType.DMA((SLOTS,)),
            pltpu.SemaphoreType.DMA,
        ],
        compiler_params=pltpu.CompilerParams(vmem_limit_bytes=BIG),
        name="build",
    )(ent, yh, yl, th, tl, gram, start, peak)


def fetch_tiles(order, weights, held, sem, base):
    here = jnp.minimum(order[LIST - 1] - base, HELD)

    def begin(i, _):
        pltpu.make_async_copy(weights.at[base + i], held.at[i], sem.at[i]).start()
        return 0

    lax.fori_loop(0, here, begin, 0)
    return here


def each_tile(order, weights, held, sem, work):
    n = order[LIST - 1]

    def batch(k, _):
        base = k * HELD
        here = jnp.minimum(n - base, HELD)

        def group(q, _):
            for u in range(GROUP):
                i = q * GROUP + u

                @pl.when(i < here)
                def _(i=i):
                    pltpu.make_async_copy(weights.at[base + i], held.at[i], sem.at[i]).wait()

            for u in range(GROUP):
                i = q * GROUP + u
                live = i < here
                code = jnp.where(live, order[base + i], 0)
                w = jnp.where(live, held[i], 0.0)
                work(code % UB, (code // UB) % 64, w)
            return 0

        lax.fori_loop(0, (here + GROUP - 1) // GROUP, group, 0)

        @pl.when(n > base + HELD)
        def _():
            fetch_tiles(order, weights, held, sem, base + HELD)

        return 0

    lax.fori_loop(0, (n + HELD - 1) // HELD, batch, 0)


def rows_of(b):
    return pl.ds(pl.multiple_of(b * BLOCK, BLOCK), BLOCK)


def dots(a, b):
    return jnp.sum(a * b, axis=1, keepdims=True)


def pull_tiles(order, weights, held, sem, yh, yl, th, tl, v, out):
    def work(b, block, w):
        at = rows_of(b)
        scores = fold(dot(v[at], by_cols(th[block], tl[block]), NN))
        out[at] += fold(dot(pair(w * scores), by_cols(yh[block], yl[block]), NN))

    each_tile(order, weights, held, sem, work)


def first_kernel(order, total, start, yh, yl, th, tl, gram, weights, out, residual, v, held, sem):
    fetch_tiles(order, weights, held, sem, 0)
    g = by_cols(*split(gram[...]))

    def begin(b, _):
        at = rows_of(b)
        p = total[at] - RIDGE * start[at]
        residual[at] = p
        both = pair(p)
        v[at] = both
        out[at] = fold(dot(both, g, NN))
        return 0

    lax.fori_loop(0, UB, begin, 0, unroll=UNROLL)
    pull_tiles(order, weights, held, sem, yh, yl, th, tl, v, out)


def update(total, iterate, residual, direction):
    image = total + RIDGE * direction
    now = dots(residual, residual)
    alpha = now / (dots(direction, image) + EPSILON)
    iterate = iterate + alpha * direction
    residual = residual - alpha * image
    after = dots(residual, residual)
    direction = residual + after / (now + EPSILON) * direction
    return iterate, residual, direction


def second_kernel(
    order, total, iterate, residual, yh, yl, th, tl, gram, weights, out, new_x, new_r, new_p, v, held, sem
):
    fetch_tiles(order, weights, held, sem, 0)
    g = by_cols(*split(gram[...]))

    def begin(b, _):
        at = rows_of(b)
        r = residual[at]
        new_x[at], new_r[at], p = update(total[at], iterate[at], r, r)
        new_p[at] = p
        both = pair(p)
        v[at] = both
        out[at] = fold(dot(both, g, NN))
        return 0

    lax.fori_loop(0, UB, begin, 0, unroll=UNROLL)
    pull_tiles(order, weights, held, sem, yh, yl, th, tl, v, out)


def third_kernel(
    order, total, iterate, residual, direction, yh, yl, th, tl, gram, weights,
    squares, new_x, new_r, new_p, v, acc, held, sem,
):
    fetch_tiles(order, weights, held, sem, 0)
    g = by_cols(*split(gram[...]))

    def begin(b, _):
        at = rows_of(b)
        new_x[at], new_r[at], p = update(total[at], iterate[at], residual[at], direction[at])
        new_p[at] = p
        both = pair(p)
        v[at] = both
        acc[at] = p * fold(dot(both, g, NN))
        return 0

    lax.fori_loop(0, UB, begin, 0, unroll=UNROLL)

    def work(b, block, w):
        at = rows_of(b)
        scores = fold(dot(v[at], by_cols(th[block], tl[block]), NN))
        acc[at] += w * scores * scores

    each_tile(order, weights, held, sem, work)
    for b in range(UB):
        squares[b : b + 1] = jnp.sum(acc[b * BLOCK : (b + 1) * BLOCK].T, axis=0, keepdims=True)


def last_kernel(squares, iterate, residual, direction, out):
    sums = squares[...]
    for b in range(UB):
        at = pl.ds(b * BLOCK, BLOCK)
        p = direction[at]
        r = residual[at]
        below = jnp.broadcast_to(sums[b : b + 1], (BLOCK, BLOCK)).T + RIDGE * dots(p, p)
        out[at] = iterate[at] + dots(r, r) / (below + EPSILON) * p


USERS = jax.ShapeDtypeStruct((UB * BLOCK, K), F32)


def local(kernel, name, outs, specs, scratch=()):
    tiles = [
        pltpu.VMEM((UB * BLOCK, 2 * K), BF16),
        *scratch,
        pltpu.VMEM((HELD, BLOCK, BLOCK), F32),
        pltpu.SemaphoreType.DMA((HELD,)),
    ]
    return pl.pallas_call(
        kernel,
        out_shape=outs,
        in_specs=specs,
        out_specs=tuple(VMEM for _ in outs),
        scratch_shapes=tiles,
        compiler_params=pltpu.CompilerParams(vmem_limit_bytes=BIG),
        name=name,
    )


def reduce_kernel(part, out, land, sums, near, send_sem, recv_sem):
    c, z, x, along_x, along_z = col_place()
    greet(along_x + along_z)
    copies = Copies(send_sem, recv_sem)
    send = copies.send
    streams = [(pl.ds(SUB * i, SUB), i % 2 == 0) for i in range(BLOCK // SUB)]

    def line(ref, way, d, rows):
        return ref.at[:, (x + d) % NX, rows] if way else ref.at[(z + d) % NZ, :, rows]

    def axes(way):
        return (along_x, along_z, z) if way else (along_z, along_x, x)

    far = [
        [send(line(part, way, d, rows), land.at[i, d - 1], axes(way)[0][d - 1]) for d in (1, 2, 3)]
        for i, (rows, way) in enumerate(streams)
    ]
    close = []
    for i, (rows, way) in enumerate(streams):
        _, along, me = axes(way)
        for copy in far[i]:
            copy.wait_recv()
        mine = part[:, x, rows] if way else part[z, :, rows]
        sums[i] = mine + land[i, 0] + (land[i, 1] + land[i, 2])
        close.append(
            [send(sums.at[i, (me + d) % 4], near.at[i, d - 1], along[d - 1]) for d in (1, 2, 3)]
        )
    back = []
    for i, (rows, way) in enumerate(streams):
        _, along, me = axes(way)
        for copy in close[i]:
            copy.wait_recv()
        out[z, x, rows] = sums[i, me] + near[i, 0] + (near[i, 1] + near[i, 2])
        here = out.at[z, x, rows]
        back.append([send(here, here, peer) for peer in along])
    end = []
    for i, (rows, way) in enumerate(streams):
        for copy in back[i]:
            copy.wait_recv()
        here = line(out, way, 0, rows)
        end += [send(here, here, peer) for peer in axes(way)[0]]
    for copy in end:
        copy.wait_recv()
    copies.finish()


def reduce(part):
    n = BLOCK // SUB
    out = pl.pallas_call(
        reduce_kernel,
        out_shape=jax.ShapeDtypeStruct((NZ, NX, BLOCK, K), F32),
        in_specs=[VMEM],
        out_specs=VMEM,
        scratch_shapes=[
            pltpu.VMEM((n, 3, 4, SUB, K), F32),
            pltpu.VMEM((n, 4, SUB, K), F32),
            pltpu.VMEM((n, 3, SUB, K), F32),
            pltpu.SemaphoreType.DMA((12 * n,)),
            pltpu.SemaphoreType.DMA((12 * n,)),
        ],
        compiler_params=pltpu.CompilerParams(
            collective_id=1, has_side_effects=True, vmem_limit_bytes=BIG
        ),
        name="reduce",
    )(part.reshape(NZ, NX, BLOCK, K))
    return out.reshape(UB * BLOCK, K)


def scalars_kernel(mine, out, land_x, land_z, half, send_sem, recv_sem):
    _, _, _, along_x, along_z = col_place()
    greet(along_x + along_z)
    copies = Copies(send_sem, recv_sem)
    for copy in [copies.send(mine, land_x.at[i], peer) for i, peer in enumerate(along_x)]:
        copy.wait_recv()
    half[...] = mine[...] + land_x[0] + (land_x[1] + land_x[2])
    for copy in [copies.send(half, land_z.at[i], peer) for i, peer in enumerate(along_z)]:
        copy.wait_recv()
    out[...] = half[...] + land_z[0] + (land_z[1] + land_z[2])
    copies.finish()


def sum_scalars(mine):
    return pl.pallas_call(
        scalars_kernel,
        out_shape=jax.ShapeDtypeStruct((UB, BLOCK), F32),
        in_specs=[VMEM],
        out_specs=VMEM,
        scratch_shapes=[
            pltpu.VMEM((3, UB, BLOCK), F32),
            pltpu.VMEM((3, UB, BLOCK), F32),
            pltpu.VMEM((UB, BLOCK), F32),
            pltpu.SemaphoreType.DMA((6,)),
            pltpu.SemaphoreType.DMA((6,)),
        ],
        compiler_params=pltpu.CompilerParams(collective_id=2, has_side_effects=True, vmem_limit_bytes=BIG),
        name="scalars",
    )(mine)


def cg_kernel(
    order, part, start, yh, yl, th, tl, gram, weights, out,
    held, v, x_now, r_now, p_now, pulls, squares, parts, tot, land, sums, near,
    row_sums, land_x, land_z, half, send_sem, recv_sem, w_sem,
):
    _, z, x, along_x, along_z = col_place()
    load = pltpu.make_async_copy(weights.at[pl.ds(0, FAST)], held, w_sem)
    load.start()
    greet(along_x + along_z)
    copies = Copies(send_sem, recv_sem)
    send = copies.send
    far, close, back, end = {}, {}, {}, {}
    rounds = (part, parts.at[0], parts.at[1])

    def streams(s):
        for i in range(4 * s, 4 * s + 4):
            way = i % 2 == 0
            first, second, me = (along_x, along_z, z) if way else (along_z, along_x, x)
            yield i, pl.ds(THIN * i, THIN), way, first, second, me

    def line(ref, way, d, rows):
        return ref.at[:, (x + d) % NX, rows] if way else ref.at[(z + d) % NZ, :, rows]

    def begin(k, s):
        for i, rows, way, first, _, _ in streams(s):
            far[k, i] = [
                send(line(rounds[k], way, d, rows), land.at[k, i, d - 1], first[d - 1])
                for d in (2, 1, 3)
            ]

    def sum_first(k, s):
        for i, rows, way, _, second, me in streams(s):
            for copy in far[k, i]:
                copy.wait_recv()
            mine = rounds[k][:, x, rows] if way else rounds[k][z, :, rows]
            sums[k, i] = mine + land[k, i, 0] + (land[k, i, 1] + land[k, i, 2])
            close[k, i] = [
                send(sums.at[k, i, (me + d) % 4], near.at[k, i, d - 1], second[d - 1])
                for d in (2, 1, 3)
            ]

    def sum_second(k, s):
        for i, rows, _, _, second, me in streams(s):
            for copy in close[k, i]:
                copy.wait_recv()
            tot[k, z, x, rows] = sums[k, i, me] + near[k, i, 0] + (near[k, i, 1] + near[k, i, 2])
            here = tot.at[k, z, x, rows]
            back[k, i] = [send(here, here, second[d]) for d in (1, 0, 2)]

    def spread(k, s):
        for i, rows, way, first, _, _ in streams(s):
            for copy in back[k, i]:
                copy.wait_recv()
            here = line(tot.at[k], way, 0, rows)
            end[k, i] = [send(here, here, first[d]) for d in (1, 0, 2)]

    def arrive(k, s):
        for i in range(4 * s, 4 * s + 4):
            for copy in end[k, i]:
                copy.wait_recv()

    g = by_cols(*split(gram[...]))
    n = order[LIST - 1]

    def compute(k, s, before_end):
        rows = pl.ds(64 * s, 64)

        def step(b, _):
            total = tot[k - 1, b // NX, b % NX, rows]
            if k == 1:
                p = total - RIDGE * start[b, rows]
                r_now[b, rows] = p
            else:
                before = start[b, rows] if k == 2 else x_now[b, rows]
                r = r_now[b, rows]
                old = r if k == 2 else p_now[b, rows]
                x_now[b, rows], r_now[b, rows], p = update(total, before, r, old)
            p_now[b, rows] = p
            v[b, rows] = pair(p)
            return 0

        lax.fori_loop(0, UB, step, 0, unroll=16)

        def some(q, acc):
            last_b, acc = acc
            for u in range(STEP):
                j = q * STEP + u
                code = order[j]
                b, block = code & (UB - 1), (code >> 4) & 63
                w = jnp.where(j < n, held[j, rows], 0.0)
                scores = fold(dot(v[b, rows], by_cols(th[block], tl[block]), NN))
                if k < 3:
                    pull = fold(dot(pair(w * scores), by_cols(yh[block], yl[block]), NN))
                else:
                    pull = w * scores * scores
                acc = jnp.where(b == last_b, acc, 0.0) + pull
                last_b = b
                pulls[s, j] = acc
            return last_b, acc

        lax.fori_loop(0, FAST // STEP, some, (jnp.int32(-1), jnp.zeros((64, K), F32)))
        before_end()

        def close_up(b, _):
            end_of = order[LAST + b]
            pulled = jnp.where(end_of >= 0, pulls[s, jnp.maximum(end_of, 0)], 0.0)
            whole = fold(dot(v[b, rows], g, NN))
            if k < 3:
                parts[k - 1, b // NX, b % NX, rows] = whole + pulled
            else:
                squares[b, rows] = p_now[b, rows] * whole + pulled
            return 0

        lax.fori_loop(0, UB, close_up, 0, unroll=16)
        if k == 3:
            for b in range(UB):
                row_sums[b : b + 1, 64 * s : 64 * s + 64] = jnp.sum(
                    squares[b, rows].T, axis=0, keepdims=True
                )

    def nothing():
        pass

    begin(0, 0)
    begin(0, 1)
    sum_first(0, 0)
    for k in range(3):
        sum_first(k, 1)
        for work in (sum_second, spread):
            work(k, 0)
            work(k, 1)
        if k == 0:
            load.wait()
        arrive(k, 0)
        compute(k + 1, 0, nothing)
        if k < 2:
            begin(k + 1, 0)
        arrive(k, 1)
        compute(k + 1, 1, functools.partial(sum_first, k + 1, 0) if k < 2 else nothing)
        if k < 2:
            begin(k + 1, 1)

    told = [send(row_sums, land_x.at[i], peer) for i, peer in enumerate(along_x)]
    for b in range(UB):
        p, r = p_now[b], r_now[b]
        rest = jnp.broadcast_to(RIDGE * dots(p, p) + EPSILON, (BLOCK, K))
        pulls[0, b] = rest[:64]
        pulls[1, b] = rest[64:]
        squares[b] = jnp.broadcast_to(dots(r, r), (BLOCK, K))
    for copy in told:
        copy.wait_recv()
    half[...] = row_sums[...] + land_x[0] + (land_x[1] + land_x[2])
    for copy in [send(half, land_z.at[i], peer) for i, peer in enumerate(along_z)]:
        copy.wait_recv()
    both = half[...] + land_z[0] + (land_z[1] + land_z[2])
    for b in range(UB):
        below = jnp.broadcast_to(both[b : b + 1], (BLOCK, BLOCK)).T
        rest = jnp.concatenate([pulls[0, b], pulls[1, b]], axis=0)
        out[b] = x_now[b] + squares[b] / (below + rest) * p_now[b]
    copies.finish()


def all_steps(order, part, start, yh, yl, th, tl, gram, weights):
    n = BLOCK // THIN
    copies = 3 * 12 * n + 6
    blocks = (UB, BLOCK, K)
    out = pl.pallas_call(
        cg_kernel,
        out_shape=jax.ShapeDtypeStruct(blocks, F32),
        in_specs=[SMEM] + [VMEM] * 7 + [ANY],
        out_specs=VMEM,
        scratch_shapes=[
            pltpu.VMEM((FAST, BLOCK, BLOCK), F32),
            pltpu.VMEM((UB, BLOCK, 2 * K), BF16),
            pltpu.VMEM(blocks, F32),
            pltpu.VMEM(blocks, F32),
            pltpu.VMEM(blocks, F32),
            pltpu.VMEM((2, FAST, 64, K), F32),
            pltpu.VMEM(blocks, F32),
            pltpu.VMEM((2, NZ, NX, BLOCK, K), F32),
            pltpu.VMEM((3, NZ, NX, BLOCK, K), F32),
            pltpu.VMEM((3, n, 3, 4, THIN, K), F32),
            pltpu.VMEM((3, n, 4, THIN, K), F32),
            pltpu.VMEM((3, n, 3, THIN, K), F32),
            pltpu.VMEM((UB, BLOCK), F32),
            pltpu.VMEM((3, UB, BLOCK), F32),
            pltpu.VMEM((3, UB, BLOCK), F32),
            pltpu.VMEM((UB, BLOCK), F32),
            pltpu.SemaphoreType.DMA((copies,)),
            pltpu.SemaphoreType.DMA((copies,)),
            pltpu.SemaphoreType.DMA,
        ],
        compiler_params=pltpu.CompilerParams(
            collective_id=3, has_side_effects=True, vmem_limit_bytes=WHOLE
        ),
        name="steps",
    )(order, part.reshape(NZ, NX, BLOCK, K), start.reshape(blocks), yh, yl, th, tl, gram, weights)
    return out.reshape(UB * BLOCK, K)


def step_by_step(order, part, start, yh, yl, th, tl, gram, weights):
    total = reduce(part)
    tail = [VMEM] * 5 + [ANY]
    part, residual = local(first_kernel, "first", (USERS,) * 2, [SMEM, VMEM, VMEM] + tail)(
        order, total, start, yh, yl, th, tl, gram, weights
    )
    total = reduce(part)
    part, iterate, residual, direction = local(
        second_kernel, "second", (USERS,) * 4, [SMEM] + [VMEM] * 3 + tail
    )(order, total, start, residual, yh, yl, th, tl, gram, weights)
    total = reduce(part)
    squares = jax.ShapeDtypeStruct((UB, BLOCK), F32)
    part, iterate, residual, direction = local(
        third_kernel,
        "third",
        (squares,) + (USERS,) * 3,
        [SMEM] + [VMEM] * 4 + tail,
        [pltpu.VMEM((UB * BLOCK, K), F32)],
    )(order, total, iterate, residual, direction, yh, yl, th, tl, gram, weights)
    squares = sum_scalars(part)
    return pl.pallas_call(
        last_kernel,
        out_shape=USERS,
        in_specs=[VMEM] * 4,
        out_specs=VMEM,
        compiler_params=pltpu.CompilerParams(vmem_limit_bytes=BIG),
        name="last",
    )(squares, iterate, residual, direction)


def shards(user_factors, item_factors, fetch_list, tile_user, tile_slot, er, ec, en, tile_count):
    yh, yl, th, tl, gram, ent, peak = gather(
        item_factors.reshape(IB, BLOCK, K),
        fetch_list.reshape(1, 128),
        tile_user.reshape(1, TILES),
        tile_slot.reshape(1, TILES),
        er.reshape(TILES, NNZ),
        ec.reshape(TILES, NNZ),
        en.reshape(TILES, NNZ),
        tile_count.reshape(1, 1),
    )
    part, weights, order, fits = build(
        ent.reshape(COLS, STAGE, NNZ), yh, yl, th, tl, gram, user_factors, peak
    )
    return lax.cond(
        fits[0] > 0,
        all_steps,
        step_by_step,
        order, part, user_factors, yh, yl, th, tl, gram, weights,
    )


def solution(mesh):
    return jax.shard_map(
        shards,
        mesh=mesh,
        in_specs=(
            P("row", None),
            P(("row", "col"), None),
            P("row", "col", None, None),
            P("row", "col", None),
            P("row", "col", None),
            P("row", "col", None, None),
            P("row", "col", None, None),
            P("row", "col", None, None),
            P("row", "col"),
        ),
        out_specs=P("row", None),
        check_vma=False,
    )
```
